32 devices in a mesh: dp: 2 (over core), fsdp: 16 (over z, y, x).
Axes of the slice: x: 2, y: 2, z: 4, core: 2. Of those that a mesh axis runs over, the one named last changes fastest.
Arguments:
- tokens: bfloat16 [512, 196, 768], P(('dp', 'fsdp')), may hold values from -40 to 40
- cotangent: bfloat16 [512, 196, 768], P(('dp', 'fsdp')), may hold values from -6 to 6
- counts: int32 [32, 2], P(('dp', 'fsdp')), may hold values from 1 to 8, as said below
- ln1_gain: bfloat16 [768], P('fsdp'), may hold values from 0.25 to 1.75
- ln1_bias: bfloat16 [768], P('fsdp'), may hold values from -4 to 4
- tok_in: bfloat16 [384, 196], P('fsdp'), may hold values from -0.4375 to 0.4375
- tok_in_bias: bfloat16 [384], P('fsdp'), may hold values from -6 to 6
- tok_out: bfloat16 [384, 196], P('fsdp'), may hold values from -0.4375 to 0.4375
- tok_out_bias: bfloat16 [196], replicated, may hold values from -4 to 4
- ln2_gain: bfloat16 [768], P('fsdp'), may hold values from 0.25 to 1.75
- ln2_bias: bfloat16 [768], P('fsdp'), may hold values from -4 to 4
- ch_in: bfloat16 [768, 3072], P('fsdp'), may hold values from -0.21875 to 0.21875
- ch_in_bias: bfloat16 [3072], P('fsdp'), may hold values from -6 to 6
- ch_out: bfloat16 [3072, 768], P('fsdp'), may hold values from -0.15625 to 0.15625
- ch_out_bias: bfloat16 [768], P('fsdp'), may hold values from -4 to 4
Outputs:
- block_out: bfloat16 [512, 196, 768], P(('dp', 'fsdp'))
- input_grad: bfloat16 [512, 196, 768], P(('dp', 'fsdp'))
- ln1_gain_grad: float32 [768], P('fsdp')
- ln1_bias_grad: float32 [768], P('fsdp')
- tok_in_grad: float32 [384, 196], P('fsdp')
- tok_in_bias_grad: float32 [384], P('fsdp')
- tok_out_grad: float32 [384, 196], P('fsdp')
- tok_out_bias_grad: float32 [196], replicated
- ln2_gain_grad: float32 [768], P('fsdp')
- ln2_bias_grad: float32 [768], P('fsdp')
- ch_in_grad: float32 [768, 3072], P('fsdp')
- ch_in_bias_grad: float32 [3072], P('fsdp')
- ch_out_grad: float32 [3072, 768], P('fsdp')
- ch_out_bias_grad: float32 [768], P('fsdp')
The draws below stay inside these ranges and needn't reach their ends.
Inputs may be any that keep to these rules, and one draw needn't show every extreme that they name: counts[r, m] is the number of live image slots, the first ones, among the 8 slots of device r in micro-batch m; the value 8 occurs in every draw.
All inputs are finite; a program needn't handle non-finite values.
Results may differ from the reference program's by a relative error of at most 0.0065.
Values may be sent and summed in bfloat16 or wider, within the bound.
A program may use at most 256 MiB of HBM per device.

```python
import math
import jax
import jax.numpy as jnp
from jax import lax

D = 768
DC = 3072
DS = 384
S = 196
IMG_CAP = 8
MB = 2
REPLICAS = 32
IMAGES = 512


def draw_tokens(key, part):
    base_key = jax.random.fold_in(key, 11)
    key_noise, key_scale, key_shift = jax.random.split(base_key, 3)
    noise_draw = jnp.clip(jax.random.normal(key_noise, (IMAGES, S, D), jnp.float32), -6.0, 6.0)
    centre = 0.5
    scales = jnp.exp(jax.random.uniform(key_scale, (IMAGES, S, 1), jnp.float32, math.log(0.5), math.log(5.0)))
    offsets = centre * jnp.clip(jax.random.normal(key_shift, (IMAGES, 1, D), jnp.float32), -4.0, 4.0)
    return (noise_draw * scales + offsets).astype(jnp.bfloat16)


def draw_counts(key, part):
    base_key = jax.random.fold_in(key, 23)
    key_full, key_small, key_mark = jax.random.split(base_key, 3)
    filled = jax.random.randint(key_full, (REPLICAS, MB), 0, 2) == 0
    partial_fill = jax.random.randint(key_small, (REPLICAS, MB), 1, IMG_CAP // 2 + 1)
    values = jnp.where(filled, IMG_CAP, partial_fill).reshape(-1)
    marked = jax.random.randint(key_mark, (), 0, REPLICAS * MB)
    values = values.at[marked].set(IMG_CAP)
    return values.reshape(REPLICAS, MB).astype(jnp.int32)


def with_spikes(values, own_key, source, target, shards_of, factor):
    owner, partner = [(jnp.arange(values.shape[dim]) // (values.shape[dim] // shards_of)).reshape([-1 if axis == dim else 1 for axis in range(values.ndim)]) for dim in (source, target)]
    chosen = jax.random.permutation(own_key, shards_of)[partner]
    strong = (owner == chosen) | (owner == (partner + shards_of // 2) % shards_of)
    return jnp.where(strong, factor * values, values)


def block_scale(key, extent, cuts, smallest, high):
    loudness = 1.0
    for dim, parts in cuts:
        draws = jax.random.uniform(jax.random.fold_in(jax.random.fold_in(key, 6), dim), (parts,), jnp.float32, smallest / len(cuts), high / len(cuts))
        loudness = loudness * jnp.repeat(jnp.exp(draws), extent[dim] // parts).reshape((-1,) + (1,) * (len(extent) - 1 - dim))
    return loudness


def gaussian(stream_key, shape, deviation, bound, shards=(), kind=jnp.bfloat16):
    values = jax.random.normal(stream_key, shape, jnp.float32) * deviation
    if len(shards) > 0:
        values = block_scale(stream_key, shape, shards, -0.22, 0.18) * values
    return jnp.clip(values, min=-bound, max=bound).astype(kind)


def noise_with(rng, shape, scale, bound, cuts, heavy, kind=jnp.bfloat16):
    entries = scale * jax.random.normal(rng, shape, jnp.float32)
    if cuts:
        entries = entries * block_scale(rng, shape, cuts, -0.22, 0.18)
    return jnp.clip(with_spikes(entries, jax.random.fold_in(rng, 3), *heavy), -bound, bound).astype(kind)


def setup_inputs(seed: int = 0) -> dict:
    keys = jax.random.split(jax.random.key(seed), 16)
    tokens = draw_tokens(jax.random.fold_in(keys[15], 71), 0)
    cotangent = noise_with(keys[1], (IMAGES, S, D), 1.0, 6.0, ((0, 32),), (0, 2, 32, 2.75))
    counts = draw_counts(jax.random.fold_in(keys[15], 71), 0)
    ln1_gain = jnp.clip(1.0 + 0.15 * jax.random.normal(keys[3], (D,), jnp.float32), 0.25, 1.75).astype(jnp.bfloat16)
    ln1_bias = gaussian(keys[4], (D,), 0.3, 4.0, ((0, 16),))
    tok_in = gaussian(keys[5], (DS, S), S ** -0.5, 0.4375, ((0, 16),))
    tok_in_bias = gaussian(keys[6], (DS,), 0.5, 6.0, ((0, 16),))
    tok_out = gaussian(keys[7], (DS, S), (DS // 2) ** -0.5, 0.4375, ((0, 16),))
    tok_out_bias = gaussian(keys[8], (S,), 0.3, 4.0)
    ln2_gain = jnp.clip(1.0 + 0.15 * jax.random.normal(keys[9], (D,), jnp.float32), 0.25, 1.75).astype(jnp.bfloat16)
    ln2_bias = gaussian(keys[10], (D,), 0.3, 4.0, ((0, 16),))
    ch_in = gaussian(keys[11], (D, DC), D ** -0.5, 0.21875, ((0, 16),))
    ch_in_bias = gaussian(keys[12], (DC,), 0.5, 6.0, ((0, 16),))
    ch_out = gaussian(keys[13], (DC, D), (DC // 2) ** -0.5, 0.15625, ((0, 16),))
    ch_out_bias = gaussian(keys[14], (D,), 0.3, 4.0, ((0, 16),))
    return {"tokens": tokens, "cotangent": cotangent, "counts": counts, "ln1_gain": ln1_gain, "ln1_bias": ln1_bias, "tok_in": tok_in, "tok_in_bias": tok_in_bias, "tok_out": tok_out, "tok_out_bias": tok_out_bias, "ln2_gain": ln2_gain, "ln2_bias": ln2_bias, "ch_in": ch_in, "ch_in_bias": ch_in_bias, "ch_out": ch_out, "ch_out_bias": ch_out_bias}


EPSILON = 1e-06
TOP_PRECISION = lax.Precision.HIGHEST

@jax.custom_vjp
def low(v):
    return lax.optimization_barrier(v.astype(jnp.bfloat16)).astype(jnp.float32)

@jax.custom_vjp
def reduced_backward(v):
    return v

def low_keep(v):
    return (low(v), None)

def low_pass(kept, grad):
    return (grad,)

def back_keep(v):
    return (v, None)

def back_low(kept, grad):
    return (low(grad),)
low.defvjp(low_keep, low_pass)
reduced_backward.defvjp(back_keep, back_low)

def normalize(rows_in, gain, shift):
    centre = lax.optimization_barrier(jnp.mean(rows_in, axis=-1, keepdims=True))
    centred = rows_in - centre
    spread = lax.optimization_barrier(jnp.mean(centred * centred, axis=-1, keepdims=True))
    return centred * lax.rsqrt(spread + EPSILON) * gain + shift

def smooth(values):
    return jax.nn.gelu(values, approximate=True)

def block(input_block, params):
    gain_one, shift_one, mixing_input_weight, mixing_input_bias, mixing_output_weight, output_shift, gain_two, shift_two, w_up, bias_up, w_down, bias_down = params
    normalized_rows = low(normalize(input_block, gain_one, shift_one))
    preactivation = reduced_backward(jnp.einsum('qx,exj->eqj', mixing_input_weight, normalized_rows, precision=TOP_PRECISION)) + mixing_input_bias[None, :, None]
    activation_result = low(smooth(preactivation))
    mixing_rows = input_block + reduced_backward(jnp.einsum('hp,zhi->zpi', mixing_output_weight, activation_result, precision=TOP_PRECISION)) + output_shift[None, :, None]
    normed_two = low(normalize(mixing_rows, gain_two, shift_two))
    pre_two = reduced_backward(jnp.einsum('bsd,df->bsf', normed_two, w_up, precision=TOP_PRECISION)) + bias_up
    activation_two = low(smooth(pre_two))
    return mixing_rows + reduced_backward(jnp.einsum('bsf,fd->bsd', activation_two, w_down, precision=TOP_PRECISION)) + bias_down

def reference(tokens, cotangent, counts, ln1_gain, ln1_bias, tok_in, tok_in_bias, tok_out, tok_out_bias, ln2_gain, ln2_bias, ch_in, ch_in_bias, ch_out, ch_out_bias):
    per_device = IMG_CAP * MB
    position = jnp.arange(IMAGES, dtype=jnp.int32)
    owners = (position // per_device).astype(jnp.int32)
    micro_index = (position // IMG_CAP % MB).astype(jnp.int32)
    places = position % IMG_CAP
    live_rows = (places < counts[owners, micro_index]).astype(jnp.float32)
    params = tuple((weight.astype(jnp.float32) for weight in (ln1_gain, ln1_bias, tok_in, tok_in_bias, tok_out, tok_out_bias, ln2_gain, ln2_bias, ch_in, ch_in_bias, ch_out, ch_out_bias)))
    token_groups = tokens.reshape(REPLICAS, per_device, S, D)
    grad_groups = cotangent.reshape(REPLICAS, per_device, S, D)
    live_groups = live_rows.reshape(REPLICAS, per_device)
    initial = tuple((jnp.zeros(weight.shape, jnp.float32) for weight in params))

    def group_step(running, inputs):
        x_group, grad_group, live_group = inputs
        result, pullback = jax.vjp(block, x_group.astype(jnp.float32), params)
        live_mask = live_group[:, None, None]
        grad_x, grad_params = pullback(grad_group.astype(jnp.float32) * live_mask)
        running = tuple((summed + addend for summed, addend in zip(running, grad_params)))
        return (running, ((result * live_mask).astype(jnp.bfloat16), grad_x.astype(jnp.bfloat16)))
    totals, (outputs, input_grads) = lax.scan(group_step, initial, (token_groups, grad_groups, live_groups))
    return (outputs.reshape(IMAGES, S, D), input_grads.reshape(IMAGES, S, D), totals[0], totals[1], totals[2], totals[3], totals[4], totals[5], totals[6], totals[7], totals[8], totals[9], totals[10], totals[11])
```

```python
import jax
import jax.numpy as jnp
from jax import lax
from jax.experimental import pallas as pl
from jax.experimental.pallas import tpu as pltpu
from jax.sharding import PartitionSpec as P

EPSILON = 1e-06


def normalize(rows_in, gain, shift):
    centre = jnp.mean(rows_in, axis=-1, keepdims=True)
    centred = rows_in - centre
    spread = jnp.mean(centred * centred, axis=-1, keepdims=True)
    return centred * lax.rsqrt(spread + EPSILON) * gain + shift


def smooth(values):
    return jax.nn.gelu(values, approximate=True)


def forward(input_block, token_full, channel_full, output_shift):
    gain_one, shift_one, mixing_input_weight, mixing_input_bias, mixing_output_weight = token_full
    gain_two, shift_two, w_up, bias_up, w_down, bias_down = channel_full
    normalized_rows = normalize(
        input_block, gain_one.astype(jnp.float32), shift_one.astype(jnp.float32)
    )
    normalized_reduced = normalized_rows.astype(jnp.bfloat16)
    preactivation = (
        jnp.einsum(
            "qx,exj->eqj",
            mixing_input_weight,
            normalized_reduced,
            preferred_element_type=jnp.float32,
        )
        + mixing_input_bias.astype(jnp.float32)[None, :, None]
    )
    activation_reduced = smooth(preactivation).astype(jnp.bfloat16)
    branch_output = jnp.einsum(
        "hp,zhi->zpi", mixing_output_weight, activation_reduced, preferred_element_type=jnp.float32
    )
    mixing_rows = input_block + branch_output + output_shift.astype(jnp.float32)[None, :, None]
    normed_two = normalize(mixing_rows, gain_two.astype(jnp.float32), shift_two.astype(jnp.float32))
    normed_two_low = normed_two.astype(jnp.bfloat16)
    pre_two = jnp.einsum(
        "bsd,df->bsf", normed_two_low, w_up, preferred_element_type=jnp.float32
    ) + bias_up.astype(jnp.float32)
    act_two_low = smooth(pre_two).astype(jnp.bfloat16)
    result = (
        mixing_rows
        + jnp.einsum("bsf,fd->bsd", act_two_low, w_down, preferred_element_type=jnp.float32)
        + bias_down.astype(jnp.float32)
    )
    kept = (
        normalized_reduced,
        preactivation,
        activation_reduced,
        mixing_rows,
        normed_two_low,
        pre_two,
        act_two_low,
    )
    return (result, kept)


def backward(grad_out, input_block, kept, token_full, channel_full):
    (
        normalized_reduced,
        preactivation,
        activation_reduced,
        mixing_rows,
        normed_two_low,
        pre_two,
        act_two_low,
    ) = kept
    gain_one, shift_one, mixing_input_weight, mixing_input_bias, mixing_output_weight = token_full
    gain_two, shift_two, w_up, bias_up, w_down, bias_down = channel_full
    grad_out_low = grad_out.astype(jnp.bfloat16)
    grad_act_two = jnp.einsum(
        "bsd,fd->bsf", grad_out_low, w_down, preferred_element_type=jnp.float32
    )
    grad_w_down = jnp.einsum(
        "bsf,bsd->fd", act_two_low, grad_out_low, preferred_element_type=jnp.float32
    )
    grad_bias_down = jnp.sum(grad_out, axis=(0, 1))
    grad_pre_two = jax.vjp(smooth, pre_two)[1](grad_act_two)[0]
    grad_bias_up = jnp.sum(grad_pre_two, axis=(0, 1))
    grad_pre_two_low = grad_pre_two.astype(jnp.bfloat16)
    grad_normed_two = jnp.einsum(
        "bsf,df->bsd", grad_pre_two_low, w_up, preferred_element_type=jnp.float32
    )
    grad_w_up = jnp.einsum(
        "bsd,bsf->df", normed_two_low, grad_pre_two_low, preferred_element_type=jnp.float32
    )
    norm_two_back = jax.vjp(
        normalize, mixing_rows, gain_two.astype(jnp.float32), shift_two.astype(jnp.float32)
    )[1]
    grad_through, grad_gain_two, grad_shift_two = norm_two_back(grad_normed_two)
    grad_mixed = grad_out + grad_through
    grad_out_shift = jnp.sum(grad_mixed, axis=(0, 2))
    mixing_gradient_reduced = grad_mixed.astype(jnp.bfloat16)
    grad_act = jnp.einsum(
        "qx,exj->eqj",
        mixing_output_weight,
        mixing_gradient_reduced,
        preferred_element_type=jnp.float32,
    )
    grad_w_mix_out = jnp.einsum(
        "oaq,oeq->ae",
        activation_reduced,
        mixing_gradient_reduced,
        preferred_element_type=jnp.float32,
    )
    grad_pre = jax.vjp(smooth, preactivation)[1](grad_act)[0]
    grad_bias_mix_in = jnp.sum(grad_pre, axis=(0, 2))
    preactivation_gradient_reduced = grad_pre.astype(jnp.bfloat16)
    grad_normed = jnp.einsum(
        "hp,zhi->zpi",
        mixing_input_weight,
        preactivation_gradient_reduced,
        preferred_element_type=jnp.float32,
    )
    grad_w_mix_in = jnp.einsum(
        "oaq,oeq->ae",
        preactivation_gradient_reduced,
        normalized_reduced,
        preferred_element_type=jnp.float32,
    )
    norm_one_back = jax.vjp(
        normalize, input_block, gain_one.astype(jnp.float32), shift_one.astype(jnp.float32)
    )[1]
    grad_inner, grad_gain_one, grad_shift_one = norm_one_back(grad_normed)
    grad_x = grad_mixed + grad_inner
    grad_list = (
        grad_gain_one,
        grad_shift_one,
        grad_w_mix_in,
        grad_bias_mix_in,
        grad_w_mix_out,
        grad_gain_two,
        grad_shift_two,
        grad_w_up,
        grad_bias_up,
        grad_w_down,
        grad_bias_down,
    )
    return (grad_x, grad_list, grad_out_shift)


def per_device(
    tokens,
    cotangent,
    counts,
    ln1_gain,
    ln1_bias,
    tok_in,
    tok_in_bias,
    tok_out,
    tok_out_bias,
    ln2_gain,
    ln2_bias,
    ch_in,
    ch_in_bias,
    ch_out,
    ch_out_bias,
):
    micro_total = counts.shape[1]
    per_micro = tokens.shape[0] // micro_total
    outputs = []
    input_grads = []
    grad_sums = None
    shift_sum = jnp.zeros((tok_out_bias.shape[0],), jnp.float32)
    for micro in range(micro_total):
        lower = micro * per_micro
        input_block = tokens[lower : lower + per_micro].astype(jnp.float32)
        live_rows = (jnp.arange(per_micro) < counts[0, micro]).astype(jnp.float32)[:, None, None]
        grad_out = cotangent[lower : lower + per_micro].astype(jnp.float32) * live_rows
        token_full = (
            lax.all_gather(ln1_gain, "fsdp", axis=0, tiled=True),
            lax.all_gather(ln1_bias, "fsdp", axis=0, tiled=True),
            lax.all_gather(tok_in, "fsdp", axis=0, tiled=True),
            lax.all_gather(tok_in_bias, "fsdp", axis=0, tiled=True),
            lax.all_gather(tok_out, "fsdp", axis=0, tiled=True),
        )
        channel_full = (
            lax.all_gather(ln2_gain, "fsdp", axis=0, tiled=True),
            lax.all_gather(ln2_bias, "fsdp", axis=0, tiled=True),
            lax.all_gather(ch_in, "fsdp", axis=0, tiled=True),
            lax.all_gather(ch_in_bias, "fsdp", axis=0, tiled=True),
            lax.all_gather(ch_out, "fsdp", axis=0, tiled=True),
            lax.all_gather(ch_out_bias, "fsdp", axis=0, tiled=True),
        )
        result, kept = forward(input_block, token_full, channel_full, tok_out_bias)
        outputs.append((result * live_rows).astype(jnp.bfloat16))
        token_back = (
            lax.all_gather(ln1_gain, "fsdp", axis=0, tiled=True),
            lax.all_gather(ln1_bias, "fsdp", axis=0, tiled=True),
            lax.all_gather(tok_in, "fsdp", axis=0, tiled=True),
            lax.all_gather(tok_in_bias, "fsdp", axis=0, tiled=True),
            lax.all_gather(tok_out, "fsdp", axis=0, tiled=True),
        )
        channel_back = (
            lax.all_gather(ln2_gain, "fsdp", axis=0, tiled=True),
            lax.all_gather(ln2_bias, "fsdp", axis=0, tiled=True),
            lax.all_gather(ch_in, "fsdp", axis=0, tiled=True),
            lax.all_gather(ch_in_bias, "fsdp", axis=0, tiled=True),
            lax.all_gather(ch_out, "fsdp", axis=0, tiled=True),
            lax.all_gather(ch_out_bias, "fsdp", axis=0, tiled=True),
        )
        grad_x, grad_list, grad_out_shift = backward(
            grad_out, input_block, kept, token_back, channel_back
        )
        input_grads.append(grad_x.astype(jnp.bfloat16))
        shift_sum = shift_sum + grad_out_shift
        grad_sums = (
            grad_list
            if grad_sums is None
            else tuple(jax.tree.map(jnp.add, tuple(grad_sums), tuple(grad_list)))
        )
    grad_sums = (
        lax.psum_scatter(grad_sums[0], "fsdp", scatter_dimension=0, tiled=True),
        lax.psum_scatter(grad_sums[1], "fsdp", scatter_dimension=0, tiled=True),
        lax.psum_scatter(grad_sums[2], "fsdp", scatter_dimension=0, tiled=True),
        lax.psum_scatter(grad_sums[3], "fsdp", scatter_dimension=0, tiled=True),
        lax.psum_scatter(grad_sums[4], "fsdp", scatter_dimension=0, tiled=True),
        lax.psum_scatter(grad_sums[5], "fsdp", scatter_dimension=0, tiled=True),
        lax.psum_scatter(grad_sums[6], "fsdp", scatter_dimension=0, tiled=True),
        lax.psum_scatter(grad_sums[7], "fsdp", scatter_dimension=0, tiled=True),
        lax.psum_scatter(grad_sums[8], "fsdp", scatter_dimension=0, tiled=True),
        lax.psum_scatter(grad_sums[9], "fsdp", scatter_dimension=0, tiled=True),
        lax.psum_scatter(grad_sums[10], "fsdp", scatter_dimension=0, tiled=True),
    )
    shards = lax.psum(
        (
            grad_sums[0],
            grad_sums[1],
            grad_sums[2],
            grad_sums[3],
            grad_sums[4],
            grad_sums[5],
            grad_sums[6],
            grad_sums[7],
            grad_sums[8],
            grad_sums[9],
            grad_sums[10],
        ),
        "dp",
    )
    shift_total = lax.psum(shift_sum, ("dp", "fsdp"))
    block_out = jnp.concatenate(outputs, axis=0)
    input_grad = jnp.concatenate(input_grads, axis=0)
    return (
        block_out,
        input_grad,
        shards[0],
        shards[1],
        shards[2],
        shards[3],
        shards[4],
        shift_total,
        shards[5],
        shards[6],
        shards[7],
        shards[8],
        shards[9],
        shards[10],
    )


MESH = pl.DeviceIdType.MESH
NN = (((1,), (0,)), ((), ()))
NT = (((1,), (1,)), ((), ()))
TN = (((0,), (0,)), ((), ()))
F32 = jnp.float32
BF16 = jnp.bfloat16
CHUNKS = 6
PAD = 208
BLOCK = 832
C_A = 0.7978845608
C_B = 0.7978845608 * 0.044715


def dot(left, right, dims=NN):
    return lax.dot_general(left, right, dims, preferred_element_type=F32)


def gelu_and_slope(v):
    v2 = v * v
    u = v * (C_B * v2 + C_A)
    h = 0.5 * jnp.tanh(u) + 0.5
    act = v * h
    slope = h + act * (1.0 - h) * ((6.0 * C_B) * v2 + 2.0 * C_A)
    return act, slope


def row_stats(v):
    centred = v - jnp.mean(v, axis=-1, keepdims=True)
    spread = jnp.mean(centred * centred, axis=-1, keepdims=True)
    root = lax.rsqrt(spread + EPSILON)
    return centred * root, root


def mega(
    counts, tokens, cotangent, pack, weights,
    block_out, input_grad, grad_shards, small_out, gathered, act_hbm, slope_hbm, mixed_hbm,
    normed_two, grad_rows, result_acc, grad_two_acc,
    grads, core_in, cross_out, cross_keep, cross_in, line_out, line_keep, line_in, shards, small_sum,
    small, tok_in, tok_in_t, tok_out, tok_out_t, vectors, hidden_bias,
    vector_sums, hidden_sums, tok_in_sum, tok_out_sum,
    small_sems, z_sems, z_local, x_sems, swap_sems, core_sems, cross_sems, line_sems, end_sems,
):
    images, patches, width = tokens.shape
    hidden = tok_in.shape[0]
    per_micro = images // counts.shape[1]
    c = lax.axis_index("dp")
    f = lax.axis_index("fsdp")
    zi, qi = f // 4, f % 4
    partner = (1 - c, f)

    def cross(k):
        return (c, zi * 4 + (qi ^ k))

    def line(k):
        return (c, (zi ^ k) * 4 + qi)

    def remote(src, dst, sems, index, device):
        return pltpu.make_async_remote_copy(
            src_ref=src, dst_ref=dst, send_sem=sems.at[(0,) + index], recv_sem=sems.at[(1,) + index],
            device_id=device, device_id_type=MESH,
        )

    barrier = pltpu.get_barrier_semaphore()
    for device in [partner] + [cross(k) for k in (1, 2, 3)] + [line(k) for k in (1, 2, 3)]:
        pl.semaphore_signal(barrier, inc=1, device_id=device, device_id_type=MESH)
    pl.semaphore_wait(barrier, 7)

    def small_line(k):
        return remote(small.at[c, zi, qi], small.at[c, zi, qi], small_sems, (k - 1,), line(k))

    def small_cross(k):
        return remote(small.at[c, :, qi], small.at[c, :, qi], small_sems, (k + 2,), cross(k))

    def small_swap():
        return remote(small.at[c], small.at[c], small_sems, (6,), partner)

    def z_copy(j, k):
        return remote(weights.at[c, j], gathered.at[c, j, zi, qi], z_sems, (j, k - 1), line(k))

    def z_own(j):
        return pltpu.make_async_copy(weights.at[c, j], gathered.at[c, j, zi, qi], z_local.at[j])

    def x_copy(j, k):
        return remote(gathered.at[c, j, :, qi], gathered.at[c, j, :, qi], x_sems, (j, k - 1), cross(k))

    def swap_copy(j):
        return remote(gathered.at[c, j], gathered.at[c, j], swap_sems, (j,), partner)

    def x_start(j):
        for k in (1, 2, 3):
            z_copy(j, k).wait()
        z_own(j).wait()
        for k in (1, 2, 3):
            x_copy(j, k).start()

    def swap_start(j):
        for k in (1, 2, 3):
            x_copy(j, k).wait()
        swap_copy(j).start()

    def core_copy(p, rows):
        return remote(
            grads.at[1 - c, :, :, pl.ds(0, rows)], core_in.at[p, :, :, pl.ds(0, rows)], core_sems, (p,), partner
        )

    def cross_copy(p, rows, k):
        return remote(
            cross_out.at[k - 1, :, pl.ds(0, rows)], cross_in.at[p, k - 1, :, pl.ds(0, rows)],
            cross_sems, (p, k - 1), cross(k),
        )

    def line_copy(p, rows, k):
        return remote(
            line_out.at[k - 1, pl.ds(0, rows)], line_in.at[p, k - 1, pl.ds(0, rows)], line_sems, (p, k - 1), line(k)
        )

    def cross_start(p, rows):
        core_copy(p, rows).wait()

        def per_line(z, carry):
            for k in range(4):
                q = qi ^ k
                total = grads[c, z, q, 0:rows] + core_in[p, z, q, 0:rows]
                if k == 0:
                    cross_keep[z, 0:rows] = total
                else:
                    cross_out[k - 1, z, 0:rows] = total.astype(BF16)
            return carry

        lax.fori_loop(0, 4, per_line, 0)
        for k in (1, 2, 3):
            cross_copy(p, rows, k).start()

    def line_start(p, rows):
        for k in (1, 2, 3):
            cross_copy(p, rows, k).wait()
        for k in range(4):
            z = zi ^ k
            total = cross_keep[z, 0:rows]
            for m in range(3):
                total = total + cross_in[p, m, z, 0:rows].astype(F32)
            if k == 0:
                line_keep[0:rows] = total
            else:
                line_out[k - 1, 0:rows] = total.astype(BF16)
        for k in (1, 2, 3):
            line_copy(p, rows, k).start()

    def line_finish(p, rows):
        for k in (1, 2, 3):
            line_copy(p, rows, k).wait()
        total = line_keep[0:rows]
        for m in range(3):
            total = total + line_in[p, m, 0:rows].astype(F32)
        return total

    piece = grads.shape[3]

    small[c, zi, qi] = pack[c]
    for k in (1, 2, 3):
        small_line(k).start()
    for k in (1, 2, 3):
        small_line(k).wait()
    for k in (1, 2, 3):
        small_cross(k).start()
    for j in range(CHUNKS):
        z_own(j).start()
        for k in (1, 2, 3):
            z_copy(j, k).start()
    for k in (1, 2, 3):
        small_cross(k).wait()
    small_swap().start()
    small_swap().wait()

    owners = 16
    part_a = small[0].astype(F32).reshape(owners, 32, 256)
    part_b = small[1].astype(F32).reshape(owners, 32, 256)
    full_in = part_a[:, 0:24].reshape(hidden, 256)
    full_out = part_b[:, 0:24].reshape(hidden, 256)
    bias_row = pack[1].astype(F32)[24:32]
    first = lax.broadcasted_iota(jnp.int32, (8, 256), 0) == 0
    bias_rows = jnp.where(first, bias_row, 0.0)
    tok_in[...] = full_in.astype(BF16)
    tok_in_t[...] = jnp.transpose(full_in)[0:PAD].astype(BF16)
    tok_out[...] = full_out.astype(BF16)
    out_rows = jnp.concatenate([full_out, bias_rows, jnp.zeros((120, 256), F32)], axis=0)
    tok_out_t[...] = jnp.transpose(out_rows)[0:PAD].astype(BF16)

    flat_a = part_a.reshape(owners * 32, 256).astype(BF16)
    pick_r = lax.broadcasted_iota(jnp.int32, (8, owners * 32), 0)
    pick_p = lax.broadcasted_iota(jnp.int32, (8, owners * 32), 1)
    pick = jnp.where((pick_p & 31) == 24 + pick_r, 1.0, 0.0).astype(BF16)
    col = lax.broadcasted_iota(jnp.int32, (256, width), 1)
    lane = lax.broadcasted_iota(jnp.int32, (256, width), 0)
    spread = jnp.where(lane == col - 48 * ((col * 43691) >> 21), 1.0, 0.0).astype(BF16)
    own_n = (lax.broadcasted_iota(jnp.int32, (owners * 32, width), 1) * 43691) >> 21
    own_p = lax.broadcasted_iota(jnp.int32, (owners * 32, width), 0) >> 5
    vectors[...] = dot(pick, jnp.where(own_n == own_p, dot(flat_a, spread), 0.0).astype(BF16))
    span = owners * 32
    own_n = lax.broadcasted_iota(jnp.int32, (span, span), 1) >> 5
    own_p = lax.broadcasted_iota(jnp.int32, (span, span), 0) >> 5
    col = lax.broadcasted_iota(jnp.int32, (256, span), 1)
    lane = lax.broadcasted_iota(jnp.int32, (256, span), 0)
    for j in range(CHUNKS):
        spread = jnp.where(lane == 32 * j + (col & 31), 1.0, 0.0).astype(BF16)
        rows = dot(pick, jnp.where(own_n == own_p, dot(flat_a, spread), 0.0).astype(BF16))
        hidden_bias[j] = rows[5:6]

    vector_sums[...] = jnp.zeros(vector_sums.shape, F32)
    hidden_sums[...] = jnp.zeros(hidden_sums.shape, F32)
    tok_in_sum[...] = jnp.zeros(tok_in_sum.shape, F32)
    tok_out_sum[...] = jnp.zeros(tok_out_sum.shape, F32)

    def image_rows(i, count=None):
        return pl.ds(pl.multiple_of(i * PAD, 16), count or patches)

    def live_of(i):
        return jnp.where(i % per_micro < counts[0, i // per_micro], 1.0, 0.0).astype(F32)

    def token_forward(x_buf, cot_buf, act_buf, slope_buf, mixed_buf, normed, in_sems, out_sems):
        def loads(i, slot):
            return (
                pltpu.make_async_copy(tokens.at[i], x_buf.at[slot], in_sems.at[slot, 0]),
                pltpu.make_async_copy(cotangent.at[i], cot_buf.at[slot], in_sems.at[slot, 1]),
            )

        def stores(i, slot):
            return (
                pltpu.make_async_copy(act_buf.at[slot, pl.ds(0, hidden)], act_hbm.at[i], out_sems.at[slot, 0]),
                pltpu.make_async_copy(slope_buf.at[slot], slope_hbm.at[i], out_sems.at[slot, 1]),
                pltpu.make_async_copy(mixed_buf.at[slot], mixed_hbm.at[i], out_sems.at[slot, 2]),
            )

        for copy in loads(0, 0):
            copy.start()
        ones_row = lax.broadcasted_iota(jnp.int32, (64, width), 0) == 8
        normed[192:256] = jnp.where(ones_row, 1.0, 0.0).astype(BF16)
        ones_row = lax.broadcasted_iota(jnp.int32, (128, width), 0) == 0
        for slot in range(2):
            act_buf[slot, hidden : hidden + 128] = jnp.where(ones_row, 1.0, 0.0).astype(BF16)

        def image(i, carry):
            slot = i % 2

            @pl.when(i + 1 < images)
            def _():
                for copy in loads(i + 1, 1 - slot):
                    copy.start()

            for copy in loads(i, slot):
                copy.wait()

            @pl.when(i >= 2)
            def _():
                for copy in stores(i - 2, slot):
                    copy.wait()

            @pl.when(i == 2)
            def _():
                x_start(0)

            @pl.when(i == 9)
            def _():
                swap_start(0)
                x_start(1)

            x = x_buf[slot].astype(F32)
            unit, _ = row_stats(x)
            normed[0:patches] = (unit * vectors[0:1] + vectors[1:2]).astype(BF16)
            act, slope = gelu_and_slope(dot(tok_in[...], normed[...]))
            act_buf[slot, 0:hidden] = act.astype(BF16)
            slope_buf[slot] = slope.astype(BF16)
            mixed = x + dot(tok_out_t[...], act_buf[slot])[0:patches]
            mixed_buf[slot] = mixed
            for copy in stores(i, slot):
                copy.start()
            unit, _ = row_stats(mixed)
            rows = image_rows(i)
            whole = image_rows(i, PAD)
            normed_two[whole] = jnp.zeros((PAD, width), BF16)
            normed_two[rows] = (unit * vectors[2:3] + vectors[3:4]).astype(BF16)
            grad = cot_buf[slot].astype(F32) * live_of(i)
            grad_rows[whole] = jnp.zeros((PAD, width), BF16)
            grad_rows[rows] = grad.astype(BF16)
            vector_sums[4:5] += jnp.sum(grad, axis=0, keepdims=True)
            result_acc[whole] = jnp.zeros((PAD, width), F32)
            result_acc[rows] = mixed + vectors[4:5]
            grad_two_acc[whole] = jnp.zeros((PAD, width), F32)
            return carry

        lax.fori_loop(0, images, image, 0)
        for i in (images - 2, images - 1):
            for copy in stores(i, i % 2):
                copy.wait()

    buffers = (
        pltpu.VMEM((2, patches, width), BF16),
        pltpu.VMEM((2, patches, width), BF16),
        pltpu.VMEM((2, hidden + 128, width), BF16),
        pltpu.VMEM((2, hidden, width), BF16),
        pltpu.VMEM((2, patches, width), F32),
        pltpu.VMEM((256, width), BF16),
    )
    pl.run_scoped(
        token_forward, *buffers, pltpu.SemaphoreType.DMA((2, 2)), pltpu.SemaphoreType.DMA((2, 3))
    )

    def channel(act_all, slope_all, w_in, w_out, load_sems):
        chunk = w_in.shape[-1]

        def loads(j, p):
            return [
                pltpu.make_async_copy(
                    gathered.at[0, j, :, :, pl.ds(48 * b, 48)], w_in.at[p, :, :, :, pl.ds(256 * b, 256)], load_sems.at[b]
                )
                for b in range(2)
            ] + [
                pltpu.make_async_copy(
                    gathered.at[1, j, :, :, pl.ds(32 * b, 32)], w_out.at[p, :, :, :, pl.ds(256 * b, 256)],
                    load_sems.at[2 + b],
                )
                for b in range(3)
            ]

        swap_copy(0).wait()
        for copy in loads(0, 0):
            copy.start()
        for copy in loads(0, 0):
            copy.wait()

        def tick(j, carry):
            p = j % 2

            @pl.when(j >= 1)
            def _():
                core_copy(1 - p, piece).start()

            @pl.when(j >= 2)
            def _():
                shards[j - 2] = line_finish(p, piece)

            @pl.when(j + 1 < CHUNKS)
            def _():
                swap_start(j + 1)

            @pl.when(j < 2)
            def _():
                x_start(2 * j + 2)
                x_start(2 * j + 3)

            def block(b, inner):
                rows = pl.ds(pl.multiple_of(b * BLOCK, 16), BLOCK)
                up = w_in[p].reshape(width, chunk)
                down = w_out[p].reshape(chunk, width)
                pre = dot(normed_two[rows], up) + hidden_bias[j]
                grad_act = dot(grad_rows[rows], down, NT)
                act, slope = gelu_and_slope(pre)
                grad_pre = grad_act * slope
                hidden_sums[pl.ds(j, 1)] += jnp.sum(grad_pre, axis=0, keepdims=True)
                act_all[rows] = act.astype(BF16)
                slope_all[rows] = grad_pre.astype(BF16)
                result_acc[rows] += dot(act_all[rows], down)
                grad_two_acc[rows] += dot(slope_all[rows], up, NT)

                @pl.when((b == 0) & (j >= 1))
                def _():
                    cross_start(1 - p, piece)

                @pl.when((b == 1) & (j + 1 < CHUNKS))
                def _():
                    swap_copy(j + 1).wait()
                    for copy in loads(j + 1, 1 - p):
                        copy.start()

                return inner

            lax.fori_loop(0, normed_two.shape[0] // BLOCK, block, 0)
            up_grad = dot(normed_two[...], slope_all[...], TN)
            for b in range(2):
                grads[0, :, :, 48 * b : 48 * b + 48] = up_grad[:, 256 * b : 256 * b + 256].reshape(4, 4, 48, 256)
            down_grad = dot(act_all[...], grad_rows[...], TN)
            for b in range(3):
                grads[1, :, :, 32 * b : 32 * b + 32] = down_grad[:, 256 * b : 256 * b + 256].reshape(4, 4, 32, 256)

            @pl.when(j >= 1)
            def _():
                line_start(1 - p, piece)

            @pl.when(j + 1 < CHUNKS)
            def _():
                for copy in loads(j + 1, 1 - p):
                    copy.wait()

            return carry

        lax.fori_loop(0, CHUNKS, tick, 0)

    total_rows = normed_two.shape[0]
    pl.run_scoped(
        channel,
        pltpu.VMEM((total_rows, 512), BF16),
        pltpu.VMEM((total_rows, 512), BF16),
        pltpu.VMEM((2, 4, 4, 48, 512), BF16),
        pltpu.VMEM((2, 4, 4, 32, 768), BF16),
        pltpu.SemaphoreType.DMA((5,)),
    )

    def token_backward(x_buf, out_buf, act_buf, slope_buf, mixed_buf, normed, mixed_low, pre_low, grad_buf, in_sems, out_sems):
        def loads(i, slot):
            return (
                pltpu.make_async_copy(tokens.at[i], x_buf.at[slot], in_sems.at[slot, 0]),
                pltpu.make_async_copy(act_hbm.at[i], act_buf.at[slot, pl.ds(0, hidden)], in_sems.at[slot, 1]),
                pltpu.make_async_copy(slope_hbm.at[i], slope_buf.at[slot], in_sems.at[slot, 2]),
                pltpu.make_async_copy(mixed_hbm.at[i], mixed_buf.at[slot], in_sems.at[slot, 3]),
            )

        def stores(i, slot):
            return (
                pltpu.make_async_copy(out_buf.at[slot], block_out.at[i], out_sems.at[slot, 0]),
                pltpu.make_async_copy(grad_buf.at[slot], input_grad.at[i], out_sems.at[slot, 1]),
            )

        for copy in loads(0, 0):
            copy.start()
        core_copy(1, piece).start()
        shards[CHUNKS - 2] = line_finish(0, piece)
        ones_row = lax.broadcasted_iota(jnp.int32, (64, width), 0) == 8
        normed[192:256] = jnp.where(ones_row, 1.0, 0.0).astype(BF16)
        mixed_low[192:256] = jnp.zeros((64, width), BF16)
        ones_row = lax.broadcasted_iota(jnp.int32, (128, width), 0) == 0
        for slot in range(2):
            act_buf[slot, hidden : hidden + 128] = jnp.where(ones_row, 1.0, 0.0).astype(BF16)

        def image(i, carry):
            slot = i % 2

            @pl.when(i + 1 < images)
            def _():
                for copy in loads(i + 1, 1 - slot):
                    copy.start()

            for copy in loads(i, slot):
                copy.wait()

            @pl.when(i >= 2)
            def _():
                for copy in stores(i - 2, slot):
                    copy.wait()

            @pl.when(i == 2)
            def _():
                cross_start(1, piece)

            @pl.when(i == 8)
            def _():
                line_start(1, piece)

            @pl.when(i == 12)
            def _():
                shards[CHUNKS - 1] = line_finish(1, piece)
                shard_swap().start()
                shard_own().start()

            rows = image_rows(i)
            unit, root = row_stats(mixed_buf[slot])
            grad = grad_two_acc[rows]
            vector_sums[2:3] += jnp.sum(grad * unit, axis=0, keepdims=True)
            vector_sums[3:4] += jnp.sum(grad, axis=0, keepdims=True)
            scaled = grad * vectors[2:3]
            inner = jnp.mean(scaled * unit, axis=-1, keepdims=True)
            mixed = grad_rows[rows].astype(F32) + root * (
                scaled - jnp.mean(scaled, axis=-1, keepdims=True) - unit * inner
            )
            mixed_low[0:patches] = mixed.astype(BF16)
            tok_out_sum[...] += dot(act_buf[slot], mixed_low[...], NT)
            grad_act = dot(tok_out[...], mixed_low[...])
            pre_low[...] = (grad_act * slope_buf[slot].astype(F32)).astype(BF16)
            unit, root = row_stats(x_buf[slot].astype(F32))
            normed[0:patches] = (unit * vectors[0:1] + vectors[1:2]).astype(BF16)
            tok_in_sum[...] += dot(pre_low[...], normed[...], NT)
            grad = dot(tok_in_t[...], pre_low[...])[0:patches]
            vector_sums[0:1] += jnp.sum(grad * unit, axis=0, keepdims=True)
            vector_sums[1:2] += jnp.sum(grad, axis=0, keepdims=True)
            scaled = grad * vectors[0:1]
            inner = jnp.mean(scaled * unit, axis=-1, keepdims=True)
            grad_buf[slot] = (
                mixed + root * (scaled - jnp.mean(scaled, axis=-1, keepdims=True) - unit * inner)
            ).astype(BF16)
            out_buf[slot] = (result_acc[rows] * live_of(i)).astype(BF16)
            for copy in stores(i, slot):
                copy.start()
            return carry

        lax.fori_loop(0, images, image, 0)
        for i in (images - 2, images - 1):
            for copy in stores(i, i % 2):
                copy.wait()

    def shard_swap():
        return remote(shards, grad_shards.at[c], end_sems, (0,), partner)

    def shard_own():
        return pltpu.make_async_copy(shards, grad_shards.at[c], end_sems.at[0, 2])

    pl.run_scoped(
        token_backward,
        *buffers,
        pltpu.VMEM((256, width), BF16),
        pltpu.VMEM((hidden, width), BF16),
        pltpu.VMEM((2, patches, width), BF16),
        pltpu.SemaphoreType.DMA((2, 4)),
        pltpu.SemaphoreType.DMA((2, 2)),
    )

    tok_in_rows = tok_in_sum[...].reshape(4, 4, 24, 256)
    tok_out_rows = tok_out_sum[0:hidden].reshape(4, 4, 24, 256)
    grads[0, :, :, 0:24] = tok_in_rows
    grads[1, :, :, 0:24] = tok_out_rows
    sums = vector_sums[...]
    hidden_rows = hidden_sums[...]
    for o in range(owners):
        grads[0, o // 4, o % 4, 24:32, 0:128] = pltpu.roll(sums, (width - 48 * o) % width, 1)[:, 0:128]
        grads[0, o // 4, o % 4, 24:32, 128:256] = jnp.zeros((8, 128), F32)
        grads[0, o // 4, o % 4, 31:32] = tok_out_sum[hidden : hidden + 1]
        grads[1, o // 4, o % 4, 24:32, 0:128] = pltpu.roll(hidden_rows, (512 - 32 * o) % 512, 1)[:, 0:128]
        grads[1, o // 4, o % 4, 24:32, 128:256] = jnp.zeros((8, 128), F32)
    core_copy(0, 32).start()
    cross_start(0, 32)
    line_start(0, 32)
    small_sum[...] = line_finish(0, 32)

    def small_end():
        return remote(small_sum, small_out.at[c], end_sems, (1,), partner)

    small_own = pltpu.make_async_copy(small_sum, small_out.at[c], end_sems.at[1, 2])
    small_end().start()
    small_own.start()
    small_end().wait()
    small_own.wait()
    shard_swap().wait()
    shard_own().wait()


def per_device_fused(
    tokens, cotangent, counts, ln1_gain, ln1_bias, tok_in, tok_in_bias, tok_out, tok_out_bias,
    ln2_gain, ln2_bias, ch_in, ch_in_bias, ch_out, ch_out_bias,
):
    images, patches, width = tokens.shape
    per_in, inner = ch_in.shape
    per_out = ch_out.shape[0]
    per_tok = tok_in.shape[0]
    owners = width // per_in
    hidden = per_tok * owners
    each = per_out // CHUNKS
    chunk = each * owners

    def row(vector):
        return jnp.pad(vector, (0, 256 - vector.shape[0]))[None]

    pad_in = jnp.concatenate(
        [tok_in, jnp.zeros((per_tok, 4), BF16), tok_in_bias[:, None], jnp.zeros((per_tok, 55), BF16)], axis=1
    )
    pad_out = jnp.pad(tok_out, ((0, 0), (0, 256 - patches)))
    none = jnp.zeros((2, 256), BF16)
    pack = jnp.stack(
        [
            jnp.concatenate(
                [pad_in, row(ln1_gain), row(ln1_bias), row(ln2_gain), row(ln2_bias), row(ch_out_bias), row(ch_in_bias), none]
            ),
            jnp.concatenate([pad_out, row(tok_out_bias), jnp.zeros((7, 256), BF16)]),
        ]
    )
    local_in = ch_in.reshape(per_in, owners, CHUNKS, each).transpose(2, 0, 1, 3).reshape(CHUNKS, per_in, 2, 256)
    local_in = local_in.transpose(0, 2, 1, 3).reshape(CHUNKS, 96, 256)
    local_out = ch_out.reshape(CHUNKS, each, 3, 256).transpose(0, 2, 1, 3).reshape(CHUNKS, 96, 256)
    weights = jnp.stack([local_in, local_out])
    any_spec = pl.BlockSpec(memory_space=pl.ANY)
    vmem = pltpu.VMEM
    dma = pltpu.SemaphoreType.DMA
    rows = images * PAD
    shape = jax.ShapeDtypeStruct
    flops = 12 * rows * width * inner
    results = pl.pallas_call(
        mega,
        in_specs=[
            pl.BlockSpec(memory_space=pltpu.SMEM), any_spec, any_spec, pl.BlockSpec(memory_space=pltpu.VMEM), any_spec,
        ],
        out_specs=[any_spec] * 8,
        out_shape=[
            shape(tokens.shape, BF16),
            shape(tokens.shape, BF16),
            shape((2, CHUNKS, 96, 256), F32),
            shape((2, 32, 256), F32),
            shape((2, CHUNKS, 4, 4, 96, 256), BF16),
            shape((images, hidden, width), BF16),
            shape((images, hidden, width), BF16),
            shape((images, patches, width), F32),
        ],
        scratch_shapes=[
            vmem((rows, width), BF16),
            vmem((rows, width), BF16),
            vmem((rows, width), F32),
            vmem((rows, width), F32),
            vmem((2, 4, 4, 96, 256), F32),
            vmem((2, 4, 4, 96, 256), F32),
            vmem((3, 4, 96, 256), BF16),
            vmem((4, 96, 256), F32),
            vmem((2, 3, 4, 96, 256), BF16),
            vmem((3, 96, 256), BF16),
            vmem((96, 256), F32),
            vmem((2, 3, 96, 256), BF16),
            vmem((CHUNKS, 96, 256), F32),
            vmem((32, 256), F32),
            vmem((2, 4, 4, 32, 256), BF16),
            vmem((hidden, 256), BF16),
            vmem((PAD, hidden), BF16),
            vmem((hidden, 256), BF16),
            vmem((PAD, hidden + 128), BF16),
            vmem((8, width), F32),
            vmem((CHUNKS, 1, chunk), F32),
            vmem((8, width), F32),
            vmem((8, chunk), F32),
            vmem((hidden, 256), F32),
            vmem((hidden + 128, 256), F32),
            dma((2, 7)),
            dma((2, CHUNKS, 3)),
            dma((CHUNKS,)),
            dma((2, CHUNKS, 3)),
            dma((2, CHUNKS)),
            dma((2, 2)),
            dma((2, 2, 3)),
            dma((2, 2, 3)),
            dma((2, 3)),
        ],
        compiler_params=pltpu.CompilerParams(
            collective_id=0, has_side_effects=True, vmem_limit_bytes=61 * 1024 * 1024
        ),
        cost_estimate=pl.CostEstimate(flops=flops, bytes_accessed=100_000_000, transcendentals=rows * inner),
    )(counts, tokens, cotangent, pack, weights)
    block_out, input_grad, shards, small_sums = results[:4]
    grad_in = shards[0].reshape(CHUNKS, 2, per_in, 256).transpose(2, 0, 1, 3).reshape(per_in, CHUNKS, owners, each)
    grad_in = grad_in.transpose(0, 2, 1, 3).reshape(per_in, inner)
    grad_out = shards[1].reshape(CHUNKS, 3, each, 256).transpose(0, 2, 1, 3).reshape(per_out, width)
    part_a, part_b = small_sums[0], small_sums[1]
    return (
        block_out,
        input_grad,
        part_a[24, :per_in],
        part_a[25, :per_in],
        part_a[:per_tok, :patches],
        part_a[:per_tok, 200],
        part_b[:per_tok, :patches],
        part_a[31, :patches],
        part_a[26, :per_in],
        part_a[27, :per_in],
        grad_in,
        part_b[24 : 24 + CHUNKS, :each].reshape(per_out),
        grad_out,
        part_a[28, :per_in],
    )


def solution(mesh):
    fused = mesh.shape["dp"] == 2 and mesh.shape["fsdp"] == 16
    return jax.shard_map(
        per_device_fused if fused else per_device,
        mesh=mesh,
        in_specs=(
            P(("dp", "fsdp"), None, None),
            P(("dp", "fsdp"), None, None),
            P(("dp", "fsdp"), None),
            P("fsdp"),
            P("fsdp"),
            P("fsdp", None),
            P("fsdp"),
            P("fsdp", None),
            P(),
            P("fsdp"),
            P("fsdp"),
            P("fsdp", None),
            P("fsdp"),
            P("fsdp", None),
            P("fsdp"),
        ),
        out_specs=(
            P(("dp", "fsdp"), None, None),
            P(("dp", "fsdp"), None, None),
            P("fsdp"),
            P("fsdp"),
            P("fsdp", None),
            P("fsdp"),
            P("fsdp", None),
            P(),
            P("fsdp"),
            P("fsdp"),
            P("fsdp", None),
            P("fsdp"),
            P("fsdp", None),
            P("fsdp"),
        ),
        check_vma=False,
    )
```

```python
import jax
import jax.numpy as jnp
from jax import lax
from jax.experimental import pallas as pl
from jax.experimental.pallas import tpu as pltpu
from jax.sharding import PartitionSpec as P

EPSILON = 1e-06


def normalize(rows_in, gain, shift):
    centre = jnp.mean(rows_in, axis=-1, keepdims=True)
    centred = rows_in - centre
    spread = jnp.mean(centred * centred, axis=-1, keepdims=True)
    return centred * lax.rsqrt(spread + EPSILON) * gain + shift


def smooth(values):
    return jax.nn.gelu(values, approximate=True)


def forward(input_block, token_full, channel_full, output_shift):
    gain_one, shift_one, mixing_input_weight, mixing_input_bias, mixing_output_weight = token_full
    gain_two, shift_two, w_up, bias_up, w_down, bias_down = channel_full
    normalized_rows = normalize(
        input_block, gain_one.astype(jnp.float32), shift_one.astype(jnp.float32)
    )
    normalized_reduced = normalized_rows.astype(jnp.bfloat16)
    preactivation = (
        jnp.einsum(
            "qx,exj->eqj",
            mixing_input_weight,
            normalized_reduced,
            preferred_element_type=jnp.float32,
        )
        + mixing_input_bias.astype(jnp.float32)[None, :, None]
    )
    activation_reduced = smooth(preactivation).astype(jnp.bfloat16)
    branch_output = jnp.einsum(
        "hp,zhi->zpi", mixing_output_weight, activation_reduced, preferred_element_type=jnp.float32
    )
    mixing_rows = input_block + branch_output + output_shift.astype(jnp.float32)[None, :, None]
    normed_two = normalize(mixing_rows, gain_two.astype(jnp.float32), shift_two.astype(jnp.float32))
    normed_two_low = normed_two.astype(jnp.bfloat16)
    pre_two = jnp.einsum(
        "bsd,df->bsf", normed_two_low, w_up, preferred_element_type=jnp.float32
    ) + bias_up.astype(jnp.float32)
    act_two_low = smooth(pre_two).astype(jnp.bfloat16)
    result = (
        mixing_rows
        + jnp.einsum("bsf,fd->bsd", act_two_low, w_down, preferred_element_type=jnp.float32)
        + bias_down.astype(jnp.float32)
    )
    kept = (
        normalized_reduced,
        preactivation,
        activation_reduced,
        mixing_rows,
        normed_two_low,
        pre_two,
        act_two_low,
    )
    return (result, kept)


def backward(grad_out, input_block, kept, token_full, channel_full):
    (
        normalized_reduced,
        preactivation,
        activation_reduced,
        mixing_rows,
        normed_two_low,
        pre_two,
        act_two_low,
    ) = kept
    gain_one, shift_one, mixing_input_weight, mixing_input_bias, mixing_output_weight = token_full
    gain_two, shift_two, w_up, bias_up, w_down, bias_down = channel_full
    grad_out_low = grad_out.astype(jnp.bfloat16)
    grad_act_two = jnp.einsum(
        "bsd,fd->bsf", grad_out_low, w_down, preferred_element_type=jnp.float32
    )
    grad_w_down = jnp.einsum(
        "bsf,bsd->fd", act_two_low, grad_out_low, preferred_element_type=jnp.float32
    )
    grad_bias_down = jnp.sum(grad_out, axis=(0, 1))
    grad_pre_two = jax.vjp(smooth, pre_two)[1](grad_act_two)[0]
    grad_bias_up = jnp.sum(grad_pre_two, axis=(0, 1))
    grad_pre_two_low = grad_pre_two.astype(jnp.bfloat16)
    grad_normed_two = jnp.einsum(
        "bsf,df->bsd", grad_pre_two_low, w_up, preferred_element_type=jnp.float32
    )
    grad_w_up = jnp.einsum(
        "bsd,bsf->df", normed_two_low, grad_pre_two_low, preferred_element_type=jnp.float32
    )
    norm_two_back = jax.vjp(
        normalize, mixing_rows, gain_two.astype(jnp.float32), shift_two.astype(jnp.float32)
    )[1]
    grad_through, grad_gain_two, grad_shift_two = norm_two_back(grad_normed_two)
    grad_mixed = grad_out + grad_through
    grad_out_shift = jnp.sum(grad_mixed, axis=(0, 2))
    mixing_gradient_reduced = grad_mixed.astype(jnp.bfloat16)
    grad_act = jnp.einsum(
        "qx,exj->eqj",
        mixing_output_weight,
        mixing_gradient_reduced,
        preferred_element_type=jnp.float32,
    )
    grad_w_mix_out = jnp.einsum(
        "oaq,oeq->ae",
        activation_reduced,
        mixing_gradient_reduced,
        preferred_element_type=jnp.float32,
    )
    grad_pre = jax.vjp(smooth, preactivation)[1](grad_act)[0]
    grad_bias_mix_in = jnp.sum(grad_pre, axis=(0, 2))
    preactivation_gradient_reduced = grad_pre.astype(jnp.bfloat16)
    grad_normed = jnp.einsum(
        "hp,zhi->zpi",
        mixing_input_weight,
        preactivation_gradient_reduced,
        preferred_element_type=jnp.float32,
    )
    grad_w_mix_in = jnp.einsum(
        "oaq,oeq->ae",
        preactivation_gradient_reduced,
        normalized_reduced,
        preferred_element_type=jnp.float32,
    )
    norm_one_back = jax.vjp(
        normalize, input_block, gain_one.astype(jnp.float32), shift_one.astype(jnp.float32)
    )[1]
    grad_inner, grad_gain_one, grad_shift_one = norm_one_back(grad_normed)
    grad_x = grad_mixed + grad_inner
    grad_list = (
        grad_gain_one,
        grad_shift_one,
        grad_w_mix_in,
        grad_bias_mix_in,
        grad_w_mix_out,
        grad_gain_two,
        grad_shift_two,
        grad_w_up,
        grad_bias_up,
        grad_w_down,
        grad_bias_down,
    )
    return (grad_x, grad_list, grad_out_shift)


def per_device(
    tokens,
    cotangent,
    counts,
    ln1_gain,
    ln1_bias,
    tok_in,
    tok_in_bias,
    tok_out,
    tok_out_bias,
    ln2_gain,
    ln2_bias,
    ch_in,
    ch_in_bias,
    ch_out,
    ch_out_bias,
):
    micro_total = counts.shape[1]
    per_micro = tokens.shape[0] // micro_total
    outputs = []
    input_grads = []
    grad_sums = None
    shift_sum = jnp.zeros((tok_out_bias.shape[0],), jnp.float32)
    for micro in range(micro_total):
        lower = micro * per_micro
        input_block = tokens[lower : lower + per_micro].astype(jnp.float32)
        live_rows = (jnp.arange(per_micro) < counts[0, micro]).astype(jnp.float32)[:, None, None]
        grad_out = cotangent[lower : lower + per_micro].astype(jnp.float32) * live_rows
        token_full = (
            lax.all_gather(ln1_gain, "fsdp", axis=0, tiled=True),
            lax.all_gather(ln1_bias, "fsdp", axis=0, tiled=True),
            lax.all_gather(tok_in, "fsdp", axis=0, tiled=True),
            lax.all_gather(tok_in_bias, "fsdp", axis=0, tiled=True),
            lax.all_gather(tok_out, "fsdp", axis=0, tiled=True),
        )
        channel_full = (
            lax.all_gather(ln2_gain, "fsdp", axis=0, tiled=True),
            lax.all_gather(ln2_bias, "fsdp", axis=0, tiled=True),
            lax.all_gather(ch_in, "fsdp", axis=0, tiled=True),
            lax.all_gather(ch_in_bias, "fsdp", axis=0, tiled=True),
            lax.all_gather(ch_out, "fsdp", axis=0, tiled=True),
            lax.all_gather(ch_out_bias, "fsdp", axis=0, tiled=True),
        )
        result, kept = forward(input_block, token_full, channel_full, tok_out_bias)
        outputs.append((result * live_rows).astype(jnp.bfloat16))
        token_back = (
            lax.all_gather(ln1_gain, "fsdp", axis=0, tiled=True),
            lax.all_gather(ln1_bias, "fsdp", axis=0, tiled=True),
            lax.all_gather(tok_in, "fsdp", axis=0, tiled=True),
            lax.all_gather(tok_in_bias, "fsdp", axis=0, tiled=True),
            lax.all_gather(tok_out, "fsdp", axis=0, tiled=True),
        )
        channel_back = (
            lax.all_gather(ln2_gain, "fsdp", axis=0, tiled=True),
            lax.all_gather(ln2_bias, "fsdp", axis=0, tiled=True),
            lax.all_gather(ch_in, "fsdp", axis=0, tiled=True),
            lax.all_gather(ch_in_bias, "fsdp", axis=0, tiled=True),
            lax.all_gather(ch_out, "fsdp", axis=0, tiled=True),
            lax.all_gather(ch_out_bias, "fsdp", axis=0, tiled=True),
        )
        grad_x, grad_list, grad_out_shift = backward(
            grad_out, input_block, kept, token_back, channel_back
        )
        input_grads.append(grad_x.astype(jnp.bfloat16))
        shift_sum = shift_sum + grad_out_shift
        grad_sums = (
            grad_list
            if grad_sums is None
            else tuple(jax.tree.map(jnp.add, tuple(grad_sums), tuple(grad_list)))
        )
    grad_sums = (
        lax.psum_scatter(grad_sums[0], "fsdp", scatter_dimension=0, tiled=True),
        lax.psum_scatter(grad_sums[1], "fsdp", scatter_dimension=0, tiled=True),
        lax.psum_scatter(grad_sums[2], "fsdp", scatter_dimension=0, tiled=True),
        lax.psum_scatter(grad_sums[3], "fsdp", scatter_dimension=0, tiled=True),
        lax.psum_scatter(grad_sums[4], "fsdp", scatter_dimension=0, tiled=True),
        lax.psum_scatter(grad_sums[5], "fsdp", scatter_dimension=0, tiled=True),
        lax.psum_scatter(grad_sums[6], "fsdp", scatter_dimension=0, tiled=True),
        lax.psum_scatter(grad_sums[7], "fsdp", scatter_dimension=0, tiled=True),
        lax.psum_scatter(grad_sums[8], "fsdp", scatter_dimension=0, tiled=True),
        lax.psum_scatter(grad_sums[9], "fsdp", scatter_dimension=0, tiled=True),
        lax.psum_scatter(grad_sums[10], "fsdp", scatter_dimension=0, tiled=True),
    )
    shards = lax.psum(
        (
            grad_sums[0],
            grad_sums[1],
            grad_sums[2],
            grad_sums[3],
            grad_sums[4],
            grad_sums[5],
            grad_sums[6],
            grad_sums[7],
            grad_sums[8],
            grad_sums[9],
            grad_sums[10],
        ),
        "dp",
    )
    shift_total = lax.psum(shift_sum, ("dp", "fsdp"))
    block_out = jnp.concatenate(outputs, axis=0)
    input_grad = jnp.concatenate(input_grads, axis=0)
    return (
        block_out,
        input_grad,
        shards[0],
        shards[1],
        shards[2],
        shards[3],
        shards[4],
        shift_total,
        shards[5],
        shards[6],
        shards[7],
        shards[8],
        shards[9],
        shards[10],
    )


MESH = pl.DeviceIdType.MESH
NN = (((1,), (0,)), ((), ()))
NT = (((1,), (1,)), ((), ()))
TN = (((0,), (0,)), ((), ()))
F32 = jnp.float32
BF16 = jnp.bfloat16
CHUNKS = 6
BLOCK = 784
SPAN = 224
STEP = 224
LANES = 128
C_A = 0.7978845608
C_B = 0.7978845608 * 0.044715


def dot(left, right, dims=NN):
    return lax.dot_general(left, right, dims, preferred_element_type=F32)


def gelu_and_slope(v):
    v2 = v * v
    u = v * (C_B * v2 + C_A)
    h = 0.5 * jnp.tanh(u) + 0.5
    act = v * h
    slope = h + act * (1.0 - h) * ((6.0 * C_B) * v2 + 2.0 * C_A)
    return act, slope


def row_stats(v):
    centred = v - jnp.mean(v, axis=-1, keepdims=True)
    spread = jnp.mean(centred * centred, axis=-1, keepdims=True)
    root = lax.rsqrt(spread + EPSILON)
    return centred * root, root


def take(buf, rows):
    return jnp.concatenate([buf.at[t][rows, :] for t in range(buf.shape[0])], axis=1)


def put(buf, rows, value):
    for t in range(buf.shape[0]):
        buf.at[t][rows, :] = value[:, LANES * t : LANES * (t + 1)]


def mega(
    counts, tokens, cotangent, vector_row, tok_in_own, tok_out_own, ch_in_own, ch_out_own,
    block_out, input_grad, ch_in_grad, ch_out_grad, small_out, gathered, act_hbm, slope_hbm, mixed_hbm,
    normed_two, grad_rows, result_acc, grad_two_acc,
    grads, core_in, cross_out, cross_keep, cross_in, line_out, line_keep, line_in, shards, stage_in, stage_out,
    small_sum, own_weights, small, tok_in, tok_in_t, tok_out, tok_out_t, vectors, hidden_bias,
    vector_sums, hidden_sums, tok_in_sum, tok_out_sum,
    small_sems, z_sems, z_local, x_sems, swap_sems, core_sems, cross_sems, line_sems, end_sems,
):
    total_rows, width = tokens.shape
    images, hidden = act_hbm.shape[0], act_hbm.shape[1]
    patches = total_rows // images
    per_micro = images // counts.shape[1]
    owners = 16
    tiles = width // LANES
    c = lax.axis_index("dp")
    f = lax.axis_index("fsdp")
    zi, qi = f // 4, f % 4
    partner = (1 - c, f)

    def cross(k):
        return (c, zi * 4 + (qi ^ k))

    def line(k):
        return (c, (zi ^ k) * 4 + qi)

    def remote(src, dst, sems, index, device):
        return pltpu.make_async_remote_copy(
            src_ref=src, dst_ref=dst, send_sem=sems.at[(0,) + index], recv_sem=sems.at[(1,) + index],
            device_id=device, device_id_type=MESH,
        )

    barrier = pltpu.get_barrier_semaphore()
    for device in [partner] + [cross(k) for k in (1, 2, 3)] + [line(k) for k in (1, 2, 3)]:
        pl.semaphore_signal(barrier, inc=1, device_id=device, device_id_type=MESH)

    row = vector_row[...].astype(F32)

    def vector_at(offset, length, lanes=256):
        moved = row if offset == 0 else pltpu.roll(row, width - offset, 1)
        lane = lax.broadcasted_iota(jnp.int32, (1, lanes), 1)
        return jnp.where(lane < length, moved[:, 0:lanes], 0.0)

    lane = lax.broadcasted_iota(jnp.int32, (24, 256), 1)
    bias_column = jnp.transpose(jnp.broadcast_to(vector_at(240, 24, LANES), (LANES, LANES)))[0:24, 0:1]
    pad = jnp.zeros((24, 256 - patches), F32)
    padded = jnp.concatenate([tok_in_own[...].astype(F32), pad], axis=1)
    padded = jnp.where(lane == 200, jnp.broadcast_to(bias_column, (24, 256)), padded)
    rows_a = [vector_at(48 * r, 48) for r in range(5)] + [vector_at(264, 192), jnp.zeros((2, 256), F32)]
    packed_a = jnp.concatenate([padded] + rows_a, axis=0)
    padded = jnp.concatenate([tok_out_own[...].astype(F32), pad], axis=1)
    bias_rows = jnp.concatenate([vector_at(456, patches), jnp.zeros((7, 256), F32)], axis=0)
    packed_b = jnp.concatenate([padded, bias_rows], axis=0)
    small[c, zi, qi] = jnp.where(c == 0, packed_a, packed_b).astype(BF16)

    @pl.when(c == 0)
    def _():
        group = lax.broadcasted_iota(jnp.int32, (48, LANES), 1) >> 5
        for j in range(CHUNKS):
            for b in range(2):
                for t in range(2):
                    tile = None
                    for g in range(4):
                        source = 192 * (8 * b + 4 * t + g) + 32 * j
                        part = ch_in_own[:, source // LANES * LANES : (source // LANES + 1) * LANES].astype(F32)
                        shift = (32 * g - source) % LANES
                        part = part if shift == 0 else pltpu.roll(part, shift, 1)
                        tile = part if tile is None else jnp.where(group == g, part, tile)
                    own_weights[j, 48 * b : 48 * b + 48, LANES * t : LANES * (t + 1)] = tile.astype(BF16)

    @pl.when(c == 1)
    def _():
        for j in range(CHUNKS):
            for b in range(3):
                own_weights[j, 32 * b : 32 * b + 32] = ch_out_own[32 * j : 32 * j + 32, 256 * b : 256 * b + 256]

    def small_line(k):
        return remote(small.at[c, zi, qi], small.at[c, zi, qi], small_sems, (k - 1,), line(k))

    def small_cross(k):
        return remote(small.at[c, :, qi], small.at[c, :, qi], small_sems, (k + 2,), cross(k))

    def small_swap():
        return remote(small.at[c], small.at[c], small_sems, (6,), partner)

    def z_copy(j, k):
        return remote(own_weights.at[j], gathered.at[c, j, zi, qi], z_sems, (j, k - 1), line(k))

    def z_own(j):
        return pltpu.make_async_copy(own_weights.at[j], gathered.at[c, j, zi, qi], z_local.at[j])

    def x_copy(j, k):
        return remote(gathered.at[c, j, :, qi], gathered.at[c, j, :, qi], x_sems, (j, k - 1), cross(k))

    def swap_copy(j):
        return remote(gathered.at[c, j], gathered.at[c, j], swap_sems, (j,), partner)

    def z_start(j):
        z_own(j).start()
        for k in (1, 2, 3):
            z_copy(j, k).start()

    def x_start(j):
        for k in (1, 2, 3):
            z_copy(j, k).wait()
        z_own(j).wait()
        for k in (1, 2, 3):
            x_copy(j, k).start()

    def swap_start(j):
        for k in (1, 2, 3):
            x_copy(j, k).wait()
        swap_copy(j).start()

    def core_copy(p, rows):
        return remote(
            grads.at[1 - c, :, :, pl.ds(0, rows)], core_in.at[p, :, :, pl.ds(0, rows)], core_sems, (p,), partner
        )

    def cross_copy(p, rows, k):
        return remote(
            cross_out.at[k - 1, :, pl.ds(0, rows)], cross_in.at[p, k - 1, :, pl.ds(0, rows)],
            cross_sems, (p, k - 1), cross(k),
        )

    def line_copy(p, rows, k):
        return remote(
            line_out.at[k - 1, pl.ds(0, rows)], line_in.at[p, k - 1, pl.ds(0, rows)], line_sems, (p, k - 1), line(k)
        )

    def cross_start(p, rows):
        core_copy(p, rows).wait()

        def per_line(z, carry):
            for k in range(4):
                q = qi ^ k
                total = grads[c, z, q, 0:rows] + core_in[p, z, q, 0:rows]
                if k == 0:
                    cross_keep[z, 0:rows] = total
                else:
                    cross_out[k - 1, z, 0:rows] = total.astype(BF16)
            return carry

        lax.fori_loop(0, 4, per_line, 0)
        for k in (1, 2, 3):
            cross_copy(p, rows, k).start()

    def line_start(p, rows):
        for k in (1, 2, 3):
            cross_copy(p, rows, k).wait()
        for k in range(4):
            z = zi ^ k
            total = cross_keep[z, 0:rows]
            for m in range(3):
                total = total + cross_in[p, m, z, 0:rows].astype(F32)
            if k == 0:
                line_keep[0:rows] = total
            else:
                line_out[k - 1, 0:rows] = total.astype(BF16)
        for k in (1, 2, 3):
            line_copy(p, rows, k).start()

    def line_finish(p, rows):
        for k in (1, 2, 3):
            line_copy(p, rows, k).wait()
        total = line_keep[0:rows]
        for m in range(3):
            total = total + line_in[p, m, 0:rows].astype(F32)
        return total

    piece = grads.shape[3]

    def live_rows(count):
        image = lax.broadcasted_iota(jnp.int32, (count, 1), 0) % images
        live = jnp.zeros((count, 1), F32)
        for micro in range(counts.shape[1]):
            inside = (image >= micro * per_micro) & (image < micro * per_micro + counts[0, micro])
            live = jnp.where(inside, 1.0, live)
        return live

    def span_rows(b, step=None):
        if step is None:
            return pl.ds(pl.multiple_of(b * SPAN, 16), SPAN)
        return pl.ds(pl.multiple_of(b * SPAN + step * STEP, 16), STEP)

    spans = total_rows // SPAN
    steps = SPAN // STEP

    def image_rows(i):
        return pl.ds(i, patches, stride=images)

    def norm_one(x_sems_local):
        def load(b):
            return pltpu.make_async_copy(tokens.at[span_rows(b)], normed_two.at[span_rows(b)], x_sems_local.at[b])

        for b in range(spans):
            load(b).start()
        pl.semaphore_wait(barrier, 7)
        for k in (1, 2, 3):
            small_line(k).start()
        for j in (0, 1):
            z_start(j)

        def span(b, carry):
            load(b).wait()

            def step(s, inner):
                rows = span_rows(b, s)
                unit, _ = row_stats(normed_two[rows].astype(F32))
                put(grad_two_acc, rows, unit)
                return inner

            lax.fori_loop(0, steps, step, 0)

            @pl.when(b == 5)
            def _():
                for k in (1, 2, 3):
                    small_line(k).wait()
                for k in (1, 2, 3):
                    small_cross(k).start()

            @pl.when(b == spans - 1)
            def _():
                for k in (1, 2, 3):
                    small_cross(k).wait()
                small_swap().start()

            return carry

        lax.fori_loop(0, spans, span, 0)

    pl.run_scoped(norm_one, pltpu.SemaphoreType.DMA((spans,)))
    cot_copy = pltpu.make_async_copy(cotangent, grad_rows, end_sems.at[0, 2])
    cot_copy.start()
    vector_sums[...] = jnp.zeros(vector_sums.shape, F32)
    hidden_sums[...] = jnp.zeros(hidden_sums.shape, F32)
    tok_in_sum[...] = jnp.zeros(tok_in_sum.shape, F32)
    tok_out_sum[...] = jnp.zeros(tok_out_sum.shape, F32)
    small_swap().wait()

    part_a = small[0].astype(F32).reshape(owners, 32, 256)
    part_b = small[1].astype(F32).reshape(owners, 32, 256)
    full_in = part_a[:, 0:24].reshape(hidden, 256)
    full_out = part_b[:, 0:24].reshape(hidden, 256)
    tok_in[...] = full_in.astype(BF16)
    tok_in_t[...] = jnp.transpose(full_in).astype(BF16)
    tok_out[...] = full_out.astype(BF16)
    out_rows = jnp.concatenate([full_out, bias_rows, jnp.zeros((120, 256), F32)], axis=0)
    tok_out_t[...] = jnp.transpose(out_rows).astype(BF16)

    flat_a = part_a.reshape(owners * 32, 256).astype(BF16)
    pick_r = lax.broadcasted_iota(jnp.int32, (8, owners * 32), 0)
    pick_p = lax.broadcasted_iota(jnp.int32, (8, owners * 32), 1)
    pick = jnp.where((pick_p & 31) == 24 + pick_r, 1.0, 0.0).astype(BF16)
    col = lax.broadcasted_iota(jnp.int32, (256, width), 1)
    lane = lax.broadcasted_iota(jnp.int32, (256, width), 0)
    spread = jnp.where(lane == col - 48 * ((col * 43691) >> 21), 1.0, 0.0).astype(BF16)
    own_n = (lax.broadcasted_iota(jnp.int32, (owners * 32, width), 1) * 43691) >> 21
    own_p = lax.broadcasted_iota(jnp.int32, (owners * 32, width), 0) >> 5
    vectors[...] = dot(pick, jnp.where(own_n == own_p, dot(flat_a, spread), 0.0).astype(BF16))
    span_n = owners * 32
    own_n = lax.broadcasted_iota(jnp.int32, (span_n, span_n), 1) >> 5
    own_p = lax.broadcasted_iota(jnp.int32, (span_n, span_n), 0) >> 5
    col = lax.broadcasted_iota(jnp.int32, (256, span_n), 1)
    lane = lax.broadcasted_iota(jnp.int32, (256, span_n), 0)
    for j in range(CHUNKS):
        spread = jnp.where(lane == 32 * j + (col & 31), 1.0, 0.0).astype(BF16)
        rows = dot(pick, jnp.where(own_n == own_p, dot(flat_a, spread), 0.0).astype(BF16))
        hidden_bias[j] = rows[5:6]

    def ready_tokens(normed, act_buf):
        ones_row = lax.broadcasted_iota(jnp.int32, (64, width), 0) == 8
        normed[192:256] = jnp.where(ones_row, 1.0, 0.0).astype(BF16)
        ones_row = lax.broadcasted_iota(jnp.int32, (128, width), 0) == 0
        for slot in range(2):
            act_buf[slot, hidden : hidden + 128] = jnp.where(ones_row, 1.0, 0.0).astype(BF16)

    def token_forward(act_buf, slope_buf, normed, out_sems, mixed_sems):
        def stores(i, slot):
            return (
                pltpu.make_async_copy(act_buf.at[slot, pl.ds(0, hidden)], act_hbm.at[i], out_sems.at[slot, 0]),
                pltpu.make_async_copy(slope_buf.at[slot], slope_hbm.at[i], out_sems.at[slot, 1]),
            )

        ready_tokens(normed, act_buf)

        def image(i, carry):
            slot = i % 2

            @pl.when(i >= 2)
            def _():
                for copy in stores(i - 2, slot):
                    copy.wait()

            @pl.when(i == 0)
            def _():
                x_start(0)
                z_start(2)

            @pl.when(i == 6)
            def _():
                x_start(1)
                z_start(3)
                swap_start(0)

            @pl.when(i == 12)
            def _():
                x_start(2)
                z_start(4)
                swap_start(1)

            unit = take(grad_two_acc, image_rows(i))
            normed[0:patches] = (unit * vectors[0:1] + vectors[1:2]).astype(BF16)
            act, slope = gelu_and_slope(dot(tok_in[...], normed[...]))
            act_buf[slot, 0:hidden] = act.astype(BF16)
            slope_buf[slot] = slope.astype(BF16)
            put(result_acc, image_rows(i), dot(tok_out_t[...], act_buf[slot])[0:patches])
            for copy in stores(i, slot):
                copy.start()
            return carry

        lax.fori_loop(0, images, image, 0)
        for i in (images - 2, images - 1):
            for copy in stores(i, i % 2):
                copy.wait()
        cot_copy.wait()

        def mixed_store(b):
            return pltpu.make_async_copy(
                result_acc.at[:, span_rows(b)], mixed_hbm.at[:, span_rows(b)], mixed_sems.at[b]
            )

        live = jnp.broadcast_to(live_rows(STEP), (STEP, width))

        def span(b, carry):
            def step(s, inner):
                rows = span_rows(b, s)
                mixed = normed_two[rows].astype(F32) + take(result_acc, rows)
                put(result_acc, rows, mixed)
                unit, _ = row_stats(mixed)
                normed_two[rows] = (unit * vectors[2:3] + vectors[3:4]).astype(BF16)
                grad = grad_rows[rows].astype(F32) * live
                grad_rows[rows] = grad.astype(BF16)
                put(grad_two_acc, rows, jnp.zeros((STEP, width), F32))
                return inner + jnp.sum(grad.reshape(STEP // 8, 8, width), axis=0)

            carry = lax.fori_loop(0, steps, step, carry)
            mixed_store(b).start()

            @pl.when(b == 4)
            def _():
                x_start(3)
                z_start(5)

            return carry

        sums = lax.fori_loop(0, spans, span, jnp.zeros((8, width), F32))
        vector_sums[4:5] = jnp.sum(sums, axis=0, keepdims=True)
        for b in range(spans):
            mixed_store(b).wait()

    pl.run_scoped(
        token_forward,
        pltpu.VMEM((2, hidden + 128, width), BF16),
        pltpu.VMEM((2, hidden, width), BF16),
        pltpu.VMEM((256, width), BF16),
        pltpu.SemaphoreType.DMA((2, 2)),
        pltpu.SemaphoreType.DMA((spans,)),
    )

    def channel(act_all, slope_all, w_in, w_out, load_sems):
        chunk = w_in.shape[-1]

        def loads(j, p):
            return [
                pltpu.make_async_copy(
                    gathered.at[0, j, :, :, pl.ds(48 * b, 48)], w_in.at[p, :, :, :, pl.ds(256 * b, 256)], load_sems.at[b]
                )
                for b in range(2)
            ] + [
                pltpu.make_async_copy(
                    gathered.at[1, j, :, :, pl.ds(32 * b, 32)], w_out.at[p, :, :, :, pl.ds(256 * b, 256)],
                    load_sems.at[2 + b],
                )
                for b in range(3)
            ]

        swap_copy(0).wait()
        for copy in loads(0, 0):
            copy.start()
        for copy in loads(0, 0):
            copy.wait()

        def tick(j, carry):
            p = j % 2

            @pl.when(j >= 1)
            def _():
                core_copy(1 - p, piece).start()

            def block(b, inner):
                rows = pl.ds(pl.multiple_of(b * BLOCK, 16), BLOCK)
                up = w_in[p].reshape(width, chunk)
                down = w_out[p].reshape(chunk, width)
                pre = dot(normed_two[rows], up) + hidden_bias[j]
                grad_act = dot(grad_rows[rows], down, NT)
                act, slope = gelu_and_slope(pre)
                grad_pre = grad_act * slope
                hidden_sums[pl.ds(j, 1)] += jnp.sum(grad_pre, axis=0, keepdims=True)
                act_all[rows] = act.astype(BF16)
                slope_all[rows] = grad_pre.astype(BF16)
                forward_part = dot(act_all[rows], down)
                for t in range(tiles):
                    result_acc[t, rows] += forward_part[:, LANES * t : LANES * (t + 1)]
                backward_part = dot(slope_all[rows], up, NT)
                for t in range(tiles):
                    grad_two_acc[t, rows] += backward_part[:, LANES * t : LANES * (t + 1)]

                @pl.when((b == 0) & (j >= 1))
                def _():
                    cross_start(1 - p, piece)

                @pl.when((b == 0) & (j == 0))
                def _():
                    x_start(4)
                    swap_start(2)

                @pl.when((b == 2) & (j == 0))
                def _():
                    x_start(5)

                @pl.when((b == 2) & (j >= 2))
                def _():
                    shards[j - 2] = line_finish(p, piece)

                @pl.when((b == 1) & (j + 1 < CHUNKS))
                def _():
                    swap_copy(j + 1).wait()
                    for copy in loads(j + 1, 1 - p):
                        copy.start()

                @pl.when((b == 3) & (j + 3 < CHUNKS))
                def _():
                    swap_start(j + 3)

                return inner

            lax.fori_loop(0, total_rows // BLOCK, block, 0)
            up_grad = dot(normed_two[...], slope_all[...], TN)
            for b in range(2):
                grads[0, :, :, 48 * b : 48 * b + 48] = up_grad[:, 256 * b : 256 * b + 256].reshape(4, 4, 48, 256)
            down_grad = dot(act_all[...], grad_rows[...], TN)
            for b in range(3):
                grads[1, :, :, 32 * b : 32 * b + 32] = down_grad[:, 256 * b : 256 * b + 256].reshape(4, 4, 32, 256)

            @pl.when(j >= 1)
            def _():
                line_start(1 - p, piece)

            @pl.when(j + 1 < CHUNKS)
            def _():
                for copy in loads(j + 1, 1 - p):
                    copy.wait()

            return carry

        lax.fori_loop(0, CHUNKS, tick, 0)

    pl.run_scoped(
        channel,
        pltpu.VMEM((total_rows, 512), BF16),
        pltpu.VMEM((total_rows, 512), BF16),
        pltpu.VMEM((2, 4, 4, 48, 512), BF16),
        pltpu.VMEM((2, 4, 4, 32, 768), BF16),
        pltpu.SemaphoreType.DMA((5,)),
    )

    def stage_send(stage, out):
        return remote(stage, out, end_sems, (0,), partner)

    def stage_own(stage, out):
        return pltpu.make_async_copy(stage, out, end_sems.at[0, 2])

    def send_stages():
        @pl.when(c == 0)
        def _():
            stage_send(stage_in, ch_in_grad).start()
            stage_own(stage_in, ch_in_grad).start()

        @pl.when(c == 1)
        def _():
            stage_send(stage_out, ch_out_grad).start()
            stage_own(stage_out, ch_out_grad).start()

    def fill_stages():
        @pl.when(c == 0)
        def _():
            group = lax.broadcasted_iota(jnp.int32, (48, LANES), 1) >> 5
            for t in range(24):
                tile = None
                for g in range(4):
                    unit = LANES * t + 32 * g
                    o, j = unit // 192, unit % 192 // 32
                    b, source = o // 8, 32 * (o % 8)
                    part = shards[j, 48 * b : 48 * b + 48, source // LANES * LANES : (source // LANES + 1) * LANES]
                    shift = (32 * g - source) % LANES
                    part = part if shift == 0 else pltpu.roll(part, shift, 1)
                    tile = part if tile is None else jnp.where(group == g, part, tile)
                stage_in[:, LANES * t : LANES * (t + 1)] = tile

        @pl.when(c == 1)
        def _():
            for j in range(CHUNKS):
                for b in range(3):
                    stage_out[32 * j : 32 * j + 32, 256 * b : 256 * b + 256] = shards[j, 32 * b : 32 * b + 32]

    def token_backward(
        units, mixed_buf, act_buf, slope_buf, normed, mixed_low, pre_low, out_buf, grad_buf, x_sem, in_sems, mixed_sems, out_sems
    ):
        def loads(i, slot):
            return (
                pltpu.make_async_copy(act_hbm.at[i], act_buf.at[slot, pl.ds(0, hidden)], in_sems.at[slot, 0]),
                pltpu.make_async_copy(slope_hbm.at[i], slope_buf.at[slot], in_sems.at[slot, 1]),
            )

        def mixed_load(b, slot):
            return pltpu.make_async_copy(mixed_hbm.at[:, span_rows(b)], mixed_buf.at[slot], mixed_sems.at[slot])

        x_copy_back = pltpu.make_async_copy(tokens, normed_two, x_sem.at[0])
        mixed_load(0, 0).start()
        x_copy_back.start()
        core_copy(1, piece).start()
        for copy in loads(0, 0):
            copy.start()
        ready_tokens(normed, act_buf)
        mixed_low[192:256] = jnp.zeros((64, width), BF16)
        x_copy_back.wait()

        def span(b, carry):
            slot = b % 2

            @pl.when(b + 1 < spans)
            def _():
                mixed_load(b + 1, 1 - slot).start()

            mixed_load(b, slot).wait()

            def step(s, sums):
                rows = span_rows(b, s)
                inside = pl.ds(pl.multiple_of(s * STEP, 16), STEP)
                unit, root = row_stats(take(mixed_buf.at[slot], inside))
                grad = take(grad_two_acc, rows)
                weighted = grad * unit
                scaled = grad * vectors[2:3]
                inner = jnp.mean(scaled * unit, axis=-1, keepdims=True)
                mixed = grad_rows[rows].astype(F32) + root * (
                    scaled - jnp.mean(scaled, axis=-1, keepdims=True) - unit * inner
                )
                put(grad_two_acc, rows, mixed)
                unit, _ = row_stats(normed_two[rows].astype(F32))
                put(units, rows, unit)
                return (
                    sums[0] + jnp.sum(weighted.reshape(STEP // 8, 8, width), axis=0),
                    sums[1] + jnp.sum(grad.reshape(STEP // 8, 8, width), axis=0),
                )

            carry = lax.fori_loop(0, steps, step, carry)

            @pl.when(b == 6)
            def _():
                cross_start(1, piece)

            return carry

        zero = jnp.zeros((8, width), F32)
        sums = lax.fori_loop(0, spans, span, (zero, zero))
        vector_sums[2:3] = jnp.sum(sums[0], axis=0, keepdims=True)
        vector_sums[3:4] = jnp.sum(sums[1], axis=0, keepdims=True)

        def image(i, carry):
            slot = i % 2

            @pl.when(i + 1 < images)
            def _():
                for copy in loads(i + 1, 1 - slot):
                    copy.start()

            for copy in loads(i, slot):
                copy.wait()

            @pl.when(i == 0)
            def _():
                shards[CHUNKS - 2] = line_finish(0, piece)

            @pl.when(i == 5)
            def _():
                line_start(1, piece)

            @pl.when(i == 11)
            def _():
                shards[CHUNKS - 1] = line_finish(1, piece)
                fill_stages()
                send_stages()

            rows = image_rows(i)
            mixed_low[0:patches] = take(grad_two_acc, rows).astype(BF16)
            tok_out_sum[...] += dot(act_buf[slot], mixed_low[...], NT)
            grad_act = dot(tok_out[...], mixed_low[...])
            pre_low[...] = (grad_act * slope_buf[slot].astype(F32)).astype(BF16)
            unit = take(units, rows)
            normed[0:patches] = (unit * vectors[0:1] + vectors[1:2]).astype(BF16)
            tok_in_sum[...] += dot(pre_low[...], normed[...], NT)
            grad = dot(tok_in_t[...], pre_low[...])[0:patches]
            vector_sums[0:1] += jnp.sum(grad * unit, axis=0, keepdims=True)
            vector_sums[1:2] += jnp.sum(grad, axis=0, keepdims=True)
            put(units, rows, grad)
            return carry

        lax.fori_loop(0, images, image, 0)

        grads[0, :, :, 0:24] = tok_in_sum[...].reshape(4, 4, 24, 256)
        grads[1, :, :, 0:24] = tok_out_sum[0:hidden].reshape(4, 4, 24, 256)
        sums = vector_sums[...]
        hidden_rows = hidden_sums[...]
        for o in range(owners):
            moved = sums if o == 0 else pltpu.roll(sums, width - 48 * o, 1)
            grads[0, o // 4, o % 4, 24:32, 0:128] = moved[:, 0:128]
            grads[0, o // 4, o % 4, 24:32, 128:256] = jnp.zeros((8, 128), F32)
            grads[0, o // 4, o % 4, 31:32] = tok_out_sum[hidden : hidden + 1]
            moved = hidden_rows if o == 0 else pltpu.roll(hidden_rows, 512 - 32 * o, 1)
            grads[1, o // 4, o % 4, 24:32, 0:128] = moved[:, 0:128]
            grads[1, o // 4, o % 4, 24:32, 128:256] = jnp.zeros((8, 128), F32)
        core_copy(0, 32).start()

        def stores(b, slot):
            return (
                pltpu.make_async_copy(out_buf.at[slot], block_out.at[span_rows(b)], out_sems.at[slot, 0]),
                pltpu.make_async_copy(grad_buf.at[slot], input_grad.at[span_rows(b)], out_sems.at[slot, 1]),
            )

        live = jnp.broadcast_to(live_rows(STEP), (STEP, width))

        def last(b, carry):
            slot = b % 2

            @pl.when(b >= 2)
            def _():
                for copy in stores(b - 2, slot):
                    copy.wait()

            def step(s, inner):
                rows = span_rows(b, s)
                inside = pl.ds(pl.multiple_of(s * STEP, 16), STEP)
                unit, root = row_stats(normed_two[rows].astype(F32))
                scaled = take(units, rows) * vectors[0:1]
                mean = jnp.mean(scaled * unit, axis=-1, keepdims=True)
                grad_buf[slot, inside] = (
                    take(grad_two_acc, rows)
                    + root * (scaled - jnp.mean(scaled, axis=-1, keepdims=True) - unit * mean)
                ).astype(BF16)
                out_buf[slot, inside] = ((take(result_acc, rows) + vectors[4:5]) * live).astype(BF16)
                return inner

            lax.fori_loop(0, steps, step, 0)
            for copy in stores(b, slot):
                copy.start()

            @pl.when(b == 3)
            def _():
                cross_start(0, 32)

            @pl.when(b == 11)
            def _():
                line_start(0, 32)

            return carry

        lax.fori_loop(0, spans, last, 0)
        for b in (spans - 2, spans - 1):
            for copy in stores(b, b % 2):
                copy.wait()

    pl.run_scoped(
        token_backward,
        pltpu.VMEM((tiles, total_rows, LANES), F32),
        pltpu.VMEM((2, tiles, SPAN, LANES), F32),
        pltpu.VMEM((2, hidden + 128, width), BF16),
        pltpu.VMEM((2, hidden, width), BF16),
        pltpu.VMEM((256, width), BF16),
        pltpu.VMEM((256, width), BF16),
        pltpu.VMEM((hidden, width), BF16),
        pltpu.VMEM((2, SPAN, width), BF16),
        pltpu.VMEM((2, SPAN, width), BF16),
        pltpu.SemaphoreType.DMA((1,)),
        pltpu.SemaphoreType.DMA((2, 2)),
        pltpu.SemaphoreType.DMA((2,)),
        pltpu.SemaphoreType.DMA((2, 2)),
    )

    small_sum[...] = line_finish(0, 32)
    small_end = remote(small_sum, small_out.at[c], end_sems, (1,), partner)
    small_own = pltpu.make_async_copy(small_sum, small_out.at[c], end_sems.at[1, 2])
    small_end.start()
    small_own.start()
    small_end.wait()
    small_own.wait()

    @pl.when(c == 0)
    def _():
        stage_send(stage_in, ch_in_grad).wait_send()
        stage_own(stage_in, ch_in_grad).wait()
        stage_send(stage_out, ch_out_grad).wait_recv()

    @pl.when(c == 1)
    def _():
        stage_send(stage_out, ch_out_grad).wait_send()
        stage_own(stage_out, ch_out_grad).wait()
        stage_send(stage_in, ch_in_grad).wait_recv()


def finish(small, ch_in_sum, ch_out_sum, *outs):
    gain_one, bias_one, tok_in, tok_in_bias, tok_out, tok_out_bias, gain_two, bias_two, ch_in, ch_in_bias, ch_out, ch_out_bias = outs
    per_tok, patches = tok_in.shape
    ch_in[...] = ch_in_sum[...]
    ch_out[...] = ch_out_sum[...]
    tok_in[...] = small[0, 0:per_tok, 0:patches]
    tok_out[...] = small[1, 0:per_tok, 0:patches]
    column = jnp.broadcast_to(small[0, 0:32, 200:201], (32, LANES))
    flipped = jnp.transpose(jnp.concatenate([column, jnp.zeros((LANES - 32, LANES), F32)], axis=0))
    tok_in_bias[...] = flipped[0:1, 0:per_tok]
    tok_out_bias[...] = small[0, 31:32, 0:patches]
    for r, out in enumerate((gain_one, bias_one, gain_two, bias_two, ch_out_bias)):
        out[...] = small[0, 24 + r : 25 + r, 0 : out.shape[1]]
    for j in range(CHUNKS):
        ch_in_bias[j : j + 1] = small[1, 24 + j : 25 + j, 0 : ch_in_bias.shape[1]]


def per_device_fused(
    tokens, cotangent, counts, ln1_gain, ln1_bias, tok_in, tok_in_bias, tok_out, tok_out_bias,
    ln2_gain, ln2_bias, ch_in, ch_in_bias, ch_out, ch_out_bias,
):
    images, patches, width = tokens.shape
    per_in, inner = ch_in.shape
    per_out = ch_out.shape[0]
    per_tok = tok_in.shape[0]
    owners = width // per_in
    hidden = per_tok * owners
    each = per_out // CHUNKS
    chunk = each * owners
    rows = images * patches

    def by_patch(array):
        return array.transpose(1, 0, 2).reshape(rows, width)

    vector_row = jnp.concatenate(
        [ln1_gain, ln1_bias, ln2_gain, ln2_bias, ch_out_bias, tok_in_bias, ch_in_bias, tok_out_bias]
    )
    vector_row = jnp.pad(vector_row, (0, width - vector_row.shape[0]))[None]
    any_spec = pl.BlockSpec(memory_space=pl.ANY)
    vmem_spec = pl.BlockSpec(memory_space=pltpu.VMEM)
    vmem = pltpu.VMEM
    dma = pltpu.SemaphoreType.DMA
    shape = jax.ShapeDtypeStruct
    tiled = (width // LANES, rows, LANES)
    results = pl.pallas_call(
        mega,
        in_specs=[pl.BlockSpec(memory_space=pltpu.SMEM), any_spec, any_spec] + [vmem_spec] * 5,
        out_specs=[any_spec] * 9,
        out_shape=[
            shape((rows, width), BF16),
            shape((rows, width), BF16),
            shape(ch_in.shape, F32),
            shape(ch_out.shape, F32),
            shape((2, 32, 256), F32),
            shape((2, CHUNKS, 4, 4, 96, 256), BF16),
            shape((images, hidden, width), BF16),
            shape((images, hidden, width), BF16),
            shape(tiled, F32),
        ],
        scratch_shapes=[
            vmem((rows, width), BF16),
            vmem((rows, width), BF16),
            vmem(tiled, F32),
            vmem(tiled, F32),
            vmem((2, 4, 4, 96, 256), F32),
            vmem((2, 4, 4, 96, 256), F32),
            vmem((3, 4, 96, 256), BF16),
            vmem((4, 96, 256), F32),
            vmem((2, 3, 4, 96, 256), BF16),
            vmem((3, 96, 256), BF16),
            vmem((96, 256), F32),
            vmem((2, 3, 96, 256), BF16),
            vmem((CHUNKS, 96, 256), F32),
            vmem(ch_in.shape, F32),
            vmem(ch_out.shape, F32),
            vmem((32, 256), F32),
            vmem((CHUNKS, 96, 256), BF16),
            vmem((2, 4, 4, 32, 256), BF16),
            vmem((hidden, 256), BF16),
            vmem((256, hidden), BF16),
            vmem((hidden, 256), BF16),
            vmem((256, hidden + 128), BF16),
            vmem((8, width), F32),
            vmem((CHUNKS, 1, chunk), F32),
            vmem((8, width), F32),
            vmem((8, chunk), F32),
            vmem((hidden, 256), F32),
            vmem((hidden + 128, 256), F32),
            dma((2, 7)),
            dma((2, CHUNKS, 3)),
            dma((CHUNKS,)),
            dma((2, CHUNKS, 3)),
            dma((2, CHUNKS)),
            dma((2, 2)),
            dma((2, 2, 3)),
            dma((2, 2, 3)),
            dma((2, 3)),
        ],
        compiler_params=pltpu.CompilerParams(
            collective_id=0, has_side_effects=True, vmem_limit_bytes=61 * 1024 * 1024
        ),
        cost_estimate=pl.CostEstimate(
            flops=12 * rows * width * inner, bytes_accessed=100_000_000, transcendentals=rows * inner
        ),
    )(counts, by_patch(tokens), by_patch(cotangent), vector_row, tok_in, tok_out, ch_in, ch_out)
    block_out, input_grad, in_sum, out_sum, small = results[:5]
    line = shape((1, per_in), F32)
    outs = pl.pallas_call(
        finish,
        in_specs=[vmem_spec] * 3,
        out_specs=[vmem_spec] * 12,
        out_shape=[
            line, line, shape(tok_in.shape, F32), shape((1, per_tok), F32), shape(tok_out.shape, F32),
            shape((1, patches), F32), line, line, shape(ch_in.shape, F32), shape((CHUNKS, each), F32),
            shape(ch_out.shape, F32), line,
        ],
    )(small, in_sum, out_sum)

    def by_image(array):
        return array.reshape(patches, images, width).transpose(1, 0, 2)

    flat = (0, 1, 3, 5, 6, 7, 9, 11)
    outs = [out.reshape(-1) if n in flat else out for n, out in enumerate(outs)]
    return (by_image(block_out), by_image(input_grad), *outs)


def solution(mesh):
    fused = mesh.shape["dp"] == 2 and mesh.shape["fsdp"] == 16
    return jax.shard_map(
        per_device_fused if fused else per_device,
        mesh=mesh,
        in_specs=(
            P(("dp", "fsdp"), None, None),
            P(("dp", "fsdp"), None, None),
            P(("dp", "fsdp"), None),
            P("fsdp"),
            P("fsdp"),
            P("fsdp", None),
            P("fsdp"),
            P("fsdp", None),
            P(),
            P("fsdp"),
            P("fsdp"),
            P("fsdp", None),
            P("fsdp"),
            P("fsdp", None),
            P("fsdp"),
        ),
        out_specs=(
            P(("dp", "fsdp"), None, None),
            P(("dp", "fsdp"), None, None),
            P("fsdp"),
            P("fsdp"),
            P("fsdp", None),
            P("fsdp"),
            P("fsdp", None),
            P(),
            P("fsdp"),
            P("fsdp"),
            P("fsdp", None),
            P("fsdp"),
            P("fsdp", None),
            P("fsdp"),
        ),
        check_vma=False,
    )
```

```python
import jax
import jax.numpy as jnp
from jax import lax
from jax.experimental import pallas as pl
from jax.experimental.pallas import tpu as pltpu
from jax.sharding import PartitionSpec as P

EPSILON = 1e-06


def normalize(rows_in, gain, shift):
    centre = jnp.mean(rows_in, axis=-1, keepdims=True)
    centred = rows_in - centre
    spread = jnp.mean(centred * centred, axis=-1, keepdims=True)
    return centred * lax.rsqrt(spread + EPSILON) * gain + shift


def smooth(values):
    return jax.nn.gelu(values, approximate=True)


def forward(input_block, token_full, channel_full, output_shift):
    gain_one, shift_one, mixing_input_weight, mixing_input_bias, mixing_output_weight = token_full
    gain_two, shift_two, w_up, bias_up, w_down, bias_down = channel_full
    normalized_rows = normalize(
        input_block, gain_one.astype(jnp.float32), shift_one.astype(jnp.float32)
    )
    normalized_reduced = normalized_rows.astype(jnp.bfloat16)
    preactivation = (
        jnp.einsum(
            "qx,exj->eqj",
            mixing_input_weight,
            normalized_reduced,
            preferred_element_type=jnp.float32,
        )
        + mixing_input_bias.astype(jnp.float32)[None, :, None]
    )
    activation_reduced = smooth(preactivation).astype(jnp.bfloat16)
    branch_output = jnp.einsum(
        "hp,zhi->zpi", mixing_output_weight, activation_reduced, preferred_element_type=jnp.float32
    )
    mixing_rows = input_block + branch_output + output_shift.astype(jnp.float32)[None, :, None]
    normed_two = normalize(mixing_rows, gain_two.astype(jnp.float32), shift_two.astype(jnp.float32))
    normed_two_low = normed_two.astype(jnp.bfloat16)
    pre_two = jnp.einsum(
        "bsd,df->bsf", normed_two_low, w_up, preferred_element_type=jnp.float32
    ) + bias_up.astype(jnp.float32)
    act_two_low = smooth(pre_two).astype(jnp.bfloat16)
    result = (
        mixing_rows
        + jnp.einsum("bsf,fd->bsd", act_two_low, w_down, preferred_element_type=jnp.float32)
        + bias_down.astype(jnp.float32)
    )
    kept = (
        normalized_reduced,
        preactivation,
        activation_reduced,
        mixing_rows,
        normed_two_low,
        pre_two,
        act_two_low,
    )
    return (result, kept)


def backward(grad_out, input_block, kept, token_full, channel_full):
    (
        normalized_reduced,
        preactivation,
        activation_reduced,
        mixing_rows,
        normed_two_low,
        pre_two,
        act_two_low,
    ) = kept
    gain_one, shift_one, mixing_input_weight, mixing_input_bias, mixing_output_weight = token_full
    gain_two, shift_two, w_up, bias_up, w_down, bias_down = channel_full
    grad_out_low = grad_out.astype(jnp.bfloat16)
    grad_act_two = jnp.einsum(
        "bsd,fd->bsf", grad_out_low, w_down, preferred_element_type=jnp.float32
    )
    grad_w_down = jnp.einsum(
        "bsf,bsd->fd", act_two_low, grad_out_low, preferred_element_type=jnp.float32
    )
    grad_bias_down = jnp.sum(grad_out, axis=(0, 1))
    grad_pre_two = jax.vjp(smooth, pre_two)[1](grad_act_two)[0]
    grad_bias_up = jnp.sum(grad_pre_two, axis=(0, 1))
    grad_pre_two_low = grad_pre_two.astype(jnp.bfloat16)
    grad_normed_two = jnp.einsum(
        "bsf,df->bsd", grad_pre_two_low, w_up, preferred_element_type=jnp.float32
    )
    grad_w_up = jnp.einsum(
        "bsd,bsf->df", normed_two_low, grad_pre_two_low, preferred_element_type=jnp.float32
    )
    norm_two_back = jax.vjp(
        normalize, mixing_rows, gain_two.astype(jnp.float32), shift_two.astype(jnp.float32)
    )[1]
    grad_through, grad_gain_two, grad_shift_two = norm_two_back(grad_normed_two)
    grad_mixed = grad_out + grad_through
    grad_out_shift = jnp.sum(grad_mixed, axis=(0, 2))
    mixing_gradient_reduced = grad_mixed.astype(jnp.bfloat16)
    grad_act = jnp.einsum(
        "qx,exj->eqj",
        mixing_output_weight,
        mixing_gradient_reduced,
        preferred_element_type=jnp.float32,
    )
    grad_w_mix_out = jnp.einsum(
        "oaq,oeq->ae",
        activation_reduced,
        mixing_gradient_reduced,
        preferred_element_type=jnp.float32,
    )
    grad_pre = jax.vjp(smooth, preactivation)[1](grad_act)[0]
    grad_bias_mix_in = jnp.sum(grad_pre, axis=(0, 2))
    preactivation_gradient_reduced = grad_pre.astype(jnp.bfloat16)
    grad_normed = jnp.einsum(
        "hp,zhi->zpi",
        mixing_input_weight,
        preactivation_gradient_reduced,
        preferred_element_type=jnp.float32,
    )
    grad_w_mix_in = jnp.einsum(
        "oaq,oeq->ae",
        preactivation_gradient_reduced,
        normalized_reduced,
        preferred_element_type=jnp.float32,
    )
    norm_one_back = jax.vjp(
        normalize, input_block, gain_one.astype(jnp.float32), shift_one.astype(jnp.float32)
    )[1]
    grad_inner, grad_gain_one, grad_shift_one = norm_one_back(grad_normed)
    grad_x = grad_mixed + grad_inner
    grad_list = (
        grad_gain_one,
        grad_shift_one,
        grad_w_mix_in,
        grad_bias_mix_in,
        grad_w_mix_out,
        grad_gain_two,
        grad_shift_two,
        grad_w_up,
        grad_bias_up,
        grad_w_down,
        grad_bias_down,
    )
    return (grad_x, grad_list, grad_out_shift)


def per_device(
    tokens,
    cotangent,
    counts,
    ln1_gain,
    ln1_bias,
    tok_in,
    tok_in_bias,
    tok_out,
    tok_out_bias,
    ln2_gain,
    ln2_bias,
    ch_in,
    ch_in_bias,
    ch_out,
    ch_out_bias,
):
    micro_total = counts.shape[1]
    per_micro = tokens.shape[0] // micro_total
    outputs = []
    input_grads = []
    grad_sums = None
    shift_sum = jnp.zeros((tok_out_bias.shape[0],), jnp.float32)
    for micro in range(micro_total):
        lower = micro * per_micro
        input_block = tokens[lower : lower + per_micro].astype(jnp.float32)
        live_rows = (jnp.arange(per_micro) < counts[0, micro]).astype(jnp.float32)[:, None, None]
        grad_out = cotangent[lower : lower + per_micro].astype(jnp.float32) * live_rows
        token_full = (
            lax.all_gather(ln1_gain, "fsdp", axis=0, tiled=True),
            lax.all_gather(ln1_bias, "fsdp", axis=0, tiled=True),
            lax.all_gather(tok_in, "fsdp", axis=0, tiled=True),
            lax.all_gather(tok_in_bias, "fsdp", axis=0, tiled=True),
            lax.all_gather(tok_out, "fsdp", axis=0, tiled=True),
        )
        channel_full = (
            lax.all_gather(ln2_gain, "fsdp", axis=0, tiled=True),
            lax.all_gather(ln2_bias, "fsdp", axis=0, tiled=True),
            lax.all_gather(ch_in, "fsdp", axis=0, tiled=True),
            lax.all_gather(ch_in_bias, "fsdp", axis=0, tiled=True),
            lax.all_gather(ch_out, "fsdp", axis=0, tiled=True),
            lax.all_gather(ch_out_bias, "fsdp", axis=0, tiled=True),
        )
        result, kept = forward(input_block, token_full, channel_full, tok_out_bias)
        outputs.append((result * live_rows).astype(jnp.bfloat16))
        token_back = (
            lax.all_gather(ln1_gain, "fsdp", axis=0, tiled=True),
            lax.all_gather(ln1_bias, "fsdp", axis=0, tiled=True),
            lax.all_gather(tok_in, "fsdp", axis=0, tiled=True),
            lax.all_gather(tok_in_bias, "fsdp", axis=0, tiled=True),
            lax.all_gather(tok_out, "fsdp", axis=0, tiled=True),
        )
        channel_back = (
            lax.all_gather(ln2_gain, "fsdp", axis=0, tiled=True),
            lax.all_gather(ln2_bias, "fsdp", axis=0, tiled=True),
            lax.all_gather(ch_in, "fsdp", axis=0, tiled=True),
            lax.all_gather(ch_in_bias, "fsdp", axis=0, tiled=True),
            lax.all_gather(ch_out, "fsdp", axis=0, tiled=True),
            lax.all_gather(ch_out_bias, "fsdp", axis=0, tiled=True),
        )
        grad_x, grad_list, grad_out_shift = backward(
            grad_out, input_block, kept, token_back, channel_back
        )
        input_grads.append(grad_x.astype(jnp.bfloat16))
        shift_sum = shift_sum + grad_out_shift
        grad_sums = (
            grad_list
            if grad_sums is None
            else tuple(jax.tree.map(jnp.add, tuple(grad_sums), tuple(grad_list)))
        )
    grad_sums = (
        lax.psum_scatter(grad_sums[0], "fsdp", scatter_dimension=0, tiled=True),
        lax.psum_scatter(grad_sums[1], "fsdp", scatter_dimension=0, tiled=True),
        lax.psum_scatter(grad_sums[2], "fsdp", scatter_dimension=0, tiled=True),
        lax.psum_scatter(grad_sums[3], "fsdp", scatter_dimension=0, tiled=True),
        lax.psum_scatter(grad_sums[4], "fsdp", scatter_dimension=0, tiled=True),
        lax.psum_scatter(grad_sums[5], "fsdp", scatter_dimension=0, tiled=True),
        lax.psum_scatter(grad_sums[6], "fsdp", scatter_dimension=0, tiled=True),
        lax.psum_scatter(grad_sums[7], "fsdp", scatter_dimension=0, tiled=True),
        lax.psum_scatter(grad_sums[8], "fsdp", scatter_dimension=0, tiled=True),
        lax.psum_scatter(grad_sums[9], "fsdp", scatter_dimension=0, tiled=True),
        lax.psum_scatter(grad_sums[10], "fsdp", scatter_dimension=0, tiled=True),
    )
    shards = lax.psum(
        (
            grad_sums[0],
            grad_sums[1],
            grad_sums[2],
            grad_sums[3],
            grad_sums[4],
            grad_sums[5],
            grad_sums[6],
            grad_sums[7],
            grad_sums[8],
            grad_sums[9],
            grad_sums[10],
        ),
        "dp",
    )
    shift_total = lax.psum(shift_sum, ("dp", "fsdp"))
    block_out = jnp.concatenate(outputs, axis=0)
    input_grad = jnp.concatenate(input_grads, axis=0)
    return (
        block_out,
        input_grad,
        shards[0],
        shards[1],
        shards[2],
        shards[3],
        shards[4],
        shift_total,
        shards[5],
        shards[6],
        shards[7],
        shards[8],
        shards[9],
        shards[10],
    )


MESH = pl.DeviceIdType.MESH
NN = (((1,), (0,)), ((), ()))
NT = (((1,), (1,)), ((), ()))
TN = (((0,), (0,)), ((), ()))
F32 = jnp.float32
BF16 = jnp.bfloat16
CHUNKS = 6
BLOCK = 784
SPAN = 224
LANES = 128
C_A = 0.7978845608
C_B = 0.7978845608 * 0.044715


def dot(left, right, dims=NN):
    return lax.dot_general(left, right, dims, preferred_element_type=F32)


def gelu_and_slope(v):
    ratio = C_B * (v * v) + C_A
    t = jnp.tanh(v * ratio)
    h = 0.5 * t + 0.5
    act = v * h
    slope = h + act * (1.0 - t) * (3.0 * ratio - 2.0 * C_A)
    return act, slope


def row_stats(v):
    mean = jnp.mean(v, axis=-1, keepdims=True)
    centred = v - mean
    spread = jnp.mean(centred * centred, axis=-1, keepdims=True)
    root = lax.rsqrt(spread + EPSILON)
    return centred * root, root, mean


def take(buf, rows, count=6):
    return jnp.concatenate([buf.at[t][rows, :] for t in range(count)], axis=1)


def put(buf, rows, value):
    for t in range(value.shape[1] // LANES):
        buf.at[t][rows, :] = value[:, LANES * t : LANES * (t + 1)]


def mega(
    counts, tokens, cotangent, vector_row, tok_in_own, tok_out_own, ch_in_own, ch_out_own,
    block_out, input_grad, ch_in_grad, ch_out_grad, small_out, gathered, act_hbm, slope_hbm, unit_two_hbm,
    normed_two, grad_rows, result_acc, grad_two_acc, stats,
    grads, core_in, cross_out, cross_keep, cross_in, line_out, line_keep, line_in, shards, stage_in,
    small_sum, own_weights, small, tok_in, tok_in_t, tok_out, tok_out_t, vectors, hidden_bias,
    vector_sums, hidden_sums, tok_in_sum, tok_out_sum,
    small_sems, z_sems, z_local, x_sems, swap_sems, core_sems, cross_sems, line_sems, end_sems,
):
    total_rows, width = tokens.shape
    images, hidden = act_hbm.shape[0], act_hbm.shape[1]
    patches = total_rows // images
    per_micro = images // counts.shape[1]
    owners = 16
    tiles = width // LANES
    c = lax.axis_index("dp")
    f = lax.axis_index("fsdp")
    zi, qi = f // 4, f % 4
    partner = (1 - c, f)

    def cross(k):
        return (c, zi * 4 + (qi ^ k))

    def line(k):
        return (c, (zi ^ k) * 4 + qi)

    def remote(src, dst, sems, index, device):
        return pltpu.make_async_remote_copy(
            src_ref=src, dst_ref=dst, send_sem=sems.at[(0,) + index], recv_sem=sems.at[(1,) + index],
            device_id=device, device_id_type=MESH,
        )

    barrier = pltpu.get_barrier_semaphore()
    for device in [partner] + [cross(k) for k in (1, 2, 3)] + [line(k) for k in (1, 2, 3)]:
        pl.semaphore_signal(barrier, inc=1, device_id=device, device_id_type=MESH)

    row = vector_row[...].astype(F32)

    def vector_at(offset, length, lanes=256):
        moved = row if offset == 0 else pltpu.roll(row, width - offset, 1)
        lane = lax.broadcasted_iota(jnp.int32, (1, lanes), 1)
        return jnp.where(lane < length, moved[:, 0:lanes], 0.0)

    lane = lax.broadcasted_iota(jnp.int32, (24, 256), 1)
    bias_column = jnp.transpose(jnp.broadcast_to(vector_at(240, 24, LANES), (LANES, LANES)))[0:24, 0:1]
    pad = jnp.zeros((24, 256 - patches), F32)
    padded = jnp.concatenate([tok_in_own[...].astype(F32), pad], axis=1)
    padded = jnp.where(lane == 200, jnp.broadcast_to(bias_column, (24, 256)), padded)
    rows_a = [vector_at(48 * r, 48) for r in range(5)] + [vector_at(264, 192), jnp.zeros((2, 256), F32)]
    packed_a = jnp.concatenate([padded] + rows_a, axis=0)
    padded = jnp.concatenate([tok_out_own[...].astype(F32), pad], axis=1)
    bias_rows = jnp.concatenate([vector_at(456, patches), jnp.zeros((7, 256), F32)], axis=0)
    packed_b = jnp.concatenate([padded, bias_rows], axis=0)
    small[c, zi, qi] = jnp.where(c == 0, packed_a, packed_b).astype(BF16)

    def small_line(k):
        return remote(small.at[c, zi, qi], small.at[c, zi, qi], small_sems, (k - 1,), line(k))

    def small_cross(k):
        return remote(small.at[c, :, qi], small.at[c, :, qi], small_sems, (k + 2,), cross(k))

    def small_swap():
        return remote(small.at[c], small.at[c], small_sems, (6,), partner)

    def z_copy(j, k):
        return remote(own_weights.at[j], gathered.at[c, j, zi, qi], z_sems, (j, k - 1), line(k))

    def z_own(j):
        return pltpu.make_async_copy(own_weights.at[j], gathered.at[c, j, zi, qi], z_local.at[j])

    def x_copy(j, k):
        return remote(gathered.at[c, j, :, qi], gathered.at[c, j, :, qi], x_sems, (j, k - 1), cross(k))

    def swap_copy(j):
        return remote(gathered.at[c, j], gathered.at[c, j], swap_sems, (j,), partner)

    def z_start(j):
        z_own(j).start()
        for k in (1, 2, 3):
            z_copy(j, k).start()

    def x_start(j):
        for k in (1, 2, 3):
            z_copy(j, k).wait()
        z_own(j).wait()
        for k in (1, 2, 3):
            x_copy(j, k).start()

    def swap_start(j):
        for k in (1, 2, 3):
            x_copy(j, k).wait()
        swap_copy(j).start()

    def core_copy(p, rows):
        return remote(
            grads.at[1 - c, :, :, pl.ds(0, rows)], core_in.at[p, :, :, pl.ds(0, rows)], core_sems, (p,), partner
        )

    def cross_copy(p, rows, k):
        return remote(
            cross_out.at[k - 1, :, pl.ds(0, rows)], cross_in.at[p, k - 1, :, pl.ds(0, rows)],
            cross_sems, (p, k - 1), cross(k),
        )

    def line_copy(p, rows, k):
        return remote(
            line_out.at[k - 1, pl.ds(0, rows)], line_in.at[p, k - 1, pl.ds(0, rows)], line_sems, (p, k - 1), line(k)
        )

    def cross_start(p, rows):
        core_copy(p, rows).wait()

        def per_line(z, carry):
            for k in range(4):
                q = qi ^ k
                total = grads[c, z, q, 0:rows] + core_in[p, z, q, 0:rows]
                if k == 0:
                    cross_keep[z, 0:rows] = total
                else:
                    cross_out[k - 1, z, 0:rows] = total.astype(BF16)
            return carry

        lax.fori_loop(0, 4, per_line, 0)
        for k in (1, 2, 3):
            cross_copy(p, rows, k).start()

    def line_start(p, rows):
        for k in (1, 2, 3):
            cross_copy(p, rows, k).wait()
        for k in range(4):
            z = zi ^ k
            total = cross_keep[z, 0:rows]
            for m in range(3):
                total = total + cross_in[p, m, z, 0:rows].astype(F32)
            if k == 0:
                line_keep[0:rows] = total
            else:
                line_out[k - 1, 0:rows] = total.astype(BF16)
        for k in (1, 2, 3):
            line_copy(p, rows, k).start()

    def line_finish(p, rows):
        for k in (1, 2, 3):
            line_copy(p, rows, k).wait()
        total = line_keep[0:rows]
        for m in range(3):
            total = total + line_in[p, m, 0:rows].astype(F32)
        return total

    piece = grads.shape[3]

    def live_rows():
        image = lax.broadcasted_iota(jnp.int32, (images, 1), 0)
        live = jnp.zeros((images, 1), F32)
        for micro in range(counts.shape[1]):
            inside = (image >= micro * per_micro) & (image < micro * per_micro + counts[0, micro])
            live = jnp.where(inside, 1.0, live)
        return jnp.broadcast_to(live, (images, width))

    def masked(value, live):
        return (value.reshape(SPAN // images, images, width) * live[None]).reshape(SPAN, width)

    def row_sum(value):
        return jnp.sum(value.reshape(4, SPAN // 32, 8, width).sum(1), axis=0)

    stat_lane = lax.broadcasted_iota(jnp.int32, (SPAN, LANES), 1)

    def span_rows(b):
        return pl.ds(pl.multiple_of(b * SPAN, 16), SPAN)

    spans = total_rows // SPAN

    def image_rows(i):
        return pl.ds(i, patches, stride=images)

    def own_rows():
        @pl.when(c == 0)
        def _():
            group = lax.broadcasted_iota(jnp.int32, (48, LANES), 1) >> 5
            for j in range(CHUNKS):
                for b in range(2):
                    for t in range(2):
                        tile = None
                        for g in range(4):
                            source = 192 * (8 * b + 4 * t + g) + 32 * j
                            part = ch_in_own[:, source // LANES * LANES : (source // LANES + 1) * LANES].astype(F32)
                            shift = (32 * g - source) % LANES
                            part = part if shift == 0 else pltpu.roll(part, shift, 1)
                            tile = part if tile is None else jnp.where(group == g, part, tile)
                        own_weights[j, 48 * b : 48 * b + 48, LANES * t : LANES * (t + 1)] = tile.astype(BF16)

        @pl.when(c == 1)
        def _():
            for j in range(CHUNKS):
                for b in range(3):
                    own_weights[j, 32 * b : 32 * b + 32] = ch_out_own[32 * j : 32 * j + 32, 256 * b : 256 * b + 256]

    def norm_one(load_sems):
        def loads(b):
            return (
                pltpu.make_async_copy(tokens.at[span_rows(b)], normed_two.at[span_rows(b)], load_sems.at[0, b]),
                pltpu.make_async_copy(cotangent.at[span_rows(b)], grad_rows.at[span_rows(b)], load_sems.at[1, b]),
            )

        for b in range(spans):
            for copy in loads(b):
                copy.start()
        pl.semaphore_wait(barrier, 7)
        for k in (1, 2, 3):
            small_line(k).start()
        own_rows()
        z_start(0)
        live = live_rows()

        def span(b, carry):
            for copy in loads(b):
                copy.wait()
            rows = span_rows(b)
            unit, root, mean = row_stats(normed_two[rows].astype(F32))
            put(grad_two_acc, rows, unit)
            stats[rows] = jnp.where(stat_lane < 32, root, mean)
            grad = masked(grad_rows[rows].astype(F32), live)
            grad_rows[rows] = grad.astype(BF16)

            @pl.when(b == 4)
            def _():
                for k in (1, 2, 3):
                    small_line(k).wait()
                for k in (1, 2, 3):
                    small_cross(k).start()
                z_start(1)

            @pl.when(b == 10)
            def _():
                for k in (1, 2, 3):
                    small_cross(k).wait()
                small_swap().start()

            return carry + row_sum(grad)

        sums = lax.fori_loop(0, spans, span, jnp.zeros((8, width), F32))
        vector_sums[...] = jnp.zeros(vector_sums.shape, F32)
        vector_sums[4:5] = jnp.sum(sums, axis=0, keepdims=True)
    pl.run_scoped(
        norm_one,
        pltpu.SemaphoreType.DMA((2, spans)),
    )
    hidden_sums[...] = jnp.zeros(hidden_sums.shape, F32)
    tok_in_sum[...] = jnp.zeros(tok_in_sum.shape, F32)
    tok_out_sum[...] = jnp.zeros(tok_out_sum.shape, F32)
    small_swap().wait()

    part_a = small[0].astype(F32).reshape(owners, 32, 256)
    part_b = small[1].astype(F32).reshape(owners, 32, 256)
    full_in = part_a[:, 0:24].reshape(hidden, 256)
    full_out = part_b[:, 0:24].reshape(hidden, 256)
    tok_in[...] = full_in.astype(BF16)
    tok_in_t[...] = jnp.transpose(full_in).astype(BF16)
    tok_out[...] = full_out.astype(BF16)
    out_rows = jnp.concatenate([full_out, bias_rows, jnp.zeros((120, 256), F32)], axis=0)
    tok_out_t[...] = jnp.transpose(out_rows).astype(BF16)

    flat_a = part_a.reshape(owners * 32, 256).astype(BF16)
    pick_r = lax.broadcasted_iota(jnp.int32, (8, owners * 32), 0)
    pick_p = lax.broadcasted_iota(jnp.int32, (8, owners * 32), 1)
    pick = jnp.where((pick_p & 31) == 24 + pick_r, 1.0, 0.0).astype(BF16)
    col = lax.broadcasted_iota(jnp.int32, (256, width), 1)
    lane = lax.broadcasted_iota(jnp.int32, (256, width), 0)
    spread = jnp.where(lane == col - 48 * ((col * 43691) >> 21), 1.0, 0.0).astype(BF16)
    own_n = (lax.broadcasted_iota(jnp.int32, (owners * 32, width), 1) * 43691) >> 21
    own_p = lax.broadcasted_iota(jnp.int32, (owners * 32, width), 0) >> 5
    vectors[...] = dot(pick, jnp.where(own_n == own_p, dot(flat_a, spread), 0.0).astype(BF16))
    span_n = owners * 32
    own_n = lax.broadcasted_iota(jnp.int32, (span_n, span_n), 1) >> 5
    own_p = lax.broadcasted_iota(jnp.int32, (span_n, span_n), 0) >> 5
    col = lax.broadcasted_iota(jnp.int32, (256, span_n), 1)
    lane = lax.broadcasted_iota(jnp.int32, (256, span_n), 0)
    for j in range(CHUNKS):
        spread = jnp.where(lane == 32 * j + (col & 31), 1.0, 0.0).astype(BF16)
        rows = dot(pick, jnp.where(own_n == own_p, dot(flat_a, spread), 0.0).astype(BF16))
        hidden_bias[j] = rows[5:6]

    ones_low = jnp.where(lax.broadcasted_iota(jnp.int32, (64, width), 0) == 8, 1.0, 0.0).astype(BF16)
    ones_act = jnp.where(lax.broadcasted_iota(jnp.int32, (128, width), 0) == 0, 1.0, 0.0).astype(BF16)

    def token_forward(act_buf, slope_buf, normed, unit_buf, out_sems, unit_sems):
        def stores(i, slot):
            return (
                pltpu.make_async_copy(act_buf.at[slot, pl.ds(0, hidden)], act_hbm.at[i], out_sems.at[slot, 0]),
                pltpu.make_async_copy(slope_buf.at[slot], slope_hbm.at[i], out_sems.at[slot, 1]),
            )

        for slot in range(4):
            act_buf[slot, hidden : hidden + 128] = ones_act
        for n in range(2):
            normed[n, 192:256] = ones_low

        def pair(g, carry):
            base = 2 * (g % 2)

            @pl.when(g >= 2)
            def _():
                for n in range(2):
                    for copy in stores(2 * g - 4 + n, base + n):
                        copy.wait()

            @pl.when(g == 0)
            def _():
                x_start(0)
                z_start(2)

            @pl.when(g == 4)
            def _():
                x_start(1)
                z_start(3)

            for n in range(2):
                unit = take(grad_two_acc, image_rows(2 * g + n))
                normed[n, 0:patches] = (unit * vectors[0:1] + vectors[1:2]).astype(BF16)
            pre = [dot(tok_in[...], normed[n]) for n in range(2)]
            for n in range(2):
                act, slope = gelu_and_slope(pre[n])
                act_buf[base + n, 0:hidden] = act.astype(BF16)
                slope_buf[base + n] = slope.astype(BF16)
            mixed = [dot(tok_out_t[...], act_buf[base + n]) for n in range(2)]
            for n in range(2):
                put(result_acc, image_rows(2 * g + n), mixed[n][0:patches])
                for copy in stores(2 * g + n, base + n):
                    copy.start()
            return carry

        lax.fori_loop(0, images // 2, pair, 0)
        for i in range(images - 4, images):
            for copy in stores(i, i % 4):
                copy.wait()
        swap_start(0)
        x_start(2)
        z_start(4)

        def unit_two_store(b):
            return pltpu.make_async_copy(unit_buf.at[b % 4], unit_two_hbm.at[span_rows(b)], unit_sems.at[b % 4])

        def span(b, carry):
            rows = span_rows(b)

            @pl.when(b >= 4)
            def _():
                unit_two_store(b - 4).wait()

            mixed = normed_two[rows].astype(F32) + take(result_acc, rows)
            put(result_acc, rows, mixed)
            unit, root, _ = row_stats(mixed)
            stats[rows] = jnp.where(stat_lane < 64, stats[rows], root)
            unit_buf[b % 4] = unit.astype(BF16)
            unit_two_store(b).start()
            normed_two[rows] = (unit * vectors[2:3] + vectors[3:4]).astype(BF16)
            put(grad_two_acc, rows, jnp.zeros((SPAN, width), F32))

            @pl.when(b == 10)
            def _():
                swap_copy(0).wait()
                swap_start(1)
                x_start(3)
                z_start(5)

            return carry

        lax.fori_loop(0, spans, span, 0)
        for b in range(spans - 4, spans):
            unit_two_store(b).wait()

    pl.run_scoped(
        token_forward,
        pltpu.VMEM((4, hidden + 128, width), BF16),
        pltpu.VMEM((4, hidden, width), BF16),
        pltpu.VMEM((2, 256, width), BF16),
        pltpu.VMEM((4, SPAN, width), BF16),
        pltpu.SemaphoreType.DMA((4, 2)),
        pltpu.SemaphoreType.DMA((4,)),
    )

    def channel(act_all, slope_all, w_in, w_out, load_sems):
        chunk = w_in.shape[-1]

        def loads(j, p):
            return [
                pltpu.make_async_copy(
                    gathered.at[0, j, :, :, pl.ds(48 * b, 48)], w_in.at[p, :, :, :, pl.ds(256 * b, 256)], load_sems.at[b]
                )
                for b in range(2)
            ] + [
                pltpu.make_async_copy(
                    gathered.at[1, j, :, :, pl.ds(32 * b, 32)], w_out.at[p, :, :, :, pl.ds(256 * b, 256)],
                    load_sems.at[2 + b],
                )
                for b in range(3)
            ]

        for copy in loads(0, 0):
            copy.start()
        for copy in loads(0, 0):
            copy.wait()

        def tick(j, carry):
            p = j % 2

            @pl.when(j >= 1)
            def _():
                core_copy(1 - p, piece).start()

            def block(b, inner):
                rows = pl.ds(pl.multiple_of(b * BLOCK, 16), BLOCK)
                up = w_in[p].reshape(width, chunk)
                down = w_out[p].reshape(chunk, width)
                pre = dot(normed_two[rows], up) + hidden_bias[j]
                grad_act = dot(grad_rows[rows], down, NT)
                act, slope = gelu_and_slope(pre)
                grad_pre = grad_act * slope
                hidden_sums[j] += jnp.sum(grad_pre.reshape(BLOCK // 112, 14, 8, chunk).sum(1), axis=0)
                act_all[rows] = act.astype(BF16)
                slope_all[rows] = grad_pre.astype(BF16)
                forward_part = dot(act_all[rows], down)
                for t in range(tiles):
                    result_acc[t, rows] += forward_part[:, LANES * t : LANES * (t + 1)]
                backward_part = dot(slope_all[rows], up, NT)
                for t in range(tiles):
                    grad_two_acc[t, rows] += backward_part[:, LANES * t : LANES * (t + 1)]

                @pl.when((b == 0) & (j >= 1))
                def _():
                    cross_start(1 - p, piece)

                @pl.when((b == 0) & (j == 0))
                def _():
                    x_start(4)
                    swap_start(2)

                @pl.when((b == 2) & (j == 0))
                def _():
                    x_start(5)

                @pl.when((b == 2) & (j >= 2))
                def _():
                    shards[j - 2] = line_finish(p, piece)

                @pl.when((b == 1) & (j + 1 < CHUNKS))
                def _():
                    swap_copy(j + 1).wait()
                    for copy in loads(j + 1, 1 - p):
                        copy.start()

                @pl.when((b == 3) & (j + 3 < CHUNKS))
                def _():
                    swap_start(j + 3)

                return inner

            lax.fori_loop(0, total_rows // BLOCK, block, 0)
            up_grad = dot(normed_two[...], slope_all[...], TN)
            for b in range(2):
                grads[0, :, :, 48 * b : 48 * b + 48] = up_grad[:, 256 * b : 256 * b + 256].reshape(4, 4, 48, 256)
            down_grad = dot(act_all[...], grad_rows[...], TN)
            for b in range(3):
                grads[1, :, :, 32 * b : 32 * b + 32] = down_grad[:, 256 * b : 256 * b + 256].reshape(4, 4, 32, 256)

            @pl.when(j >= 1)
            def _():
                line_start(1 - p, piece)

            @pl.when(j + 1 < CHUNKS)
            def _():
                for copy in loads(j + 1, 1 - p):
                    copy.wait()

            return carry

        lax.fori_loop(0, CHUNKS, tick, 0)

    pl.run_scoped(
        channel,
        pltpu.VMEM((total_rows, 512), BF16),
        pltpu.VMEM((total_rows, 512), BF16),
        pltpu.VMEM((2, 4, 4, 48, 512), BF16),
        pltpu.VMEM((2, 4, 4, 32, 768), BF16),
        pltpu.SemaphoreType.DMA((5,)),
    )

    def stage_out_copy(b):
        return remote(
            shards.at[:, pl.ds(32 * b, 32)], ch_out_grad.at[:, :, pl.ds(256 * b, 256)], end_sems, (b,), partner
        )

    def stage_out_own(b):
        return pltpu.make_async_copy(
            shards.at[:, pl.ds(32 * b, 32)], ch_out_grad.at[:, :, pl.ds(256 * b, 256)], end_sems.at[0, 4 + b]
        )

    def send_stages():
        @pl.when(c == 0)
        def _():
            remote(stage_in, ch_in_grad, end_sems, (0,), partner).start()
            pltpu.make_async_copy(stage_in, ch_in_grad, end_sems.at[0, 4]).start()

        @pl.when(c == 1)
        def _():
            for b in range(3):
                stage_out_copy(b).start()
                stage_out_own(b).start()

    def fill_stages():
        @pl.when(c == 0)
        def _():
            group = lax.broadcasted_iota(jnp.int32, (48, LANES), 1) >> 5
            for t in range(24):
                tile = None
                for g in range(4):
                    unit = LANES * t + 32 * g
                    o, j = unit // 192, unit % 192 // 32
                    b, source = o // 8, 32 * (o % 8)
                    part = shards[j, 48 * b : 48 * b + 48, source // LANES * LANES : (source // LANES + 1) * LANES]
                    shift = (32 * g - source) % LANES
                    part = part if shift == 0 else pltpu.roll(part, shift, 1)
                    tile = part if tile is None else jnp.where(group == g, part, tile)
                stage_in[:, LANES * t : LANES * (t + 1)] = tile

    def token_backward(units, unit_buf, out_buf, x_load_sems, in_sems, unit_sems, out_sems):
        def act_at(slot, count):
            return normed_two.at[pl.ds(pl.multiple_of(512 * slot, 16), count)]

        def slope_at(slot):
            return grad_rows.at[pl.ds(pl.multiple_of(384 * slot, 16), hidden)]

        def loads(i, slot):
            return (
                pltpu.make_async_copy(act_hbm.at[i], act_at(slot, hidden), in_sems.at[slot, 0]),
                pltpu.make_async_copy(slope_hbm.at[i], slope_at(slot), in_sems.at[slot, 1]),
            )

        def unit_two_load(b):
            return pltpu.make_async_copy(unit_two_hbm.at[span_rows(b)], unit_buf.at[b % 4], unit_sems.at[b % 4])

        def x_load(b):
            return pltpu.make_async_copy(tokens.at[span_rows(b)], normed_two.at[span_rows(b)], x_load_sems.at[b])

        core_copy(1, piece).start()
        for b in range(spans):
            x_load(b).start()
            if b < 3:
                unit_two_load(b).start()
        live = live_rows()

        def out_store(b, slot):
            return pltpu.make_async_copy(out_buf.at[slot], block_out.at[span_rows(b)], out_sems.at[slot])

        def span(b, sums):
            slot = b % 2

            @pl.when(b + 3 < spans)
            def _():
                unit_two_load(b + 3).start()

            @pl.when(b >= 2)
            def _():
                out_store(b - 2, slot).wait()

            x_load(b).wait()
            unit_two_load(b).wait()
            rows = span_rows(b)
            put(units, rows, (normed_two[rows].astype(F32) - stats[rows, 32:33]) * stats[rows, 0:1])
            unit = unit_buf[b % 4].astype(F32)
            root = stats[rows, 64:65]
            grad = take(grad_two_acc, rows)
            weighted = grad * unit
            scaled = grad * vectors[2:3]
            inner = jnp.mean(weighted * vectors[2:3], axis=-1, keepdims=True)
            mixed = grad_rows[rows].astype(F32) + root * (
                scaled - jnp.mean(scaled, axis=-1, keepdims=True) - unit * inner
            )
            put(grad_two_acc, rows, mixed)
            out_buf[slot] = masked(take(result_acc, rows) + vectors[4:5], live).astype(BF16)
            out_store(b, slot).start()

            @pl.when(b == 8)
            def _():
                cross_start(1, piece)

            return sums[0] + row_sum(weighted), sums[1] + row_sum(grad)

        zero = jnp.zeros((8, width), F32)
        sums = lax.fori_loop(0, spans, span, (zero, zero))
        for b in (spans - 2, spans - 1):
            out_store(b, b % 2).wait()
        for n in range(2):
            for copy in loads(n, n):
                copy.start()
        for slot in range(4):
            normed_two[512 * slot + hidden : 512 * slot + 512] = ones_act
        for n in range(2):
            normed_two[2048 + 256 * n + 192 : 2048 + 256 * n + 256] = ones_low
            normed_two[2560 + 256 * n + 192 : 2560 + 256 * n + 256] = jnp.zeros((64, width), BF16)
        vector_sums[2:3] = jnp.sum(sums[0], axis=0, keepdims=True)
        vector_sums[3:4] = jnp.sum(sums[1], axis=0, keepdims=True)
        shards[CHUNKS - 2] = line_finish(0, piece)

        def pair(g, carry):
            base = 2 * (g % 2)

            @pl.when(g + 1 < images // 2)
            def _():
                for n in range(2):
                    for copy in loads(2 * g + 2 + n, 2 - base + n):
                        copy.start()

            for n in range(2):
                for copy in loads(2 * g + n, base + n):
                    copy.wait()

            @pl.when(g == 3)
            def _():
                line_start(1, piece)

            @pl.when(g == 6)
            def _():
                shards[CHUNKS - 1] = line_finish(1, piece)
                fill_stages()
                send_stages()

            for n in range(2):
                low = take(grad_two_acc, image_rows(2 * g + n))
                normed_two[2560 + 256 * n : 2560 + 256 * n + patches] = low.astype(BF16)
            unit = [take(units, image_rows(2 * g + n)) for n in range(2)]
            for n in range(2):
                normed_two[2048 + 256 * n : 2048 + 256 * n + patches] = (
                    unit[n] * vectors[0:1] + vectors[1:2]
                ).astype(BF16)
            lows = [normed_two[2560 + 256 * n : 2816 + 256 * n] for n in range(2)]
            grad_act = [dot(tok_out[...], lows[n]) for n in range(2)]
            for n in range(2):
                grad_rows[1536 + 384 * n : 1920 + 384 * n] = (
                    grad_act[n] * slope_at(base + n)[...].astype(F32)
                ).astype(BF16)
            tok_out_sum[...] += dot(act_at(base, 512)[...], lows[0], NT) + dot(act_at(base + 1, 512)[...], lows[1], NT)
            pres = [grad_rows[1536 + 384 * n : 1920 + 384 * n] for n in range(2)]
            grad = [dot(tok_in_t[...], pres[n])[0:patches] for n in range(2)]
            tok_in_sum[...] += dot(pres[0], normed_two[2048:2304], NT) + dot(pres[1], normed_two[2304:2560], NT)
            for n in range(2):
                put(result_acc, image_rows(2 * g + n), grad[n])
            gain = grad[0] * unit[0] + grad[1] * unit[1]
            vector_sums[0:1] += jnp.sum(gain, axis=0, keepdims=True)
            vector_sums[1:2] += jnp.sum(grad[0] + grad[1], axis=0, keepdims=True)
            return carry

        lax.fori_loop(0, images // 2, pair, 0)

        grads[0, :, :, 0:24] = tok_in_sum[...].reshape(4, 4, 24, 256)
        grads[1, :, :, 0:24] = tok_out_sum[0:hidden].reshape(4, 4, 24, 256)
        sums = vector_sums[...]
        hidden_rows = jnp.concatenate(
            [jnp.sum(hidden_sums[j], axis=0, keepdims=True) for j in range(CHUNKS)] + [jnp.zeros((2, 512), F32)], axis=0
        )
        for o in range(owners):
            moved = sums if o == 0 else pltpu.roll(sums, width - 48 * o, 1)
            grads[0, o // 4, o % 4, 24:32, 0:128] = moved[:, 0:128]
            grads[0, o // 4, o % 4, 24:32, 128:256] = jnp.zeros((8, 128), F32)
            grads[0, o // 4, o % 4, 31:32] = tok_out_sum[hidden : hidden + 1]
            moved = hidden_rows if o == 0 else pltpu.roll(hidden_rows, 512 - 32 * o, 1)
            grads[1, o // 4, o % 4, 24:32, 0:128] = moved[:, 0:128]
            grads[1, o // 4, o % 4, 24:32, 128:256] = jnp.zeros((8, 128), F32)
        core_copy(0, 32).start()

        def grad_store(b, slot):
            return pltpu.make_async_copy(out_buf.at[slot], input_grad.at[span_rows(b)], out_sems.at[slot])

        def last(b, carry):
            slot = b % 2

            @pl.when(b >= 2)
            def _():
                grad_store(b - 2, slot).wait()

            rows = span_rows(b)
            unit = take(units, rows)
            root = stats[rows, 0:1]
            scaled = take(result_acc, rows) * vectors[0:1]
            inner = jnp.mean(scaled * unit, axis=-1, keepdims=True)
            out_buf[slot] = (
                take(grad_two_acc, rows)
                + root * (scaled - jnp.mean(scaled, axis=-1, keepdims=True) - unit * inner)
            ).astype(BF16)
            grad_store(b, slot).start()

            @pl.when(b == 4)
            def _():
                cross_start(0, 32)

            @pl.when(b == spans - 1)
            def _():
                line_start(0, 32)

            return carry

        lax.fori_loop(0, spans, last, 0)
        for b in (spans - 2, spans - 1):
            grad_store(b, b % 2).wait()

    pl.run_scoped(
        token_backward,
        pltpu.VMEM((tiles, total_rows, LANES), F32),
        pltpu.VMEM((4, SPAN, width), BF16),
        pltpu.VMEM((2, SPAN, width), BF16),
        pltpu.SemaphoreType.DMA((spans,)),
        pltpu.SemaphoreType.DMA((4, 2)),
        pltpu.SemaphoreType.DMA((4,)),
        pltpu.SemaphoreType.DMA((2,)),
    )

    small_sum[...] = line_finish(0, 32)
    small_end = remote(small_sum, small_out.at[c], end_sems, (3,), partner)
    small_own = pltpu.make_async_copy(small_sum, small_out.at[c], end_sems.at[1, 4])
    small_end.start()
    small_own.start()
    small_end.wait()
    small_own.wait()

    @pl.when(c == 0)
    def _():
        remote(stage_in, ch_in_grad, end_sems, (0,), partner).wait_send()
        pltpu.make_async_copy(stage_in, ch_in_grad, end_sems.at[0, 4]).wait()
        for b in range(3):
            stage_out_copy(b).wait_recv()

    @pl.when(c == 1)
    def _():
        for b in range(3):
            stage_out_copy(b).wait_send()
            stage_out_own(b).wait()
        remote(stage_in, ch_in_grad, end_sems, (0,), partner).wait_recv()


def finish(small, ch_in_sum, ch_out_sum, *outs):
    gain_one, bias_one, tok_in, tok_in_bias, tok_out, tok_out_bias, gain_two, bias_two, ch_in, ch_in_bias, ch_out, ch_out_bias = outs
    per_tok, patches = tok_in.shape
    ch_in[...] = ch_in_sum[...]
    ch_out[...] = ch_out_sum[...]
    tok_in[...] = small[0, 0:per_tok, 0:patches]
    tok_out[...] = small[1, 0:per_tok, 0:patches]
    column = jnp.broadcast_to(small[0, 0:32, 200:201], (32, LANES))
    flipped = jnp.transpose(jnp.concatenate([column, jnp.zeros((LANES - 32, LANES), F32)], axis=0))
    tok_in_bias[...] = flipped[0:1, 0:per_tok]
    tok_out_bias[...] = small[0, 31:32, 0:patches]
    for r, out in enumerate((gain_one, bias_one, gain_two, bias_two, ch_out_bias)):
        out[...] = small[0, 24 + r : 25 + r, 0 : out.shape[1]]
    each = ch_in_bias.shape[1] // CHUNKS
    lane = lax.broadcasted_iota(jnp.int32, (1, 256), 1)
    total = jnp.zeros((1, 256), F32)
    for j in range(CHUNKS):
        part = small[1, 24 + j : 25 + j]
        part = part if j == 0 else pltpu.roll(part, each * j, 1)
        total = jnp.where((lane >= each * j) & (lane < each * (j + 1)), part, total)
    ch_in_bias[...] = total[:, 0 : ch_in_bias.shape[1]]


def per_device_fused(
    tokens, cotangent, counts, ln1_gain, ln1_bias, tok_in, tok_in_bias, tok_out, tok_out_bias,
    ln2_gain, ln2_bias, ch_in, ch_in_bias, ch_out, ch_out_bias,
):
    images, patches, width = tokens.shape
    per_in, inner = ch_in.shape
    per_out = ch_out.shape[0]
    per_tok = tok_in.shape[0]
    owners = width // per_in
    hidden = per_tok * owners
    each = per_out // CHUNKS
    chunk = each * owners
    rows = images * patches

    def by_patch(array):
        return array.transpose(1, 0, 2).reshape(rows, width)

    vector_row = jnp.zeros((width,), F32)
    offset = 0
    for vector in (ln1_gain, ln1_bias, ln2_gain, ln2_bias, ch_out_bias, tok_in_bias, ch_in_bias, tok_out_bias):
        length = vector.shape[0]
        vector_row = vector_row + jnp.pad(vector, (offset, width - offset - length)).astype(F32)
        offset += length
    vector_row = vector_row[None]
    any_spec = pl.BlockSpec(memory_space=pl.ANY)
    vmem_spec = pl.BlockSpec(memory_space=pltpu.VMEM)
    vmem = pltpu.VMEM
    dma = pltpu.SemaphoreType.DMA
    shape = jax.ShapeDtypeStruct
    tiled = (width // LANES, rows, LANES)
    results = pl.pallas_call(
        mega,
        in_specs=[pl.BlockSpec(memory_space=pltpu.SMEM), any_spec, any_spec] + [vmem_spec] * 5,
        out_specs=[any_spec] * 9,
        out_shape=[
            shape((rows, width), BF16),
            shape((rows, width), BF16),
            shape(ch_in.shape, F32),
            shape((CHUNKS, each, width), F32),
            shape((2, 32, 256), F32),
            shape((2, CHUNKS, 4, 4, 96, 256), BF16),
            shape((images, hidden, width), BF16),
            shape((images, hidden, width), BF16),
            shape((rows, width), BF16),
        ],
        scratch_shapes=[
            vmem((rows, width), BF16),
            vmem((rows, width), BF16),
            vmem(tiled, F32),
            vmem(tiled, F32),
            vmem((rows, LANES), F32),
            vmem((2, 4, 4, 96, 256), F32),
            vmem((2, 4, 4, 96, 256), F32),
            vmem((3, 4, 96, 256), BF16),
            vmem((4, 96, 256), F32),
            vmem((2, 3, 4, 96, 256), BF16),
            vmem((3, 96, 256), BF16),
            vmem((96, 256), F32),
            vmem((2, 3, 96, 256), BF16),
            vmem((CHUNKS, 96, 256), F32),
            vmem(ch_in.shape, F32),
            vmem((32, 256), F32),
            vmem((CHUNKS, 96, 256), BF16),
            vmem((2, 4, 4, 32, 256), BF16),
            vmem((hidden, 256), BF16),
            vmem((256, hidden), BF16),
            vmem((hidden, 256), BF16),
            vmem((256, hidden + 128), BF16),
            vmem((8, width), F32),
            vmem((CHUNKS, 1, chunk), F32),
            vmem((8, width), F32),
            vmem((CHUNKS, 8, chunk), F32),
            vmem((hidden, 256), F32),
            vmem((hidden + 128, 256), F32),
            dma((2, 7)),
            dma((2, CHUNKS, 3)),
            dma((CHUNKS,)),
            dma((2, CHUNKS, 3)),
            dma((2, CHUNKS)),
            dma((2, 2)),
            dma((2, 2, 3)),
            dma((2, 2, 3)),
            dma((2, 7)),
        ],
        compiler_params=pltpu.CompilerParams(
            collective_id=0, has_side_effects=True, vmem_limit_bytes=61 * 1024 * 1024
        ),
        cost_estimate=pl.CostEstimate(
            flops=12 * rows * width * inner, bytes_accessed=100_000_000, transcendentals=rows * inner
        ),
    )(counts, by_patch(tokens), by_patch(cotangent), vector_row, tok_in, tok_out, ch_in, ch_out)
    block_out, input_grad, in_sum, out_sum, small = results[:5]
    line = shape((1, per_in), F32)
    outs = pl.pallas_call(
        finish,
        in_specs=[vmem_spec] * 3,
        out_specs=[vmem_spec] * 12,
        out_shape=[
            line, line, shape(tok_in.shape, F32), shape((1, per_tok), F32), shape(tok_out.shape, F32),
            shape((1, patches), F32), line, line, shape(ch_in.shape, F32), shape((1, per_out), F32),
            shape(ch_out.shape, F32), line,
        ],
    )(small, in_sum, out_sum.reshape(ch_out.shape))

    def by_image(array):
        return array.reshape(patches, images, width).transpose(1, 0, 2)

    flat = (0, 1, 3, 5, 6, 7, 9, 11)
    outs = [out.reshape(-1) if n in flat else out for n, out in enumerate(outs)]
    return (by_image(block_out), by_image(input_grad), *outs)


def solution(mesh):
    fused = mesh.shape["dp"] == 2 and mesh.shape["fsdp"] == 16
    return jax.shard_map(
        per_device_fused if fused else per_device,
        mesh=mesh,
        in_specs=(
            P(("dp", "fsdp"), None, None),
            P(("dp", "fsdp"), None, None),
            P(("dp", "fsdp"), None),
            P("fsdp"),
            P("fsdp"),
            P("fsdp", None),
            P("fsdp"),
            P("fsdp", None),
            P(),
            P("fsdp"),
            P("fsdp"),
            P("fsdp", None),
            P("fsdp"),
            P("fsdp", None),
            P("fsdp"),
        ),
        out_specs=(
            P(("dp", "fsdp"), None, None),
            P(("dp", "fsdp"), None, None),
            P("fsdp"),
            P("fsdp"),
            P("fsdp", None),
            P("fsdp"),
            P("fsdp", None),
            P(),
            P("fsdp"),
            P("fsdp"),
            P("fsdp", None),
            P("fsdp"),
            P("fsdp", None),
            P("fsdp"),
        ),
        check_vma=False,
    )
```

```python
import jax
import jax.numpy as jnp
from jax import lax
from jax.experimental import pallas as pl
from jax.experimental.pallas import tpu as pltpu
from jax.sharding import PartitionSpec as P

EPSILON = 1e-06


def normalize(rows_in, gain, shift):
    centre = jnp.mean(rows_in, axis=-1, keepdims=True)
    centred = rows_in - centre
    spread = jnp.mean(centred * centred, axis=-1, keepdims=True)
    return centred * lax.rsqrt(spread + EPSILON) * gain + shift


def smooth(values):
    return jax.nn.gelu(values, approximate=True)


def forward(input_block, token_full, channel_full, output_shift):
    gain_one, shift_one, mixing_input_weight, mixing_input_bias, mixing_output_weight = token_full
    gain_two, shift_two, w_up, bias_up, w_down, bias_down = channel_full
    normalized_rows = normalize(
        input_block, gain_one.astype(jnp.float32), shift_one.astype(jnp.float32)
    )
    normalized_reduced = normalized_rows.astype(jnp.bfloat16)
    preactivation = (
        jnp.einsum(
            "qx,exj->eqj",
            mixing_input_weight,
            normalized_reduced,
            preferred_element_type=jnp.float32,
        )
        + mixing_input_bias.astype(jnp.float32)[None, :, None]
    )
    activation_reduced = smooth(preactivation).astype(jnp.bfloat16)
    branch_output = jnp.einsum(
        "hp,zhi->zpi", mixing_output_weight, activation_reduced, preferred_element_type=jnp.float32
    )
    mixing_rows = input_block + branch_output + output_shift.astype(jnp.float32)[None, :, None]
    normed_two = normalize(mixing_rows, gain_two.astype(jnp.float32), shift_two.astype(jnp.float32))
    normed_two_low = normed_two.astype(jnp.bfloat16)
    pre_two = jnp.einsum(
        "bsd,df->bsf", normed_two_low, w_up, preferred_element_type=jnp.float32
    ) + bias_up.astype(jnp.float32)
    act_two_low = smooth(pre_two).astype(jnp.bfloat16)
    result = (
        mixing_rows
        + jnp.einsum("bsf,fd->bsd", act_two_low, w_down, preferred_element_type=jnp.float32)
        + bias_down.astype(jnp.float32)
    )
    kept = (
        normalized_reduced,
        preactivation,
        activation_reduced,
        mixing_rows,
        normed_two_low,
        pre_two,
        act_two_low,
    )
    return (result, kept)


def backward(grad_out, input_block, kept, token_full, channel_full):
    (
        normalized_reduced,
        preactivation,
        activation_reduced,
        mixing_rows,
        normed_two_low,
        pre_two,
        act_two_low,
    ) = kept
    gain_one, shift_one, mixing_input_weight, mixing_input_bias, mixing_output_weight = token_full
    gain_two, shift_two, w_up, bias_up, w_down, bias_down = channel_full
    grad_out_low = grad_out.astype(jnp.bfloat16)
    grad_act_two = jnp.einsum(
        "bsd,fd->bsf", grad_out_low, w_down, preferred_element_type=jnp.float32
    )
    grad_w_down = jnp.einsum(
        "bsf,bsd->fd", act_two_low, grad_out_low, preferred_element_type=jnp.float32
    )
    grad_bias_down = jnp.sum(grad_out, axis=(0, 1))
    grad_pre_two = jax.vjp(smooth, pre_two)[1](grad_act_two)[0]
    grad_bias_up = jnp.sum(grad_pre_two, axis=(0, 1))
    grad_pre_two_low = grad_pre_two.astype(jnp.bfloat16)
    grad_normed_two = jnp.einsum(
        "bsf,df->bsd", grad_pre_two_low, w_up, preferred_element_type=jnp.float32
    )
    grad_w_up = jnp.einsum(
        "bsd,bsf->df", normed_two_low, grad_pre_two_low, preferred_element_type=jnp.float32
    )
    norm_two_back = jax.vjp(
        normalize, mixing_rows, gain_two.astype(jnp.float32), shift_two.astype(jnp.float32)
    )[1]
    grad_through, grad_gain_two, grad_shift_two = norm_two_back(grad_normed_two)
    grad_mixed = grad_out + grad_through
    grad_out_shift = jnp.sum(grad_mixed, axis=(0, 2))
    mixing_gradient_reduced = grad_mixed.astype(jnp.bfloat16)
    grad_act = jnp.einsum(
        "qx,exj->eqj",
        mixing_output_weight,
        mixing_gradient_reduced,
        preferred_element_type=jnp.float32,
    )
    grad_w_mix_out = jnp.einsum(
        "oaq,oeq->ae",
        activation_reduced,
        mixing_gradient_reduced,
        preferred_element_type=jnp.float32,
    )
    grad_pre = jax.vjp(smooth, preactivation)[1](grad_act)[0]
    grad_bias_mix_in = jnp.sum(grad_pre, axis=(0, 2))
    preactivation_gradient_reduced = grad_pre.astype(jnp.bfloat16)
    grad_normed = jnp.einsum(
        "hp,zhi->zpi",
        mixing_input_weight,
        preactivation_gradient_reduced,
        preferred_element_type=jnp.float32,
    )
    grad_w_mix_in = jnp.einsum(
        "oaq,oeq->ae",
        preactivation_gradient_reduced,
        normalized_reduced,
        preferred_element_type=jnp.float32,
    )
    norm_one_back = jax.vjp(
        normalize, input_block, gain_one.astype(jnp.float32), shift_one.astype(jnp.float32)
    )[1]
    grad_inner, grad_gain_one, grad_shift_one = norm_one_back(grad_normed)
    grad_x = grad_mixed + grad_inner
    grad_list = (
        grad_gain_one,
        grad_shift_one,
        grad_w_mix_in,
        grad_bias_mix_in,
        grad_w_mix_out,
        grad_gain_two,
        grad_shift_two,
        grad_w_up,
        grad_bias_up,
        grad_w_down,
        grad_bias_down,
    )
    return (grad_x, grad_list, grad_out_shift)


def per_device(
    tokens,
    cotangent,
    counts,
    ln1_gain,
    ln1_bias,
    tok_in,
    tok_in_bias,
    tok_out,
    tok_out_bias,
    ln2_gain,
    ln2_bias,
    ch_in,
    ch_in_bias,
    ch_out,
    ch_out_bias,
):
    micro_total = counts.shape[1]
    per_micro = tokens.shape[0] // micro_total
    outputs = []
    input_grads = []
    grad_sums = None
    shift_sum = jnp.zeros((tok_out_bias.shape[0],), jnp.float32)
    for micro in range(micro_total):
        lower = micro * per_micro
        input_block = tokens[lower : lower + per_micro].astype(jnp.float32)
        live_rows = (jnp.arange(per_micro) < counts[0, micro]).astype(jnp.float32)[:, None, None]
        grad_out = cotangent[lower : lower + per_micro].astype(jnp.float32) * live_rows
        token_full = (
            lax.all_gather(ln1_gain, "fsdp", axis=0, tiled=True),
            lax.all_gather(ln1_bias, "fsdp", axis=0, tiled=True),
            lax.all_gather(tok_in, "fsdp", axis=0, tiled=True),
            lax.all_gather(tok_in_bias, "fsdp", axis=0, tiled=True),
            lax.all_gather(tok_out, "fsdp", axis=0, tiled=True),
        )
        channel_full = (
            lax.all_gather(ln2_gain, "fsdp", axis=0, tiled=True),
            lax.all_gather(ln2_bias, "fsdp", axis=0, tiled=True),
            lax.all_gather(ch_in, "fsdp", axis=0, tiled=True),
            lax.all_gather(ch_in_bias, "fsdp", axis=0, tiled=True),
            lax.all_gather(ch_out, "fsdp", axis=0, tiled=True),
            lax.all_gather(ch_out_bias, "fsdp", axis=0, tiled=True),
        )
        result, kept = forward(input_block, token_full, channel_full, tok_out_bias)
        outputs.append((result * live_rows).astype(jnp.bfloat16))
        token_back = (
            lax.all_gather(ln1_gain, "fsdp", axis=0, tiled=True),
            lax.all_gather(ln1_bias, "fsdp", axis=0, tiled=True),
            lax.all_gather(tok_in, "fsdp", axis=0, tiled=True),
            lax.all_gather(tok_in_bias, "fsdp", axis=0, tiled=True),
            lax.all_gather(tok_out, "fsdp", axis=0, tiled=True),
        )
        channel_back = (
            lax.all_gather(ln2_gain, "fsdp", axis=0, tiled=True),
            lax.all_gather(ln2_bias, "fsdp", axis=0, tiled=True),
            lax.all_gather(ch_in, "fsdp", axis=0, tiled=True),
            lax.all_gather(ch_in_bias, "fsdp", axis=0, tiled=True),
            lax.all_gather(ch_out, "fsdp", axis=0, tiled=True),
            lax.all_gather(ch_out_bias, "fsdp", axis=0, tiled=True),
        )
        grad_x, grad_list, grad_out_shift = backward(
            grad_out, input_block, kept, token_back, channel_back
        )
        input_grads.append(grad_x.astype(jnp.bfloat16))
        shift_sum = shift_sum + grad_out_shift
        grad_sums = (
            grad_list
            if grad_sums is None
            else tuple(jax.tree.map(jnp.add, tuple(grad_sums), tuple(grad_list)))
        )
    grad_sums = (
        lax.psum_scatter(grad_sums[0], "fsdp", scatter_dimension=0, tiled=True),
        lax.psum_scatter(grad_sums[1], "fsdp", scatter_dimension=0, tiled=True),
        lax.psum_scatter(grad_sums[2], "fsdp", scatter_dimension=0, tiled=True),
        lax.psum_scatter(grad_sums[3], "fsdp", scatter_dimension=0, tiled=True),
        lax.psum_scatter(grad_sums[4], "fsdp", scatter_dimension=0, tiled=True),
        lax.psum_scatter(grad_sums[5], "fsdp", scatter_dimension=0, tiled=True),
        lax.psum_scatter(grad_sums[6], "fsdp", scatter_dimension=0, tiled=True),
        lax.psum_scatter(grad_sums[7], "fsdp", scatter_dimension=0, tiled=True),
        lax.psum_scatter(grad_sums[8], "fsdp", scatter_dimension=0, tiled=True),
        lax.psum_scatter(grad_sums[9], "fsdp", scatter_dimension=0, tiled=True),
        lax.psum_scatter(grad_sums[10], "fsdp", scatter_dimension=0, tiled=True),
    )
    shards = lax.psum(
        (
            grad_sums[0],
            grad_sums[1],
            grad_sums[2],
            grad_sums[3],
            grad_sums[4],
            grad_sums[5],
            grad_sums[6],
            grad_sums[7],
            grad_sums[8],
            grad_sums[9],
            grad_sums[10],
        ),
        "dp",
    )
    shift_total = lax.psum(shift_sum, ("dp", "fsdp"))
    block_out = jnp.concatenate(outputs, axis=0)
    input_grad = jnp.concatenate(input_grads, axis=0)
    return (
        block_out,
        input_grad,
        shards[0],
        shards[1],
        shards[2],
        shards[3],
        shards[4],
        shift_total,
        shards[5],
        shards[6],
        shards[7],
        shards[8],
        shards[9],
        shards[10],
    )


MESH = pl.DeviceIdType.MESH
NN = (((1,), (0,)), ((), ()))
NT = (((1,), (1,)), ((), ()))
TN = (((0,), (0,)), ((), ()))
F32 = jnp.float32
BF16 = jnp.bfloat16
CHUNKS = 6
BLOCK = 784
SPAN = 224
LANES = 128
C_A = 0.7978845608
C_B = 0.7978845608 * 0.044715


def dot(left, right, dims=NN):
    return lax.dot_general(left, right, dims, preferred_element_type=F32)


def gelu_and_slope(v):
    ratio = C_B * (v * v) + C_A
    t = jnp.tanh(v * ratio)
    h = 0.5 * t + 0.5
    act = v * h
    slope = h + act * (1.0 - t) * (3.0 * ratio - 2.0 * C_A)
    return act, slope


def row_stats(v):
    mean = jnp.mean(v, axis=-1, keepdims=True)
    centred = v - mean
    spread = jnp.mean(centred * centred, axis=-1, keepdims=True)
    root = lax.rsqrt(spread + EPSILON)
    return centred * root, root, mean


def take(buf, rows, count=6):
    return jnp.concatenate([buf.at[t][rows, :] for t in range(count)], axis=1)


def put(buf, rows, value):
    for t in range(value.shape[1] // LANES):
        buf.at[t][rows, :] = value[:, LANES * t : LANES * (t + 1)]


def mega(
    counts, tokens, cotangent, vector_row, tok_in_own, tok_out_own, ch_in_own, ch_out_own,
    block_out, input_grad, ch_in_grad, ch_out_grad, small_out, gathered, act_hbm, slope_hbm, unit_two_hbm,
    normed_two, grad_rows, result_acc, grad_two_acc, stats, w_in, w_out,
    grads, core_in, cross_out, cross_keep, cross_in, line_out, line_keep, line_in, shards, stage_in,
    small_sum, own_weights, small, tok_in, tok_in_t, tok_out, tok_out_t, vectors, hidden_bias,
    vector_sums, hidden_sums, tok_in_sum, tok_out_sum,
    small_sems, z_sems, z_local, x_sems, swap_sems, core_sems, cross_sems, line_sems, end_sems, load_sems, weight_sems,
):
    total_rows, width = tokens.shape
    images, hidden = act_hbm.shape[0], act_hbm.shape[1]
    patches = total_rows // images
    per_micro = images // counts.shape[1]
    owners = 16
    tiles = width // LANES
    c = lax.axis_index("dp")
    f = lax.axis_index("fsdp")
    zi, qi = f // 4, f % 4
    partner = (1 - c, f)

    def cross(k):
        return (c, zi * 4 + (qi ^ k))

    def line(k):
        return (c, (zi ^ k) * 4 + qi)

    def remote(src, dst, sems, index, device):
        return pltpu.make_async_remote_copy(
            src_ref=src, dst_ref=dst, send_sem=sems.at[(0,) + index], recv_sem=sems.at[(1,) + index],
            device_id=device, device_id_type=MESH,
        )

    def span_rows(b):
        return pl.ds(pl.multiple_of(b * SPAN, 16), SPAN)

    spans = total_rows // SPAN

    def row_loads(b):
        return (
            pltpu.make_async_copy(tokens.at[span_rows(b)], normed_two.at[span_rows(b)], load_sems.at[0, b]),
            pltpu.make_async_copy(cotangent.at[span_rows(b)], grad_rows.at[span_rows(b)], load_sems.at[1, b]),
        )

    for b in range(spans):
        for copy in row_loads(b):
            copy.start()
    barrier = pltpu.get_barrier_semaphore()
    for device in [partner] + [cross(k) for k in (1, 2, 3)] + [line(k) for k in (1, 2, 3)]:
        pl.semaphore_signal(barrier, inc=1, device_id=device, device_id_type=MESH)

    row = vector_row[...].astype(F32)

    def vector_at(offset, length, lanes=256):
        moved = row if offset == 0 else pltpu.roll(row, width - offset, 1)
        lane = lax.broadcasted_iota(jnp.int32, (1, lanes), 1)
        return jnp.where(lane < length, moved[:, 0:lanes], 0.0)

    lane = lax.broadcasted_iota(jnp.int32, (24, 256), 1)
    bias_column = jnp.transpose(jnp.broadcast_to(vector_at(240, 24, LANES), (LANES, LANES)))[0:24, 0:1]
    pad = jnp.zeros((24, 256 - patches), F32)
    padded = jnp.concatenate([tok_in_own[...].astype(F32), pad], axis=1)
    padded = jnp.where(lane == 200, jnp.broadcast_to(bias_column, (24, 256)), padded)
    rows_a = [vector_at(48 * r, 48) for r in range(5)] + [vector_at(264, 192), jnp.zeros((2, 256), F32)]
    packed_a = jnp.concatenate([padded] + rows_a, axis=0)
    padded = jnp.concatenate([tok_out_own[...].astype(F32), pad], axis=1)
    bias_rows = jnp.concatenate([vector_at(456, patches), jnp.zeros((7, 256), F32)], axis=0)
    packed_b = jnp.concatenate([padded, bias_rows], axis=0)
    small[c, zi, qi] = jnp.where(c == 0, packed_a, packed_b).astype(BF16)

    def small_line(k):
        return remote(small.at[c, zi, qi], small.at[c, zi, qi], small_sems, (k - 1,), line(k))

    def small_cross(k):
        return remote(small.at[c, :, qi], small.at[c, :, qi], small_sems, (k + 2,), cross(k))

    def small_swap():
        return remote(small.at[c], small.at[c], small_sems, (6,), partner)

    def z_copy(j, k):
        return remote(own_weights.at[j], gathered.at[c, j, zi, qi], z_sems, (j, k - 1), line(k))

    def z_own(j):
        return pltpu.make_async_copy(own_weights.at[j], gathered.at[c, j, zi, qi], z_local.at[j])

    def x_copy(j, k):
        return remote(gathered.at[c, j, :, qi], gathered.at[c, j, :, qi], x_sems, (j, k - 1), cross(k))

    def swap_copy(j):
        return remote(gathered.at[c, j], gathered.at[c, j], swap_sems, (j,), partner)

    def z_start(j):
        z_own(j).start()
        for k in (1, 2, 3):
            z_copy(j, k).start()

    def x_start(j):
        for k in (1, 2, 3):
            z_copy(j, k).wait()
        z_own(j).wait()
        for k in (1, 2, 3):
            x_copy(j, k).start()

    def swap_start(j):
        for k in (1, 2, 3):
            x_copy(j, k).wait()
        swap_copy(j).start()

    def core_copy(p, rows):
        return remote(
            grads.at[1 - c, :, :, pl.ds(0, rows)], core_in.at[p, :, :, pl.ds(0, rows)], core_sems, (p,), partner
        )

    def cross_copy(p, rows, k):
        return remote(
            cross_out.at[k - 1, :, pl.ds(0, rows)], cross_in.at[p, k - 1, :, pl.ds(0, rows)],
            cross_sems, (p, k - 1), cross(k),
        )

    def line_copy(p, rows, k):
        return remote(
            line_out.at[k - 1, pl.ds(0, rows)], line_in.at[p, k - 1, pl.ds(0, rows)], line_sems, (p, k - 1), line(k)
        )

    def cross_start(p, rows):
        core_copy(p, rows).wait()

        def per_line(z, carry):
            for k in range(4):
                q = qi ^ k
                total = grads[c, z, q, 0:rows] + core_in[p, z, q, 0:rows]
                if k == 0:
                    cross_keep[z, 0:rows] = total
                else:
                    cross_out[k - 1, z, 0:rows] = total.astype(BF16)
            return carry

        lax.fori_loop(0, 4, per_line, 0)
        for k in (1, 2, 3):
            cross_copy(p, rows, k).start()

    def line_start(p, rows):
        for k in (1, 2, 3):
            cross_copy(p, rows, k).wait()
        for k in range(4):
            z = zi ^ k
            total = cross_keep[z, 0:rows]
            for m in range(3):
                total = total + cross_in[p, m, z, 0:rows].astype(F32)
            if k == 0:
                line_keep[0:rows] = total
            else:
                line_out[k - 1, 0:rows] = total.astype(BF16)
        for k in (1, 2, 3):
            line_copy(p, rows, k).start()

    def line_finish(p, rows):
        for k in (1, 2, 3):
            line_copy(p, rows, k).wait()
        total = line_keep[0:rows]
        for m in range(3):
            total = total + line_in[p, m, 0:rows].astype(F32)
        return total

    piece = grads.shape[3]

    def live_rows():
        image = lax.broadcasted_iota(jnp.int32, (images, 1), 0)
        live = jnp.zeros((images, 1), F32)
        for micro in range(counts.shape[1]):
            inside = (image >= micro * per_micro) & (image < micro * per_micro + counts[0, micro])
            live = jnp.where(inside, 1.0, live)
        return jnp.broadcast_to(live, (images, width))

    def masked(value, live):
        return (value.reshape(SPAN // images, images, width) * live[None]).reshape(SPAN, width)

    def row_sum(value):
        return jnp.sum(value.reshape(4, SPAN // 32, 8, width).sum(1), axis=0)

    stat_lane = lax.broadcasted_iota(jnp.int32, (SPAN, LANES), 1)

    def image_rows(i):
        return pl.ds(i, patches, stride=images)

    def own_rows():
        @pl.when(c == 0)
        def _():
            group = lax.broadcasted_iota(jnp.int32, (48, LANES), 1) >> 5
            for j in range(CHUNKS):
                for b in range(2):
                    for t in range(2):
                        tile = None
                        for g in range(4):
                            source = 192 * (8 * b + 4 * t + g) + 32 * j
                            part = ch_in_own[:, source // LANES * LANES : (source // LANES + 1) * LANES].astype(F32)
                            shift = (32 * g - source) % LANES
                            part = part if shift == 0 else pltpu.roll(part, shift, 1)
                            tile = part if tile is None else jnp.where(group == g, part, tile)
                        own_weights[j, 48 * b : 48 * b + 48, LANES * t : LANES * (t + 1)] = tile.astype(BF16)

        @pl.when(c == 1)
        def _():
            for j in range(CHUNKS):
                for b in range(3):
                    own_weights[j, 32 * b : 32 * b + 32] = ch_out_own[32 * j : 32 * j + 32, 256 * b : 256 * b + 256]

    def norm_one():
        pl.semaphore_wait(barrier, 7)
        for k in (1, 2, 3):
            small_line(k).start()
        own_rows()
        z_start(0)
        live = live_rows()

        def span(b, carry):
            for copy in row_loads(b):
                copy.wait()
            rows = span_rows(b)
            unit, root, mean = row_stats(normed_two[rows].astype(F32))
            put(grad_two_acc, rows, unit)
            stats[rows] = jnp.where(stat_lane < 32, root, mean)
            grad = masked(grad_rows[rows].astype(F32), live)
            grad_rows[rows] = grad.astype(BF16)

            @pl.when(b == 4)
            def _():
                for k in (1, 2, 3):
                    small_line(k).wait()
                for k in (1, 2, 3):
                    small_cross(k).start()
                z_start(1)

            @pl.when(b == 10)
            def _():
                for k in (1, 2, 3):
                    small_cross(k).wait()
                small_swap().start()

            return carry + row_sum(grad)

        sums = lax.fori_loop(0, spans, span, jnp.zeros((8, width), F32))
        vector_sums[...] = jnp.zeros(vector_sums.shape, F32)
        vector_sums[4:5] = jnp.sum(sums, axis=0, keepdims=True)
    norm_one()
    hidden_sums[...] = jnp.zeros(hidden_sums.shape, F32)
    tok_in_sum[...] = jnp.zeros(tok_in_sum.shape, F32)
    tok_out_sum[...] = jnp.zeros(tok_out_sum.shape, F32)
    small_swap().wait()

    part_a = small[0].astype(F32).reshape(owners, 32, 256)
    part_b = small[1].astype(F32).reshape(owners, 32, 256)
    full_in = part_a[:, 0:24].reshape(hidden, 256)
    full_out = part_b[:, 0:24].reshape(hidden, 256)
    tok_in[...] = full_in.astype(BF16)
    tok_in_t[...] = jnp.transpose(full_in).astype(BF16)
    tok_out[...] = full_out.astype(BF16)
    out_rows = jnp.concatenate([full_out, bias_rows, jnp.zeros((120, 256), F32)], axis=0)
    tok_out_t[...] = jnp.transpose(out_rows).astype(BF16)

    flat_a = part_a.reshape(owners * 32, 256).astype(BF16)
    pick_r = lax.broadcasted_iota(jnp.int32, (8, owners * 32), 0)
    pick_p = lax.broadcasted_iota(jnp.int32, (8, owners * 32), 1)
    pick = jnp.where((pick_p & 31) == 24 + pick_r, 1.0, 0.0).astype(BF16)
    col = lax.broadcasted_iota(jnp.int32, (256, width), 1)
    lane = lax.broadcasted_iota(jnp.int32, (256, width), 0)
    spread = jnp.where(lane == col - 48 * ((col * 43691) >> 21), 1.0, 0.0).astype(BF16)
    own_n = (lax.broadcasted_iota(jnp.int32, (owners * 32, width), 1) * 43691) >> 21
    own_p = lax.broadcasted_iota(jnp.int32, (owners * 32, width), 0) >> 5
    vectors[...] = dot(pick, jnp.where(own_n == own_p, dot(flat_a, spread), 0.0).astype(BF16))
    span_n = owners * 32
    own_n = lax.broadcasted_iota(jnp.int32, (span_n, span_n), 1) >> 5
    own_p = lax.broadcasted_iota(jnp.int32, (span_n, span_n), 0) >> 5
    col = lax.broadcasted_iota(jnp.int32, (256, span_n), 1)
    lane = lax.broadcasted_iota(jnp.int32, (256, span_n), 0)
    for j in range(CHUNKS):
        spread = jnp.where(lane == 32 * j + (col & 31), 1.0, 0.0).astype(BF16)
        rows = dot(pick, jnp.where(own_n == own_p, dot(flat_a, spread), 0.0).astype(BF16))
        hidden_bias[j] = rows[5:6]

    def weight_loads(j, p):
        return [
            pltpu.make_async_copy(
                gathered.at[0, j, :, :, pl.ds(48 * b, 48)], w_in.at[p, :, :, :, pl.ds(256 * b, 256)], weight_sems.at[b]
            )
            for b in range(2)
        ] + [
            pltpu.make_async_copy(
                gathered.at[1, j, :, :, pl.ds(32 * b, 32)], w_out.at[p, :, :, :, pl.ds(256 * b, 256)],
                weight_sems.at[2 + b],
            )
            for b in range(3)
        ]

    ones_low = jnp.where(lax.broadcasted_iota(jnp.int32, (64, width), 0) == 8, 1.0, 0.0).astype(BF16)
    ones_act = jnp.where(lax.broadcasted_iota(jnp.int32, (128, width), 0) == 0, 1.0, 0.0).astype(BF16)

    def token_forward(act_buf, slope_buf, normed, unit_buf, out_sems, unit_sems):
        def stores(i, slot):
            return (
                pltpu.make_async_copy(act_buf.at[slot, pl.ds(0, hidden)], act_hbm.at[i], out_sems.at[slot, 0]),
                pltpu.make_async_copy(slope_buf.at[slot], slope_hbm.at[i], out_sems.at[slot, 1]),
            )

        for slot in range(4):
            act_buf[slot, hidden : hidden + 128] = ones_act
        for n in range(2):
            normed[n, 192:256] = ones_low

        def pair(g, base):
            @pl.when(g >= 2)
            def _():
                for n in range(2):
                    for copy in stores(2 * g - 4 + n, base + n):
                        copy.wait()

            @pl.when(g == 0)
            def _():
                x_start(0)
                z_start(2)

            @pl.when(g == 4)
            def _():
                x_start(1)
                z_start(3)

            for n in range(2):
                unit = take(grad_two_acc, image_rows(2 * g + n))
                normed[n, 0:patches] = (unit * vectors[0:1] + vectors[1:2]).astype(BF16)
            pre = [dot(tok_in[...], normed[n]) for n in range(2)]
            for n in range(2):
                act, slope = gelu_and_slope(pre[n])
                act_buf[base + n, 0:hidden] = act.astype(BF16)
                slope_buf[base + n] = slope.astype(BF16)
            mixed = [dot(tok_out_t[...], act_buf[base + n]) for n in range(2)]
            for n in range(2):
                put(result_acc, image_rows(2 * g + n), mixed[n][0:patches])
                for copy in stores(2 * g + n, base + n):
                    copy.start()

        def pairs(h, carry):
            for half in range(2):
                pair(2 * h + half, 2 * half)
            return carry

        lax.fori_loop(0, images // 4, pairs, 0)
        for i in range(images - 4, images):
            for copy in stores(i, i % 4):
                copy.wait()
        swap_start(0)
        x_start(2)
        z_start(4)

        def unit_two_store(b):
            return pltpu.make_async_copy(unit_buf.at[b % 4], unit_two_hbm.at[span_rows(b)], unit_sems.at[b % 4])

        def span(b, carry):
            rows = span_rows(b)

            @pl.when(b >= 4)
            def _():
                unit_two_store(b - 4).wait()

            mixed = normed_two[rows].astype(F32) + take(result_acc, rows)
            put(result_acc, rows, mixed)
            unit, root, _ = row_stats(mixed)
            stats[rows] = jnp.where(stat_lane < 64, stats[rows], root)
            unit_buf[b % 4] = unit.astype(BF16)
            unit_two_store(b).start()
            normed_two[rows] = (unit * vectors[2:3] + vectors[3:4]).astype(BF16)
            put(grad_two_acc, rows, jnp.zeros((SPAN, width), F32))

            @pl.when(b == 10)
            def _():
                swap_copy(0).wait()
                for copy in weight_loads(0, 0):
                    copy.start()
                swap_start(1)
                x_start(3)
                z_start(5)

            return carry

        lax.fori_loop(0, spans, span, 0)
        for b in range(spans - 4, spans):
            unit_two_store(b).wait()

    pl.run_scoped(
        token_forward,
        pltpu.VMEM((4, hidden + 128, width), BF16),
        pltpu.VMEM((4, hidden, width), BF16),
        pltpu.VMEM((2, 256, width), BF16),
        pltpu.VMEM((4, SPAN, width), BF16),
        pltpu.SemaphoreType.DMA((4, 2)),
        pltpu.SemaphoreType.DMA((4,)),
    )

    def channel(act_all, slope_all):
        chunk = w_in.shape[-1]

        for copy in weight_loads(0, 0):
            copy.wait()

        def tick(j, carry):
            p = j % 2

            @pl.when(j >= 1)
            def _():
                core_copy(1 - p, piece).start()

            def block(b, inner):
                rows = pl.ds(pl.multiple_of(b * BLOCK, 16), BLOCK)
                up = w_in[p].reshape(width, chunk)
                down = w_out[p].reshape(chunk, width)
                pre = dot(normed_two[rows], up) + hidden_bias[j]
                grad_act = dot(grad_rows[rows], down, NT)
                act, slope = gelu_and_slope(pre)
                grad_pre = grad_act * slope
                hidden_sums[j] += jnp.sum(grad_pre.reshape(BLOCK // 112, 14, 8, chunk).sum(1), axis=0)
                act_all[rows] = act.astype(BF16)
                slope_all[rows] = grad_pre.astype(BF16)
                forward_part = dot(act_all[rows], down)
                for t in range(tiles):
                    result_acc[t, rows] += forward_part[:, LANES * t : LANES * (t + 1)]
                backward_part = dot(slope_all[rows], up, NT)
                for t in range(tiles):
                    grad_two_acc[t, rows] += backward_part[:, LANES * t : LANES * (t + 1)]

                @pl.when((b == 0) & (j >= 2))
                def _():
                    line_start(p, piece)

                @pl.when((b == 1) & (j >= 1))
                def _():
                    cross_start(1 - p, piece)

                @pl.when((b == 0) & (j == 0))
                def _():
                    x_start(4)
                    swap_start(2)

                @pl.when((b == 2) & (j == 0))
                def _():
                    x_start(5)

                @pl.when((b == 2) & (j >= 2))
                def _():
                    shards[j - 2] = line_finish(p, piece)

                @pl.when((b == 2) & (j + 1 < CHUNKS))
                def _():
                    swap_copy(j + 1).wait()
                    for copy in weight_loads(j + 1, 1 - p):
                        copy.start()

                @pl.when((b == 3) & (j + 3 < CHUNKS))
                def _():
                    swap_start(j + 3)

                return inner

            lax.fori_loop(0, total_rows // BLOCK, block, 0)
            up_grad = dot(normed_two[...], slope_all[...], TN)
            for b in range(2):
                grads[0, :, :, 48 * b : 48 * b + 48] = up_grad[:, 256 * b : 256 * b + 256].reshape(4, 4, 48, 256)
            down_grad = dot(act_all[...], grad_rows[...], TN)
            for b in range(3):
                grads[1, :, :, 32 * b : 32 * b + 32] = down_grad[:, 256 * b : 256 * b + 256].reshape(4, 4, 32, 256)

            @pl.when(j + 1 < CHUNKS)
            def _():
                for copy in weight_loads(j + 1, 1 - p):
                    copy.wait()

            return carry

        lax.fori_loop(0, CHUNKS, tick, 0)

    pl.run_scoped(
        channel,
        pltpu.VMEM((total_rows, 512), BF16),
        pltpu.VMEM((total_rows, 512), BF16),
    )

    def stage_out_copy(b):
        return remote(
            shards.at[:, pl.ds(32 * b, 32)], ch_out_grad.at[:, :, pl.ds(256 * b, 256)], end_sems, (b,), partner
        )

    def stage_out_own(b):
        return pltpu.make_async_copy(
            shards.at[:, pl.ds(32 * b, 32)], ch_out_grad.at[:, :, pl.ds(256 * b, 256)], end_sems.at[0, 4 + b]
        )

    def send_stages():
        @pl.when(c == 0)
        def _():
            remote(stage_in, ch_in_grad, end_sems, (0,), partner).start()
            pltpu.make_async_copy(stage_in, ch_in_grad, end_sems.at[0, 4]).start()

        @pl.when(c == 1)
        def _():
            for b in range(3):
                stage_out_copy(b).start()
                stage_out_own(b).start()

    def fill_stages():
        @pl.when(c == 0)
        def _():
            group = lax.broadcasted_iota(jnp.int32, (48, LANES), 1) >> 5
            for t in range(24):
                tile = None
                for g in range(4):
                    unit = LANES * t + 32 * g
                    o, j = unit // 192, unit % 192 // 32
                    b, source = o // 8, 32 * (o % 8)
                    part = shards[j, 48 * b : 48 * b + 48, source // LANES * LANES : (source // LANES + 1) * LANES]
                    shift = (32 * g - source) % LANES
                    part = part if shift == 0 else pltpu.roll(part, shift, 1)
                    tile = part if tile is None else jnp.where(group == g, part, tile)
                stage_in[:, LANES * t : LANES * (t + 1)] = tile

    def token_backward(units, unit_buf, out_buf, x_load_sems, in_sems, unit_sems, out_sems):
        def act_at(slot, count):
            return normed_two.at[pl.ds(512 * slot, count)]

        def slope_at(slot):
            return grad_rows.at[pl.ds(384 * slot, hidden)]

        def loads(i, slot):
            return (
                pltpu.make_async_copy(act_hbm.at[i], act_at(slot, hidden), in_sems.at[slot, 0]),
                pltpu.make_async_copy(slope_hbm.at[i], slope_at(slot), in_sems.at[slot, 1]),
            )

        def unit_two_load(b):
            return pltpu.make_async_copy(unit_two_hbm.at[span_rows(b)], unit_buf.at[b % 4], unit_sems.at[b % 4])

        def x_load(b):
            return pltpu.make_async_copy(tokens.at[span_rows(b)], normed_two.at[span_rows(b)], x_load_sems.at[b])

        core_copy(1, piece).start()
        for b in range(spans):
            x_load(b).start()
            if b < 3:
                unit_two_load(b).start()
        live = live_rows()

        def out_store(b, slot):
            return pltpu.make_async_copy(out_buf.at[slot], block_out.at[span_rows(b)], out_sems.at[slot])

        def span(b, sums):
            slot = b % 2

            @pl.when(b + 3 < spans)
            def _():
                unit_two_load(b + 3).start()

            @pl.when(b >= 2)
            def _():
                out_store(b - 2, slot).wait()

            x_load(b).wait()
            unit_two_load(b).wait()
            rows = span_rows(b)
            put(units, rows, (normed_two[rows].astype(F32) - stats[rows, 32:33]) * stats[rows, 0:1])
            unit = unit_buf[b % 4].astype(F32)
            root = stats[rows, 64:65]
            grad = take(grad_two_acc, rows)
            weighted = grad * unit
            scaled = grad * vectors[2:3]
            inner = jnp.mean(weighted * vectors[2:3], axis=-1, keepdims=True)
            mixed = grad_rows[rows].astype(F32) + root * (
                scaled - jnp.mean(scaled, axis=-1, keepdims=True) - unit * inner
            )
            put(grad_two_acc, rows, mixed)
            out_buf[slot] = masked(take(result_acc, rows) + vectors[4:5], live).astype(BF16)
            out_store(b, slot).start()

            @pl.when(b == 2)
            def _():
                line_start(0, piece)

            @pl.when(b == 7)
            def _():
                cross_start(1, piece)

            return sums[0] + row_sum(weighted), sums[1] + row_sum(grad)

        zero = jnp.zeros((8, width), F32)
        sums = lax.fori_loop(0, spans, span, (zero, zero))
        for b in (spans - 2, spans - 1):
            out_store(b, b % 2).wait()
        for n in range(2):
            for copy in loads(n, n):
                copy.start()
        for slot in range(4):
            normed_two[512 * slot + hidden : 512 * slot + 512] = ones_act
        for n in range(2):
            normed_two[2048 + 256 * n + 192 : 2048 + 256 * n + 256] = ones_low
            normed_two[2560 + 256 * n + 192 : 2560 + 256 * n + 256] = jnp.zeros((64, width), BF16)
        vector_sums[2:3] = jnp.sum(sums[0], axis=0, keepdims=True)
        vector_sums[3:4] = jnp.sum(sums[1], axis=0, keepdims=True)
        shards[CHUNKS - 2] = line_finish(0, piece)

        def pair(g, base):
            @pl.when(g + 1 < images // 2)
            def _():
                for n in range(2):
                    for copy in loads(2 * g + 2 + n, 2 - base + n):
                        copy.start()

            for n in range(2):
                for copy in loads(2 * g + n, base + n):
                    copy.wait()

            @pl.when(g == 3)
            def _():
                line_start(1, piece)

            @pl.when(g == 6)
            def _():
                shards[CHUNKS - 1] = line_finish(1, piece)
                fill_stages()
                send_stages()

            for n in range(2):
                low = take(grad_two_acc, image_rows(2 * g + n))
                normed_two[2560 + 256 * n : 2560 + 256 * n + patches] = low.astype(BF16)
            unit = [take(units, image_rows(2 * g + n)) for n in range(2)]
            for n in range(2):
                normed_two[2048 + 256 * n : 2048 + 256 * n + patches] = (
                    unit[n] * vectors[0:1] + vectors[1:2]
                ).astype(BF16)
            lows = [normed_two[2560 + 256 * n : 2816 + 256 * n] for n in range(2)]
            grad_act = [dot(tok_out[...], lows[n]) for n in range(2)]
            for n in range(2):
                grad_rows[1536 + 384 * n : 1920 + 384 * n] = (
                    grad_act[n] * slope_at(base + n)[...].astype(F32)
                ).astype(BF16)
            tok_out_sum[...] += dot(act_at(base, 512)[...], lows[0], NT) + dot(act_at(base + 1, 512)[...], lows[1], NT)
            pres = [grad_rows[1536 + 384 * n : 1920 + 384 * n] for n in range(2)]
            grad = [dot(tok_in_t[...], pres[n])[0:patches] for n in range(2)]
            tok_in_sum[...] += dot(pres[0], normed_two[2048:2304], NT) + dot(pres[1], normed_two[2304:2560], NT)
            for n in range(2):
                put(result_acc, image_rows(2 * g + n), grad[n])
            gain = grad[0] * unit[0] + grad[1] * unit[1]
            vector_sums[0:1] += jnp.sum(gain, axis=0, keepdims=True)
            vector_sums[1:2] += jnp.sum(grad[0] + grad[1], axis=0, keepdims=True)

        def pairs(h, carry):
            for half in range(2):
                pair(2 * h + half, 2 * half)
            return carry

        lax.fori_loop(0, images // 4, pairs, 0)

        grads[0, :, :, 0:24] = tok_in_sum[...].reshape(4, 4, 24, 256)
        grads[1, :, :, 0:24] = tok_out_sum[0:hidden].reshape(4, 4, 24, 256)
        sums = vector_sums[...]
        hidden_rows = jnp.concatenate(
            [jnp.sum(hidden_sums[j], axis=0, keepdims=True) for j in range(CHUNKS)] + [jnp.zeros((2, 512), F32)], axis=0
        )
        for o in range(owners):
            moved = sums if o == 0 else pltpu.roll(sums, width - 48 * o, 1)
            grads[0, o // 4, o % 4, 24:32, 0:128] = moved[:, 0:128]
            grads[0, o // 4, o % 4, 24:32, 128:256] = jnp.zeros((8, 128), F32)
            grads[0, o // 4, o % 4, 31:32] = tok_out_sum[hidden : hidden + 1]
            moved = hidden_rows if o == 0 else pltpu.roll(hidden_rows, 512 - 32 * o, 1)
            grads[1, o // 4, o % 4, 24:32, 0:128] = moved[:, 0:128]
            grads[1, o // 4, o % 4, 24:32, 128:256] = jnp.zeros((8, 128), F32)
        core_copy(0, 32).start()

        def grad_store(b, slot):
            return pltpu.make_async_copy(out_buf.at[slot], input_grad.at[span_rows(b)], out_sems.at[slot])

        def last(b, carry):
            slot = b % 2

            @pl.when(b >= 2)
            def _():
                grad_store(b - 2, slot).wait()

            rows = span_rows(b)
            unit = take(units, rows)
            root = stats[rows, 0:1]
            scaled = take(result_acc, rows) * vectors[0:1]
            inner = jnp.mean(scaled * unit, axis=-1, keepdims=True)
            out_buf[slot] = (
                take(grad_two_acc, rows)
                + root * (scaled - jnp.mean(scaled, axis=-1, keepdims=True) - unit * inner)
            ).astype(BF16)
            grad_store(b, slot).start()

            @pl.when(b == 4)
            def _():
                cross_start(0, 32)

            @pl.when(b == spans - 1)
            def _():
                line_start(0, 32)

            return carry

        lax.fori_loop(0, spans, last, 0)
        for b in (spans - 2, spans - 1):
            grad_store(b, b % 2).wait()

    pl.run_scoped(
        token_backward,
        pltpu.VMEM((tiles, total_rows, LANES), F32),
        pltpu.VMEM((4, SPAN, width), BF16),
        pltpu.VMEM((2, SPAN, width), BF16),
        pltpu.SemaphoreType.DMA((spans,)),
        pltpu.SemaphoreType.DMA((4, 2)),
        pltpu.SemaphoreType.DMA((4,)),
        pltpu.SemaphoreType.DMA((2,)),
    )

    small_sum[...] = line_finish(0, 32)
    small_end = remote(small_sum, small_out.at[c], end_sems, (3,), partner)
    small_own = pltpu.make_async_copy(small_sum, small_out.at[c], end_sems.at[1, 4])
    small_end.start()
    small_own.start()
    small_end.wait()
    small_own.wait()

    @pl.when(c == 0)
    def _():
        remote(stage_in, ch_in_grad, end_sems, (0,), partner).wait_send()
        pltpu.make_async_copy(stage_in, ch_in_grad, end_sems.at[0, 4]).wait()
        for b in range(3):
            stage_out_copy(b).wait_recv()

    @pl.when(c == 1)
    def _():
        for b in range(3):
            stage_out_copy(b).wait_send()
            stage_out_own(b).wait()
        remote(stage_in, ch_in_grad, end_sems, (0,), partner).wait_recv()


def finish(small, ch_in_sum, ch_out_sum, *outs):
    gain_one, bias_one, tok_in, tok_in_bias, tok_out, tok_out_bias, gain_two, bias_two, ch_in, ch_in_bias, ch_out, ch_out_bias = outs
    per_tok, patches = tok_in.shape
    ch_in[...] = ch_in_sum[...]
    ch_out[...] = ch_out_sum[...]
    tok_in[...] = small[0, 0:per_tok, 0:patches]
    tok_out[...] = small[1, 0:per_tok, 0:patches]
    column = jnp.broadcast_to(small[0, 0:32, 200:201], (32, LANES))
    flipped = jnp.transpose(jnp.concatenate([column, jnp.zeros((LANES - 32, LANES), F32)], axis=0))
    tok_in_bias[...] = flipped[0:1, 0:per_tok]
    tok_out_bias[...] = small[0, 31:32, 0:patches]
    for r, out in enumerate((gain_one, bias_one, gain_two, bias_two, ch_out_bias)):
        out[...] = small[0, 24 + r : 25 + r, 0 : out.shape[1]]
    each = ch_in_bias.shape[1] // CHUNKS
    lane = lax.broadcasted_iota(jnp.int32, (1, 256), 1)
    total = jnp.zeros((1, 256), F32)
    for j in range(CHUNKS):
        part = small[1, 24 + j : 25 + j]
        part = part if j == 0 else pltpu.roll(part, each * j, 1)
        total = jnp.where((lane >= each * j) & (lane < each * (j + 1)), part, total)
    ch_in_bias[...] = total[:, 0 : ch_in_bias.shape[1]]


def per_device_fused(
    tokens, cotangent, counts, ln1_gain, ln1_bias, tok_in, tok_in_bias, tok_out, tok_out_bias,
    ln2_gain, ln2_bias, ch_in, ch_in_bias, ch_out, ch_out_bias,
):
    images, patches, width = tokens.shape
    per_in, inner = ch_in.shape
    per_out = ch_out.shape[0]
    per_tok = tok_in.shape[0]
    owners = width // per_in
    hidden = per_tok * owners
    each = per_out // CHUNKS
    chunk = each * owners
    rows = images * patches

    def by_patch(array):
        return array.transpose(1, 0, 2).reshape(rows, width)

    vector_row = jnp.zeros((width,), F32)
    offset = 0
    for vector in (ln1_gain, ln1_bias, ln2_gain, ln2_bias, ch_out_bias, tok_in_bias, ch_in_bias, tok_out_bias):
        length = vector.shape[0]
        vector_row = vector_row + jnp.pad(vector, (offset, width - offset - length)).astype(F32)
        offset += length
    vector_row = vector_row[None]
    any_spec = pl.BlockSpec(memory_space=pl.ANY)
    vmem_spec = pl.BlockSpec(memory_space=pltpu.VMEM)
    vmem = pltpu.VMEM
    dma = pltpu.SemaphoreType.DMA
    shape = jax.ShapeDtypeStruct
    tiled = (width // LANES, rows, LANES)
    results = pl.pallas_call(
        mega,
        in_specs=[pl.BlockSpec(memory_space=pltpu.SMEM), any_spec, any_spec] + [vmem_spec] * 5,
        out_specs=[any_spec] * 9,
        out_shape=[
            shape((rows, width), BF16),
            shape((rows, width), BF16),
            shape(ch_in.shape, F32),
            shape((CHUNKS, each, width), F32),
            shape((2, 32, 256), F32),
            shape((2, CHUNKS, 4, 4, 96, 256), BF16),
            shape((images, hidden, width), BF16),
            shape((images, hidden, width), BF16),
            shape((rows, width), BF16),
        ],
        scratch_shapes=[
            vmem((rows, width), BF16),
            vmem((rows, width), BF16),
            vmem(tiled, F32),
            vmem(tiled, F32),
            vmem((rows, LANES), F32),
            vmem((2, 4, 4, per_in, chunk), BF16),
            vmem((2, 4, 4, each, width), BF16),
            vmem((2, 4, 4, 96, 256), F32),
            vmem((2, 4, 4, 96, 256), F32),
            vmem((3, 4, 96, 256), BF16),
            vmem((4, 96, 256), F32),
            vmem((2, 3, 4, 96, 256), BF16),
            vmem((3, 96, 256), BF16),
            vmem((96, 256), F32),
            vmem((2, 3, 96, 256), BF16),
            vmem((CHUNKS, 96, 256), F32),
            vmem(ch_in.shape, F32),
            vmem((32, 256), F32),
            vmem((CHUNKS, 96, 256), BF16),
            vmem((2, 4, 4, 32, 256), BF16),
            vmem((hidden, 256), BF16),
            vmem((256, hidden), BF16),
            vmem((hidden, 256), BF16),
            vmem((256, hidden + 128), BF16),
            vmem((8, width), F32),
            vmem((CHUNKS, 1, chunk), F32),
            vmem((8, width), F32),
            vmem((CHUNKS, 8, chunk), F32),
            vmem((hidden, 256), F32),
            vmem((hidden + 128, 256), F32),
            dma((2, 7)),
            dma((2, CHUNKS, 3)),
            dma((CHUNKS,)),
            dma((2, CHUNKS, 3)),
            dma((2, CHUNKS)),
            dma((2, 2)),
            dma((2, 2, 3)),
            dma((2, 2, 3)),
            dma((2, 7)),
            dma((2, 14)),
            dma((5,)),
        ],
        compiler_params=pltpu.CompilerParams(
            collective_id=0, has_side_effects=True, vmem_limit_bytes=61 * 1024 * 1024
        ),
        cost_estimate=pl.CostEstimate(
            flops=12 * rows * width * inner, bytes_accessed=100_000_000, transcendentals=rows * inner
        ),
    )(counts, by_patch(tokens), by_patch(cotangent), vector_row, tok_in, tok_out, ch_in, ch_out)
    block_out, input_grad, in_sum, out_sum, small = results[:5]
    line = shape((1, per_in), F32)
    outs = pl.pallas_call(
        finish,
        in_specs=[vmem_spec] * 3,
        out_specs=[vmem_spec] * 12,
        out_shape=[
            line, line, shape(tok_in.shape, F32), shape((1, per_tok), F32), shape(tok_out.shape, F32),
            shape((1, patches), F32), line, line, shape(ch_in.shape, F32), shape((1, per_out), F32),
            shape(ch_out.shape, F32), line,
        ],
    )(small, in_sum, out_sum.reshape(ch_out.shape))

    def by_image(array):
        return array.reshape(patches, images, width).transpose(1, 0, 2)

    flat = (0, 1, 3, 5, 6, 7, 9, 11)
    outs = [out.reshape(-1) if n in flat else out for n, out in enumerate(outs)]
    return (by_image(block_out), by_image(input_grad), *outs)


def solution(mesh):
    fused = mesh.shape["dp"] == 2 and mesh.shape["fsdp"] == 16
    return jax.shard_map(
        per_device_fused if fused else per_device,
        mesh=mesh,
        in_specs=(
            P(("dp", "fsdp"), None, None),
            P(("dp", "fsdp"), None, None),
            P(("dp", "fsdp"), None),
            P("fsdp"),
            P("fsdp"),
            P("fsdp", None),
            P("fsdp"),
            P("fsdp", None),
            P(),
            P("fsdp"),
            P("fsdp"),
            P("fsdp", None),
            P("fsdp"),
            P("fsdp", None),
            P("fsdp"),
        ),
        out_specs=(
            P(("dp", "fsdp"), None, None),
            P(("dp", "fsdp"), None, None),
            P("fsdp"),
            P("fsdp"),
            P("fsdp", None),
            P("fsdp"),
            P("fsdp", None),
            P(),
            P("fsdp"),
            P("fsdp"),
            P("fsdp", None),
            P("fsdp"),
            P("fsdp", None),
            P("fsdp"),
        ),
        check_vma=False,
    )
```

```python
import jax
import jax.numpy as jnp
from jax import lax
from jax.experimental import pallas as pl
from jax.experimental.pallas import tpu as pltpu
from jax.sharding import PartitionSpec as P

EPSILON = 1e-06


def normalize(rows_in, gain, shift):
    centre = jnp.mean(rows_in, axis=-1, keepdims=True)
    centred = rows_in - centre
    spread = jnp.mean(centred * centred, axis=-1, keepdims=True)
    return centred * lax.rsqrt(spread + EPSILON) * gain + shift


def smooth(values):
    return jax.nn.gelu(values, approximate=True)


def forward(input_block, token_full, channel_full, output_shift):
    gain_one, shift_one, mixing_input_weight, mixing_input_bias, mixing_output_weight = token_full
    gain_two, shift_two, w_up, bias_up, w_down, bias_down = channel_full
    normalized_rows = normalize(
        input_block, gain_one.astype(jnp.float32), shift_one.astype(jnp.float32)
    )
    normalized_reduced = normalized_rows.astype(jnp.bfloat16)
    preactivation = (
        jnp.einsum(
            "qx,exj->eqj",
            mixing_input_weight,
            normalized_reduced,
            preferred_element_type=jnp.float32,
        )
        + mixing_input_bias.astype(jnp.float32)[None, :, None]
    )
    activation_reduced = smooth(preactivation).astype(jnp.bfloat16)
    branch_output = jnp.einsum(
        "hp,zhi->zpi", mixing_output_weight, activation_reduced, preferred_element_type=jnp.float32
    )
    mixing_rows = input_block + branch_output + output_shift.astype(jnp.float32)[None, :, None]
    normed_two = normalize(mixing_rows, gain_two.astype(jnp.float32), shift_two.astype(jnp.float32))
    normed_two_low = normed_two.astype(jnp.bfloat16)
    pre_two = jnp.einsum(
        "bsd,df->bsf", normed_two_low, w_up, preferred_element_type=jnp.float32
    ) + bias_up.astype(jnp.float32)
    act_two_low = smooth(pre_two).astype(jnp.bfloat16)
    result = (
        mixing_rows
        + jnp.einsum("bsf,fd->bsd", act_two_low, w_down, preferred_element_type=jnp.float32)
        + bias_down.astype(jnp.float32)
    )
    kept = (
        normalized_reduced,
        preactivation,
        activation_reduced,
        mixing_rows,
        normed_two_low,
        pre_two,
        act_two_low,
    )
    return (result, kept)


def backward(grad_out, input_block, kept, token_full, channel_full):
    (
        normalized_reduced,
        preactivation,
        activation_reduced,
        mixing_rows,
        normed_two_low,
        pre_two,
        act_two_low,
    ) = kept
    gain_one, shift_one, mixing_input_weight, mixing_input_bias, mixing_output_weight = token_full
    gain_two, shift_two, w_up, bias_up, w_down, bias_down = channel_full
    grad_out_low = grad_out.astype(jnp.bfloat16)
    grad_act_two = jnp.einsum(
        "bsd,fd->bsf", grad_out_low, w_down, preferred_element_type=jnp.float32
    )
    grad_w_down = jnp.einsum(
        "bsf,bsd->fd", act_two_low, grad_out_low, preferred_element_type=jnp.float32
    )
    grad_bias_down = jnp.sum(grad_out, axis=(0, 1))
    grad_pre_two = jax.vjp(smooth, pre_two)[1](grad_act_two)[0]
    grad_bias_up = jnp.sum(grad_pre_two, axis=(0, 1))
    grad_pre_two_low = grad_pre_two.astype(jnp.bfloat16)
    grad_normed_two = jnp.einsum(
        "bsf,df->bsd", grad_pre_two_low, w_up, preferred_element_type=jnp.float32
    )
    grad_w_up = jnp.einsum(
        "bsd,bsf->df", normed_two_low, grad_pre_two_low, preferred_element_type=jnp.float32
    )
    norm_two_back = jax.vjp(
        normalize, mixing_rows, gain_two.astype(jnp.float32), shift_two.astype(jnp.float32)
    )[1]
    grad_through, grad_gain_two, grad_shift_two = norm_two_back(grad_normed_two)
    grad_mixed = grad_out + grad_through
    grad_out_shift = jnp.sum(grad_mixed, axis=(0, 2))
    mixing_gradient_reduced = grad_mixed.astype(jnp.bfloat16)
    grad_act = jnp.einsum(
        "qx,exj->eqj",
        mixing_output_weight,
        mixing_gradient_reduced,
        preferred_element_type=jnp.float32,
    )
    grad_w_mix_out = jnp.einsum(
        "oaq,oeq->ae",
        activation_reduced,
        mixing_gradient_reduced,
        preferred_element_type=jnp.float32,
    )
    grad_pre = jax.vjp(smooth, preactivation)[1](grad_act)[0]
    grad_bias_mix_in = jnp.sum(grad_pre, axis=(0, 2))
    preactivation_gradient_reduced = grad_pre.astype(jnp.bfloat16)
    grad_normed = jnp.einsum(
        "hp,zhi->zpi",
        mixing_input_weight,
        preactivation_gradient_reduced,
        preferred_element_type=jnp.float32,
    )
    grad_w_mix_in = jnp.einsum(
        "oaq,oeq->ae",
        preactivation_gradient_reduced,
        normalized_reduced,
        preferred_element_type=jnp.float32,
    )
    norm_one_back = jax.vjp(
        normalize, input_block, gain_one.astype(jnp.float32), shift_one.astype(jnp.float32)
    )[1]
    grad_inner, grad_gain_one, grad_shift_one = norm_one_back(grad_normed)
    grad_x = grad_mixed + grad_inner
    grad_list = (
        grad_gain_one,
        grad_shift_one,
        grad_w_mix_in,
        grad_bias_mix_in,
        grad_w_mix_out,
        grad_gain_two,
        grad_shift_two,
        grad_w_up,
        grad_bias_up,
        grad_w_down,
        grad_bias_down,
    )
    return (grad_x, grad_list, grad_out_shift)


def per_device(
    tokens,
    cotangent,
    counts,
    ln1_gain,
    ln1_bias,
    tok_in,
    tok_in_bias,
    tok_out,
    tok_out_bias,
    ln2_gain,
    ln2_bias,
    ch_in,
    ch_in_bias,
    ch_out,
    ch_out_bias,
):
    micro_total = counts.shape[1]
    per_micro = tokens.shape[0] // micro_total
    outputs = []
    input_grads = []
    grad_sums = None
    shift_sum = jnp.zeros((tok_out_bias.shape[0],), jnp.float32)
    for micro in range(micro_total):
        lower = micro * per_micro
        input_block = tokens[lower : lower + per_micro].astype(jnp.float32)
        live_rows = (jnp.arange(per_micro) < counts[0, micro]).astype(jnp.float32)[:, None, None]
        grad_out = cotangent[lower : lower + per_micro].astype(jnp.float32) * live_rows
        token_full = (
            lax.all_gather(ln1_gain, "fsdp", axis=0, tiled=True),
            lax.all_gather(ln1_bias, "fsdp", axis=0, tiled=True),
            lax.all_gather(tok_in, "fsdp", axis=0, tiled=True),
            lax.all_gather(tok_in_bias, "fsdp", axis=0, tiled=True),
            lax.all_gather(tok_out, "fsdp", axis=0, tiled=True),
        )
        channel_full = (
            lax.all_gather(ln2_gain, "fsdp", axis=0, tiled=True),
            lax.all_gather(ln2_bias, "fsdp", axis=0, tiled=True),
            lax.all_gather(ch_in, "fsdp", axis=0, tiled=True),
            lax.all_gather(ch_in_bias, "fsdp", axis=0, tiled=True),
            lax.all_gather(ch_out, "fsdp", axis=0, tiled=True),
            lax.all_gather(ch_out_bias, "fsdp", axis=0, tiled=True),
        )
        result, kept = forward(input_block, token_full, channel_full, tok_out_bias)
        outputs.append((result * live_rows).astype(jnp.bfloat16))
        token_back = (
            lax.all_gather(ln1_gain, "fsdp", axis=0, tiled=True),
            lax.all_gather(ln1_bias, "fsdp", axis=0, tiled=True),
            lax.all_gather(tok_in, "fsdp", axis=0, tiled=True),
            lax.all_gather(tok_in_bias, "fsdp", axis=0, tiled=True),
            lax.all_gather(tok_out, "fsdp", axis=0, tiled=True),
        )
        channel_back = (
            lax.all_gather(ln2_gain, "fsdp", axis=0, tiled=True),
            lax.all_gather(ln2_bias, "fsdp", axis=0, tiled=True),
            lax.all_gather(ch_in, "fsdp", axis=0, tiled=True),
            lax.all_gather(ch_in_bias, "fsdp", axis=0, tiled=True),
            lax.all_gather(ch_out, "fsdp", axis=0, tiled=True),
            lax.all_gather(ch_out_bias, "fsdp", axis=0, tiled=True),
        )
        grad_x, grad_list, grad_out_shift = backward(
            grad_out, input_block, kept, token_back, channel_back
        )
        input_grads.append(grad_x.astype(jnp.bfloat16))
        shift_sum = shift_sum + grad_out_shift
        grad_sums = (
            grad_list
            if grad_sums is None
            else tuple(jax.tree.map(jnp.add, tuple(grad_sums), tuple(grad_list)))
        )
    grad_sums = (
        lax.psum_scatter(grad_sums[0], "fsdp", scatter_dimension=0, tiled=True),
        lax.psum_scatter(grad_sums[1], "fsdp", scatter_dimension=0, tiled=True),
        lax.psum_scatter(grad_sums[2], "fsdp", scatter_dimension=0, tiled=True),
        lax.psum_scatter(grad_sums[3], "fsdp", scatter_dimension=0, tiled=True),
        lax.psum_scatter(grad_sums[4], "fsdp", scatter_dimension=0, tiled=True),
        lax.psum_scatter(grad_sums[5], "fsdp", scatter_dimension=0, tiled=True),
        lax.psum_scatter(grad_sums[6], "fsdp", scatter_dimension=0, tiled=True),
        lax.psum_scatter(grad_sums[7], "fsdp", scatter_dimension=0, tiled=True),
        lax.psum_scatter(grad_sums[8], "fsdp", scatter_dimension=0, tiled=True),
        lax.psum_scatter(grad_sums[9], "fsdp", scatter_dimension=0, tiled=True),
        lax.psum_scatter(grad_sums[10], "fsdp", scatter_dimension=0, tiled=True),
    )
    shards = lax.psum(
        (
            grad_sums[0],
            grad_sums[1],
            grad_sums[2],
            grad_sums[3],
            grad_sums[4],
            grad_sums[5],
            grad_sums[6],
            grad_sums[7],
            grad_sums[8],
            grad_sums[9],
            grad_sums[10],
        ),
        "dp",
    )
    shift_total = lax.psum(shift_sum, ("dp", "fsdp"))
    block_out = jnp.concatenate(outputs, axis=0)
    input_grad = jnp.concatenate(input_grads, axis=0)
    return (
        block_out,
        input_grad,
        shards[0],
        shards[1],
        shards[2],
        shards[3],
        shards[4],
        shift_total,
        shards[5],
        shards[6],
        shards[7],
        shards[8],
        shards[9],
        shards[10],
    )


MESH = pl.DeviceIdType.MESH
NN = (((1,), (0,)), ((), ()))
NT = (((1,), (1,)), ((), ()))
TN = (((0,), (0,)), ((), ()))
F32 = jnp.float32
BF16 = jnp.bfloat16
CHUNKS = 6
BLOCK = 784
SPAN = 224
LANES = 128
ROOM = 200
C_A = 0.7978845608
C_B = 0.7978845608 * 0.044715


def dot(left, right, dims=NN):
    return lax.dot_general(left, right, dims, preferred_element_type=F32)


def gelu_and_slope(v):
    ratio = C_B * (v * v) + C_A
    t = jnp.tanh(v * ratio)
    h = 0.5 * t + 0.5
    act = v * h
    slope = h + act * (1.0 - t) * (3.0 * ratio - 2.0 * C_A)
    return act, slope


def row_stats(v):
    mean = jnp.mean(v, axis=-1, keepdims=True)
    centred = v - mean
    spread = jnp.mean(centred * centred, axis=-1, keepdims=True)
    root = lax.rsqrt(spread + EPSILON)
    return centred * root, root, mean


def take(buf, rows, count=6):
    return jnp.concatenate([buf.at[t][rows, :] for t in range(count)], axis=1)


def put(buf, rows, value):
    for t in range(value.shape[1] // LANES):
        buf.at[t][rows, :] = value[:, LANES * t : LANES * (t + 1)]


def mega(
    counts, tokens, cotangent, vector_row, tok_in_own, tok_out_own, ch_in_own, ch_out_own,
    block_out, input_grad, ch_in_grad, ch_out_grad, small_out, gathered, act_hbm, slope_hbm, unit_two_hbm,
    normed_two, grad_rows, result_acc, grad_two_acc, stats, w_in, w_out,
    grads, core_in, cross_out, cross_keep, cross_in, line_out, line_keep, line_in, shards, stage_in,
    small_sum, own_weights, small, tok_in, tok_in_t, tok_out, tok_out_t, vectors, hidden_bias,
    vector_sums, hidden_sums, tok_in_sum, tok_out_sum,
    small_sems, z_sems, z_local, x_sems, swap_sems, core_sems, cross_sems, line_sems, end_sems, load_sems, weight_sems,
):
    total_rows, width = tokens.shape
    images, hidden = act_hbm.shape[0], act_hbm.shape[1]
    patches = total_rows // images
    per_micro = images // counts.shape[1]
    owners = 16
    tiles = width // LANES
    c = lax.axis_index("dp")
    f = lax.axis_index("fsdp")
    zi, qi = f // 4, f % 4
    partner = (1 - c, f)

    def cross(k):
        return (c, zi * 4 + (qi ^ k))

    def line(k):
        return (c, (zi ^ k) * 4 + qi)

    def remote(src, dst, sems, index, device):
        return pltpu.make_async_remote_copy(
            src_ref=src, dst_ref=dst, send_sem=sems.at[(0,) + index], recv_sem=sems.at[(1,) + index],
            device_id=device, device_id_type=MESH,
        )

    def span_rows(b):
        return pl.ds(pl.multiple_of(b * SPAN, 16), SPAN)

    spans = total_rows // SPAN

    parts = total_rows // (16 * images)
    rest = total_rows - parts * 16 * images

    def part_rows(b):
        return pl.ds(pl.multiple_of(b * 16 * images, 16), 16 * images)

    last_part = pl.ds(parts * 16 * images, rest)

    def row_loads(b, rows):
        return (
            pltpu.make_async_copy(tokens.at[rows], normed_two.at[rows], load_sems.at[0, b]),
            pltpu.make_async_copy(cotangent.at[rows], grad_rows.at[rows], load_sems.at[1, b]),
        )

    for b in range(parts):
        for copy in row_loads(b, part_rows(b)):
            copy.start()
    for copy in row_loads(parts, last_part):
        copy.start()
    barrier = pltpu.get_barrier_semaphore()
    for device in [partner] + [cross(k) for k in (1, 2, 3)] + [line(k) for k in (1, 2, 3)]:
        pl.semaphore_signal(barrier, inc=1, device_id=device, device_id_type=MESH)

    row = vector_row[...].astype(F32)

    def vector_at(offset, length, lanes=256):
        moved = row if offset == 0 else pltpu.roll(row, width - offset, 1)
        lane = lax.broadcasted_iota(jnp.int32, (1, lanes), 1)
        return jnp.where(lane < length, moved[:, 0:lanes], 0.0)

    lane = lax.broadcasted_iota(jnp.int32, (24, 256), 1)
    bias_column = jnp.transpose(jnp.broadcast_to(vector_at(240, 24, LANES), (LANES, LANES)))[0:24, 0:1]
    pad = jnp.zeros((24, 256 - patches), F32)
    padded = jnp.concatenate([tok_in_own[...].astype(F32), pad], axis=1)
    padded = jnp.where(lane == 200, jnp.broadcast_to(bias_column, (24, 256)), padded)
    rows_a = [vector_at(48 * r, 48) for r in range(5)] + [vector_at(264, 192), jnp.zeros((2, 256), F32)]
    packed_a = jnp.concatenate([padded] + rows_a, axis=0)
    padded = jnp.concatenate([tok_out_own[...].astype(F32), pad], axis=1)
    bias_rows = jnp.concatenate([vector_at(456, patches), jnp.zeros((7, 256), F32)], axis=0)
    packed_b = jnp.concatenate([padded, bias_rows], axis=0)
    small[c, zi, qi] = jnp.where(c == 0, packed_a, packed_b).astype(BF16)

    def small_line(k):
        return remote(small.at[c, zi, qi], small.at[c, zi, qi], small_sems, (k - 1,), line(k))

    def small_cross(k):
        return remote(small.at[c, :, qi], small.at[c, :, qi], small_sems, (k + 2,), cross(k))

    def small_swap():
        return remote(small.at[c], small.at[c], small_sems, (6,), partner)

    def z_copy(j, k):
        return remote(own_weights.at[j], gathered.at[c, j, zi, qi], z_sems, (j, k - 1), line(k))

    def z_own(j):
        return pltpu.make_async_copy(own_weights.at[j], gathered.at[c, j, zi, qi], z_local.at[j])

    def x_copy(j, k):
        return remote(gathered.at[c, j, :, qi], gathered.at[c, j, :, qi], x_sems, (j, k - 1), cross(k))

    def swap_copy(j):
        return remote(gathered.at[c, j], gathered.at[c, j], swap_sems, (j,), partner)

    def z_start(j):
        z_own(j).start()
        for k in (1, 2, 3):
            z_copy(j, k).start()

    def x_start(j):
        for k in (1, 2, 3):
            z_copy(j, k).wait()
        z_own(j).wait()
        for k in (1, 2, 3):
            x_copy(j, k).start()

    def swap_start(j):
        for k in (1, 2, 3):
            x_copy(j, k).wait()
        swap_copy(j).start()

    def core_copy(p, rows):
        return remote(
            grads.at[1 - c, :, :, pl.ds(0, rows)], core_in.at[p, :, :, pl.ds(0, rows)], core_sems, (p,), partner
        )

    def cross_copy(p, rows, k):
        return remote(
            cross_out.at[k - 1, :, pl.ds(0, rows)], cross_in.at[p, k - 1, :, pl.ds(0, rows)],
            cross_sems, (p, k - 1), cross(k),
        )

    def line_copy(p, rows, k):
        return remote(
            line_out.at[k - 1, pl.ds(0, rows)], line_in.at[p, k - 1, pl.ds(0, rows)], line_sems, (p, k - 1), line(k)
        )

    def cross_start(p, rows):
        core_copy(p, rows).wait()

        def per_line(z, carry):
            for k in range(4):
                q = qi ^ k
                total = grads[c, z, q, 0:rows] + core_in[p, z, q, 0:rows]
                if k == 0:
                    cross_keep[z, 0:rows] = total
                else:
                    cross_out[k - 1, z, 0:rows] = total.astype(BF16)
            return carry

        lax.fori_loop(0, 4, per_line, 0)
        for k in (1, 2, 3):
            cross_copy(p, rows, k).start()

    def line_start(p, rows):
        for k in (1, 2, 3):
            cross_copy(p, rows, k).wait()
        for k in range(4):
            z = zi ^ k
            total = cross_keep[z, 0:rows]
            for m in range(3):
                total = total + cross_in[p, m, z, 0:rows].astype(F32)
            if k == 0:
                line_keep[0:rows] = total
            else:
                line_out[k - 1, 0:rows] = total.astype(BF16)
        for k in (1, 2, 3):
            line_copy(p, rows, k).start()

    def line_finish(p, rows):
        for k in (1, 2, 3):
            line_copy(p, rows, k).wait()
        total = line_keep[0:rows]
        for m in range(3):
            total = total + line_in[p, m, 0:rows].astype(F32)
        return total

    piece = grads.shape[3]

    def live_rows():
        image = lax.broadcasted_iota(jnp.int32, (images, 1), 0)
        live = jnp.zeros((images, 1), F32)
        for micro in range(counts.shape[1]):
            inside = (image >= micro * per_micro) & (image < micro * per_micro + counts[0, micro])
            live = jnp.where(inside, 1.0, live)
        return jnp.broadcast_to(live, (images, width))

    def masked(value, live):
        return (value.reshape(-1, images, width) * live[None]).reshape(value.shape)

    def row_sum(value):
        return jnp.sum(value.reshape(4, value.shape[0] // 32, 8, width).sum(1), axis=0)

    stat_lane = lax.broadcasted_iota(jnp.int32, (SPAN, LANES), 1)

    def image_rows(i):
        return pl.ds(i, patches, stride=images)

    def own_rows():
        @pl.when(c == 0)
        def _():
            group = lax.broadcasted_iota(jnp.int32, (48, LANES), 1) >> 5
            for j in range(CHUNKS):
                for b in range(2):
                    for t in range(2):
                        tile = None
                        for g in range(4):
                            source = 192 * (8 * b + 4 * t + g) + 32 * j
                            part = ch_in_own[:, source // LANES * LANES : (source // LANES + 1) * LANES].astype(F32)
                            shift = (32 * g - source) % LANES
                            part = part if shift == 0 else pltpu.roll(part, shift, 1)
                            tile = part if tile is None else jnp.where(group == g, part, tile)
                        own_weights[j, 48 * b : 48 * b + 48, LANES * t : LANES * (t + 1)] = tile.astype(BF16)

        @pl.when(c == 1)
        def _():
            for j in range(CHUNKS):
                for b in range(3):
                    own_weights[j, 32 * b : 32 * b + 32] = ch_out_own[32 * j : 32 * j + 32, 256 * b : 256 * b + 256]

    def norm_one():
        pl.semaphore_wait(barrier, 7)
        for k in (1, 2, 3):
            small_line(k).start()
        own_rows()
        z_start(0)
        live = live_rows()

        def part(b, rows):
            count = rows.size
            each = count // images
            for copy in row_loads(b, rows):
                copy.wait()
            unit, root, mean = row_stats(normed_two[rows].astype(F32))
            for t in range(tiles):
                by_image = jnp.swapaxes(unit[:, LANES * t : LANES * (t + 1)].reshape(each, images, LANES), 0, 1)
                for i in range(images):
                    grad_two_acc[t, pl.ds(pl.multiple_of(ROOM * i + 16 * b, 8), each)] = by_image[i]
            stat = lax.broadcasted_iota(jnp.int32, (count, LANES), 1)
            stats[rows] = jnp.where(stat < 32, root, mean)
            grad = masked(grad_rows[rows].astype(F32), live)
            grad_rows[rows] = grad.astype(BF16)
            return row_sum(grad)

        def step(b, carry):
            carry = carry + part(b, part_rows(b))

            @pl.when(b == 4)
            def _():
                for k in (1, 2, 3):
                    small_line(k).wait()
                for k in (1, 2, 3):
                    small_cross(k).start()
                z_start(1)

            @pl.when(b == 9)
            def _():
                for k in (1, 2, 3):
                    small_cross(k).wait()
                small_swap().start()

            return carry

        sums = lax.fori_loop(0, parts, step, jnp.zeros((8, width), F32))
        sums = sums + part(parts, last_part)
        vector_sums[...] = jnp.zeros(vector_sums.shape, F32)
        vector_sums[4:5] = jnp.sum(sums, axis=0, keepdims=True)
    norm_one()
    hidden_sums[...] = jnp.zeros(hidden_sums.shape, F32)
    tok_in_sum[...] = jnp.zeros(tok_in_sum.shape, F32)
    tok_out_sum[...] = jnp.zeros(tok_out_sum.shape, F32)
    small_swap().wait()

    part_a = small[0].astype(F32).reshape(owners, 32, 256)
    part_b = small[1].astype(F32).reshape(owners, 32, 256)
    full_in = part_a[:, 0:24].reshape(hidden, 256)
    full_out = part_b[:, 0:24].reshape(hidden, 256)
    tok_in[...] = full_in.astype(BF16)
    tok_in_t[...] = jnp.transpose(full_in).astype(BF16)
    tok_out[...] = full_out.astype(BF16)
    out_rows = jnp.concatenate([full_out, bias_rows, jnp.zeros((120, 256), F32)], axis=0)
    tok_out_t[...] = jnp.transpose(out_rows).astype(BF16)

    flat_a = part_a.reshape(owners * 32, 256).astype(BF16)
    pick_r = lax.broadcasted_iota(jnp.int32, (8, owners * 32), 0)
    pick_p = lax.broadcasted_iota(jnp.int32, (8, owners * 32), 1)
    pick = jnp.where((pick_p & 31) == 24 + pick_r, 1.0, 0.0).astype(BF16)
    col = lax.broadcasted_iota(jnp.int32, (256, width), 1)
    lane = lax.broadcasted_iota(jnp.int32, (256, width), 0)
    spread = jnp.where(lane == col - 48 * ((col * 43691) >> 21), 1.0, 0.0).astype(BF16)
    own_n = (lax.broadcasted_iota(jnp.int32, (owners * 32, width), 1) * 43691) >> 21
    own_p = lax.broadcasted_iota(jnp.int32, (owners * 32, width), 0) >> 5
    vectors[...] = dot(pick, jnp.where(own_n == own_p, dot(flat_a, spread), 0.0).astype(BF16))
    span_n = owners * 32
    own_n = lax.broadcasted_iota(jnp.int32, (span_n, span_n), 1) >> 5
    own_p = lax.broadcasted_iota(jnp.int32, (span_n, span_n), 0) >> 5
    col = lax.broadcasted_iota(jnp.int32, (256, span_n), 1)
    lane = lax.broadcasted_iota(jnp.int32, (256, span_n), 0)
    for j in range(CHUNKS):
        spread = jnp.where(lane == 32 * j + (col & 31), 1.0, 0.0).astype(BF16)
        rows = dot(pick, jnp.where(own_n == own_p, dot(flat_a, spread), 0.0).astype(BF16))
        hidden_bias[j] = rows[5:6]

    def weight_loads(j, p):
        return [
            pltpu.make_async_copy(
                gathered.at[0, j, :, :, pl.ds(48 * b, 48)], w_in.at[p, :, :, :, pl.ds(256 * b, 256)], weight_sems.at[b]
            )
            for b in range(2)
        ] + [
            pltpu.make_async_copy(
                gathered.at[1, j, :, :, pl.ds(32 * b, 32)], w_out.at[p, :, :, :, pl.ds(256 * b, 256)],
                weight_sems.at[2 + b],
            )
            for b in range(3)
        ]

    ones_low = jnp.where(lax.broadcasted_iota(jnp.int32, (64, width), 0) == 8, 1.0, 0.0).astype(BF16)
    ones_act = jnp.where(lax.broadcasted_iota(jnp.int32, (128, width), 0) == 0, 1.0, 0.0).astype(BF16)

    def token_forward(act_buf, slope_buf, normed, unit_buf, out_sems, unit_sems):
        def stores(i, slot):
            return (
                pltpu.make_async_copy(act_buf.at[slot, pl.ds(0, hidden)], act_hbm.at[i], out_sems.at[slot, 0]),
                pltpu.make_async_copy(slope_buf.at[slot], slope_hbm.at[i], out_sems.at[slot, 1]),
            )

        for slot in range(4):
            act_buf[slot, hidden : hidden + 128] = ones_act
        for n in range(2):
            normed[n, 192:256] = ones_low

        def pair(g, base):
            @pl.when(g >= 2)
            def _():
                for n in range(2):
                    for copy in stores(2 * g - 4 + n, base + n):
                        copy.wait()

            @pl.when(g == 0)
            def _():
                x_start(0)
                z_start(2)

            @pl.when(g == 4)
            def _():
                x_start(1)
                z_start(3)

            for n in range(2):
                unit = take(grad_two_acc, pl.ds(pl.multiple_of(ROOM * (2 * g + n), 8), patches))
                normed[n, 0:patches] = (unit * vectors[0:1] + vectors[1:2]).astype(BF16)
            pre = [dot(tok_in[...], normed[n]) for n in range(2)]
            for n in range(2):
                act, slope = gelu_and_slope(pre[n])
                act_buf[base + n, 0:hidden] = act.astype(BF16)
                slope_buf[base + n] = slope.astype(BF16)
            mixed = [dot(tok_out_t[...], act_buf[base + n]) for n in range(2)]
            for n in range(2):
                put(result_acc, image_rows(2 * g + n), mixed[n][0:patches])
                for copy in stores(2 * g + n, base + n):
                    copy.start()

        def pairs(h, carry):
            for half in range(2):
                pair(2 * h + half, 2 * half)
            return carry

        lax.fori_loop(0, images // 4, pairs, 0)
        for i in range(images - 4, images):
            for copy in stores(i, i % 4):
                copy.wait()
        swap_start(0)
        x_start(2)
        z_start(4)

        def unit_two_store(b):
            return pltpu.make_async_copy(unit_buf.at[b % 4], unit_two_hbm.at[span_rows(b)], unit_sems.at[b % 4])

        def span(b, carry):
            rows = span_rows(b)

            @pl.when(b >= 4)
            def _():
                unit_two_store(b - 4).wait()

            mixed = normed_two[rows].astype(F32) + take(result_acc, rows)
            put(result_acc, rows, mixed)
            unit, root, _ = row_stats(mixed)
            stats[rows] = jnp.where(stat_lane < 64, stats[rows], root)
            unit_buf[b % 4] = unit.astype(BF16)
            unit_two_store(b).start()
            normed_two[rows] = (unit * vectors[2:3] + vectors[3:4]).astype(BF16)
            put(grad_two_acc, rows, jnp.zeros((SPAN, width), F32))

            @pl.when(b == 10)
            def _():
                swap_copy(0).wait()
                for copy in weight_loads(0, 0):
                    copy.start()
                swap_start(1)
                x_start(3)
                z_start(5)

            return carry

        lax.fori_loop(0, spans, span, 0)
        for b in range(spans - 4, spans):
            unit_two_store(b).wait()

    pl.run_scoped(
        token_forward,
        pltpu.VMEM((4, hidden + 128, width), BF16),
        pltpu.VMEM((4, hidden, width), BF16),
        pltpu.VMEM((2, 256, width), BF16),
        pltpu.VMEM((4, SPAN, width), BF16),
        pltpu.SemaphoreType.DMA((4, 2)),
        pltpu.SemaphoreType.DMA((4,)),
    )

    def channel(act_all, slope_all):
        chunk = w_in.shape[-1]

        for copy in weight_loads(0, 0):
            copy.wait()

        def tick(j, carry):
            p = j % 2

            @pl.when(j >= 1)
            def _():
                core_copy(1 - p, piece).start()

            def block(b, inner):
                rows = pl.ds(pl.multiple_of(b * BLOCK, 16), BLOCK)
                up = w_in[p].reshape(width, chunk)
                down = w_out[p].reshape(chunk, width)
                pre = dot(normed_two[rows], up) + hidden_bias[j]
                grad_act = dot(grad_rows[rows], down, NT)
                act, slope = gelu_and_slope(pre)
                grad_pre = grad_act * slope
                hidden_sums[j] += jnp.sum(grad_pre.reshape(BLOCK // 112, 14, 8, chunk).sum(1), axis=0)
                act_all[rows] = act.astype(BF16)
                slope_all[rows] = grad_pre.astype(BF16)
                forward_part = dot(act_all[rows], down)
                for t in range(tiles):
                    result_acc[t, rows] += forward_part[:, LANES * t : LANES * (t + 1)]
                backward_part = dot(slope_all[rows], up, NT)
                for t in range(tiles):
                    grad_two_acc[t, rows] += backward_part[:, LANES * t : LANES * (t + 1)]

                @pl.when((b == 0) & (j >= 2))
                def _():
                    line_start(p, piece)

                @pl.when((b == 1) & (j >= 1))
                def _():
                    cross_start(1 - p, piece)

                @pl.when((b == 0) & (j == 0))
                def _():
                    x_start(4)
                    swap_start(2)

                @pl.when((b == 2) & (j == 0))
                def _():
                    x_start(5)

                @pl.when((b == 2) & (j >= 2))
                def _():
                    shards[j - 2] = line_finish(p, piece)

                @pl.when((b == 2) & (j + 1 < CHUNKS))
                def _():
                    swap_copy(j + 1).wait()
                    for copy in weight_loads(j + 1, 1 - p):
                        copy.start()

                @pl.when((b == 3) & (j + 3 < CHUNKS))
                def _():
                    swap_start(j + 3)

                return inner

            lax.fori_loop(0, total_rows // BLOCK, block, 0)
            up_grad = dot(normed_two[...], slope_all[...], TN)
            for b in range(2):
                grads[0, :, :, 48 * b : 48 * b + 48] = up_grad[:, 256 * b : 256 * b + 256].reshape(4, 4, 48, 256)
            down_grad = dot(act_all[...], grad_rows[...], TN)
            for b in range(3):
                grads[1, :, :, 32 * b : 32 * b + 32] = down_grad[:, 256 * b : 256 * b + 256].reshape(4, 4, 32, 256)

            @pl.when(j + 1 < CHUNKS)
            def _():
                for copy in weight_loads(j + 1, 1 - p):
                    copy.wait()

            return carry

        lax.fori_loop(0, CHUNKS, tick, 0)

    pl.run_scoped(
        channel,
        pltpu.VMEM((total_rows, 512), BF16),
        pltpu.VMEM((total_rows, 512), BF16),
    )

    def stage_out_copy(b):
        return remote(
            shards.at[:, pl.ds(32 * b, 32)], ch_out_grad.at[:, :, pl.ds(256 * b, 256)], end_sems, (b,), partner
        )

    def stage_out_own(b):
        return pltpu.make_async_copy(
            shards.at[:, pl.ds(32 * b, 32)], ch_out_grad.at[:, :, pl.ds(256 * b, 256)], end_sems.at[0, 4 + b]
        )

    def send_stages():
        @pl.when(c == 0)
        def _():
            remote(stage_in, ch_in_grad, end_sems, (0,), partner).start()
            pltpu.make_async_copy(stage_in, ch_in_grad, end_sems.at[0, 4]).start()

        @pl.when(c == 1)
        def _():
            for b in range(3):
                stage_out_copy(b).start()
                stage_out_own(b).start()

    def fill_stages():
        @pl.when(c == 0)
        def _():
            group = lax.broadcasted_iota(jnp.int32, (48, LANES), 1) >> 5
            for t in range(24):
                tile = None
                for g in range(4):
                    unit = LANES * t + 32 * g
                    o, j = unit // 192, unit % 192 // 32
                    b, source = o // 8, 32 * (o % 8)
                    part = shards[j, 48 * b : 48 * b + 48, source // LANES * LANES : (source // LANES + 1) * LANES]
                    shift = (32 * g - source) % LANES
                    part = part if shift == 0 else pltpu.roll(part, shift, 1)
                    tile = part if tile is None else jnp.where(group == g, part, tile)
                stage_in[:, LANES * t : LANES * (t + 1)] = tile

    def token_backward(units, unit_buf, out_buf, x_load_sems, in_sems, unit_sems, out_sems):
        def act_at(slot, count):
            return normed_two.at[pl.ds(512 * slot, count)]

        def slope_at(slot):
            return grad_rows.at[pl.ds(384 * slot, hidden)]

        def loads(i, slot):
            return (
                pltpu.make_async_copy(act_hbm.at[i], act_at(slot, hidden), in_sems.at[slot, 0]),
                pltpu.make_async_copy(slope_hbm.at[i], slope_at(slot), in_sems.at[slot, 1]),
            )

        def unit_two_load(b):
            return pltpu.make_async_copy(unit_two_hbm.at[span_rows(b)], unit_buf.at[b % 4], unit_sems.at[b % 4])

        def x_load(b):
            return pltpu.make_async_copy(tokens.at[span_rows(b)], normed_two.at[span_rows(b)], x_load_sems.at[b])

        core_copy(1, piece).start()
        for b in range(spans):
            x_load(b).start()
            if b < 3:
                unit_two_load(b).start()
        live = live_rows()

        def out_store(b, slot):
            return pltpu.make_async_copy(out_buf.at[slot], block_out.at[span_rows(b)], out_sems.at[slot])

        def span(b, sums):
            slot = b % 2

            @pl.when(b + 3 < spans)
            def _():
                unit_two_load(b + 3).start()

            @pl.when(b >= 2)
            def _():
                out_store(b - 2, slot).wait()

            x_load(b).wait()
            unit_two_load(b).wait()
            rows = span_rows(b)
            put(units, rows, (normed_two[rows].astype(F32) - stats[rows, 32:33]) * stats[rows, 0:1])
            unit = unit_buf[b % 4].astype(F32)
            root = stats[rows, 64:65]
            grad = take(grad_two_acc, rows)
            weighted = grad * unit
            scaled = grad * vectors[2:3]
            inner = jnp.mean(weighted * vectors[2:3], axis=-1, keepdims=True)
            mixed = grad_rows[rows].astype(F32) + root * (
                scaled - jnp.mean(scaled, axis=-1, keepdims=True) - unit * inner
            )
            put(grad_two_acc, rows, mixed)
            out_buf[slot] = masked(take(result_acc, rows) + vectors[4:5], live).astype(BF16)
            out_store(b, slot).start()

            @pl.when(b == 2)
            def _():
                line_start(0, piece)

            @pl.when(b == 7)
            def _():
                cross_start(1, piece)

            return sums[0] + row_sum(weighted), sums[1] + row_sum(grad)

        zero = jnp.zeros((8, width), F32)
        sums = lax.fori_loop(0, spans, span, (zero, zero))
        for b in (spans - 2, spans - 1):
            out_store(b, b % 2).wait()
        for n in range(2):
            for copy in loads(n, n):
                copy.start()
        for slot in range(4):
            normed_two[512 * slot + hidden : 512 * slot + 512] = ones_act
        for n in range(2):
            normed_two[2048 + 256 * n + 192 : 2048 + 256 * n + 256] = ones_low
            normed_two[2560 + 256 * n + 192 : 2560 + 256 * n + 256] = jnp.zeros((64, width), BF16)
        vector_sums[2:3] = jnp.sum(sums[0], axis=0, keepdims=True)
        vector_sums[3:4] = jnp.sum(sums[1], axis=0, keepdims=True)
        shards[CHUNKS - 2] = line_finish(0, piece)

        def pair(g, base):
            @pl.when(g + 1 < images // 2)
            def _():
                for n in range(2):
                    for copy in loads(2 * g + 2 + n, 2 - base + n):
                        copy.start()

            for n in range(2):
                for copy in loads(2 * g + n, base + n):
                    copy.wait()

            @pl.when(g == 3)
            def _():
                line_start(1, piece)

            @pl.when(g == 6)
            def _():
                shards[CHUNKS - 1] = line_finish(1, piece)
                fill_stages()
                send_stages()

            for n in range(2):
                low = take(grad_two_acc, image_rows(2 * g + n))
                normed_two[2560 + 256 * n : 2560 + 256 * n + patches] = low.astype(BF16)
            unit = [take(units, image_rows(2 * g + n)) for n in range(2)]
            for n in range(2):
                normed_two[2048 + 256 * n : 2048 + 256 * n + patches] = (
                    unit[n] * vectors[0:1] + vectors[1:2]
                ).astype(BF16)
            lows = [normed_two[2560 + 256 * n : 2816 + 256 * n] for n in range(2)]
            grad_act = [dot(tok_out[...], lows[n]) for n in range(2)]
            for n in range(2):
                grad_rows[1536 + 384 * n : 1920 + 384 * n] = (
                    grad_act[n] * slope_at(base + n)[...].astype(F32)
                ).astype(BF16)
            tok_out_sum[...] += dot(act_at(base, 512)[...], lows[0], NT) + dot(act_at(base + 1, 512)[...], lows[1], NT)
            pres = [grad_rows[1536 + 384 * n : 1920 + 384 * n] for n in range(2)]
            grad = [dot(tok_in_t[...], pres[n])[0:patches] for n in range(2)]
            tok_in_sum[...] += dot(pres[0], normed_two[2048:2304], NT) + dot(pres[1], normed_two[2304:2560], NT)
            for n in range(2):
                put(result_acc, image_rows(2 * g + n), grad[n])
            gain = grad[0] * unit[0] + grad[1] * unit[1]
            vector_sums[0:1] += jnp.sum(gain, axis=0, keepdims=True)
            vector_sums[1:2] += jnp.sum(grad[0] + grad[1], axis=0, keepdims=True)

        def pairs(h, carry):
            for half in range(2):
                pair(2 * h + half, 2 * half)
            return carry

        lax.fori_loop(0, images // 4, pairs, 0)

        grads[0, :, :, 0:24] = tok_in_sum[...].reshape(4, 4, 24, 256)
        grads[1, :, :, 0:24] = tok_out_sum[0:hidden].reshape(4, 4, 24, 256)
        sums = vector_sums[...]
        hidden_rows = jnp.concatenate(
            [jnp.sum(hidden_sums[j], axis=0, keepdims=True) for j in range(CHUNKS)] + [jnp.zeros((2, 512), F32)], axis=0
        )
        for o in range(owners):
            moved = sums if o == 0 else pltpu.roll(sums, width - 48 * o, 1)
            grads[0, o // 4, o % 4, 24:32, 0:128] = moved[:, 0:128]
            grads[0, o // 4, o % 4, 24:32, 128:256] = jnp.zeros((8, 128), F32)
            grads[0, o // 4, o % 4, 31:32] = tok_out_sum[hidden : hidden + 1]
            moved = hidden_rows if o == 0 else pltpu.roll(hidden_rows, 512 - 32 * o, 1)
            grads[1, o // 4, o % 4, 24:32, 0:128] = moved[:, 0:128]
            grads[1, o // 4, o % 4, 24:32, 128:256] = jnp.zeros((8, 128), F32)
        core_copy(0, 32).start()

        def grad_store(b, slot):
            return pltpu.make_async_copy(out_buf.at[slot], input_grad.at[span_rows(b)], out_sems.at[slot])

        def last(b, carry):
            slot = b % 2

            @pl.when(b >= 2)
            def _():
                grad_store(b - 2, slot).wait()

            rows = span_rows(b)
            unit = take(units, rows)
            root = stats[rows, 0:1]
            scaled = take(result_acc, rows) * vectors[0:1]
            inner = jnp.mean(scaled * unit, axis=-1, keepdims=True)
            out_buf[slot] = (
                take(grad_two_acc, rows)
                + root * (scaled - jnp.mean(scaled, axis=-1, keepdims=True) - unit * inner)
            ).astype(BF16)
            grad_store(b, slot).start()

            @pl.when(b == 4)
            def _():
                cross_start(0, 32)

            @pl.when(b == spans - 1)
            def _():
                line_start(0, 32)

            return carry

        lax.fori_loop(0, spans, last, 0)
        for b in (spans - 2, spans - 1):
            grad_store(b, b % 2).wait()

    pl.run_scoped(
        token_backward,
        pltpu.VMEM((tiles, total_rows, LANES), F32),
        pltpu.VMEM((4, SPAN, width), BF16),
        pltpu.VMEM((2, SPAN, width), BF16),
        pltpu.SemaphoreType.DMA((spans,)),
        pltpu.SemaphoreType.DMA((4, 2)),
        pltpu.SemaphoreType.DMA((4,)),
        pltpu.SemaphoreType.DMA((2,)),
    )

    small_sum[...] = line_finish(0, 32)
    small_end = remote(small_sum, small_out.at[c], end_sems, (3,), partner)
    small_own = pltpu.make_async_copy(small_sum, small_out.at[c], end_sems.at[1, 4])
    small_end.start()
    small_own.start()
    small_end.wait()
    small_own.wait()

    @pl.when(c == 0)
    def _():
        remote(stage_in, ch_in_grad, end_sems, (0,), partner).wait_send()
        pltpu.make_async_copy(stage_in, ch_in_grad, end_sems.at[0, 4]).wait()
        for b in range(3):
            stage_out_copy(b).wait_recv()

    @pl.when(c == 1)
    def _():
        for b in range(3):
            stage_out_copy(b).wait_send()
            stage_out_own(b).wait()
        remote(stage_in, ch_in_grad, end_sems, (0,), partner).wait_recv()


def finish(small, ch_in_sum, ch_out_sum, *outs):
    gain_one, bias_one, tok_in, tok_in_bias, tok_out, tok_out_bias, gain_two, bias_two, ch_in, ch_in_bias, ch_out, ch_out_bias = outs
    per_tok, patches = tok_in.shape
    ch_in[...] = ch_in_sum[...]
    ch_out[...] = ch_out_sum[...]
    tok_in[...] = small[0, 0:per_tok, 0:patches]
    tok_out[...] = small[1, 0:per_tok, 0:patches]
    column = jnp.broadcast_to(small[0, 0:32, 200:201], (32, LANES))
    flipped = jnp.transpose(jnp.concatenate([column, jnp.zeros((LANES - 32, LANES), F32)], axis=0))
    tok_in_bias[...] = flipped[0:1, 0:per_tok]
    tok_out_bias[...] = small[0, 31:32, 0:patches]
    for r, out in enumerate((gain_one, bias_one, gain_two, bias_two, ch_out_bias)):
        out[...] = small[0, 24 + r : 25 + r, 0 : out.shape[1]]
    each = ch_in_bias.shape[1] // CHUNKS
    lane = lax.broadcasted_iota(jnp.int32, (1, 256), 1)
    total = jnp.zeros((1, 256), F32)
    for j in range(CHUNKS):
        part = small[1, 24 + j : 25 + j]
        part = part if j == 0 else pltpu.roll(part, each * j, 1)
        total = jnp.where((lane >= each * j) & (lane < each * (j + 1)), part, total)
    ch_in_bias[...] = total[:, 0 : ch_in_bias.shape[1]]


def per_device_fused(
    tokens, cotangent, counts, ln1_gain, ln1_bias, tok_in, tok_in_bias, tok_out, tok_out_bias,
    ln2_gain, ln2_bias, ch_in, ch_in_bias, ch_out, ch_out_bias,
):
    images, patches, width = tokens.shape
    per_in, inner = ch_in.shape
    per_out = ch_out.shape[0]
    per_tok = tok_in.shape[0]
    owners = width // per_in
    hidden = per_tok * owners
    each = per_out // CHUNKS
    chunk = each * owners
    rows = images * patches

    def by_patch(array):
        return array.transpose(1, 0, 2).reshape(rows, width)

    vector_row = jnp.zeros((width,), F32)
    offset = 0
    for vector in (ln1_gain, ln1_bias, ln2_gain, ln2_bias, ch_out_bias, tok_in_bias, ch_in_bias, tok_out_bias):
        length = vector.shape[0]
        vector_row = vector_row + jnp.pad(vector, (offset, width - offset - length)).astype(F32)
        offset += length
    vector_row = vector_row[None]
    any_spec = pl.BlockSpec(memory_space=pl.ANY)
    vmem_spec = pl.BlockSpec(memory_space=pltpu.VMEM)
    vmem = pltpu.VMEM
    dma = pltpu.SemaphoreType.DMA
    shape = jax.ShapeDtypeStruct
    tiled = (width // LANES, rows, LANES)
    results = pl.pallas_call(
        mega,
        in_specs=[pl.BlockSpec(memory_space=pltpu.SMEM), any_spec, any_spec] + [vmem_spec] * 5,
        out_specs=[any_spec] * 9,
        out_shape=[
            shape((rows, width), BF16),
            shape((rows, width), BF16),
            shape(ch_in.shape, F32),
            shape((CHUNKS, each, width), F32),
            shape((2, 32, 256), F32),
            shape((2, CHUNKS, 4, 4, 96, 256), BF16),
            shape((images, hidden, width), BF16),
            shape((images, hidden, width), BF16),
            shape((rows, width), BF16),
        ],
        scratch_shapes=[
            vmem((rows, width), BF16),
            vmem((rows, width), BF16),
            vmem(tiled, F32),
            vmem((width // LANES, images * ROOM, LANES), F32),
            vmem((rows, LANES), F32),
            vmem((2, 4, 4, per_in, chunk), BF16),
            vmem((2, 4, 4, each, width), BF16),
            vmem((2, 4, 4, 96, 256), F32),
            vmem((2, 4, 4, 96, 256), F32),
            vmem((3, 4, 96, 256), BF16),
            vmem((4, 96, 256), F32),
            vmem((2, 3, 4, 96, 256), BF16),
            vmem((3, 96, 256), BF16),
            vmem((96, 256), F32),
            vmem((2, 3, 96, 256), BF16),
            vmem((CHUNKS, 96, 256), F32),
            vmem(ch_in.shape, F32),
            vmem((32, 256), F32),
            vmem((CHUNKS, 96, 256), BF16),
            vmem((2, 4, 4, 32, 256), BF16),
            vmem((hidden, 256), BF16),
            vmem((256, hidden), BF16),
            vmem((hidden, 256), BF16),
            vmem((256, hidden + 128), BF16),
            vmem((8, width), F32),
            vmem((CHUNKS, 1, chunk), F32),
            vmem((8, width), F32),
            vmem((CHUNKS, 8, chunk), F32),
            vmem((hidden, 256), F32),
            vmem((hidden + 128, 256), F32),
            dma((2, 7)),
            dma((2, CHUNKS, 3)),
            dma((CHUNKS,)),
            dma((2, CHUNKS, 3)),
            dma((2, CHUNKS)),
            dma((2, 2)),
            dma((2, 2, 3)),
            dma((2, 2, 3)),
            dma((2, 7)),
            dma((2, 14)),
            dma((5,)),
        ],
        compiler_params=pltpu.CompilerParams(
            collective_id=0, has_side_effects=True, vmem_limit_bytes=61 * 1024 * 1024
        ),
        cost_estimate=pl.CostEstimate(
            flops=12 * rows * width * inner, bytes_accessed=100_000_000, transcendentals=rows * inner
        ),
    )(counts, by_patch(tokens), by_patch(cotangent), vector_row, tok_in, tok_out, ch_in, ch_out)
    block_out, input_grad, in_sum, out_sum, small = results[:5]
    line = shape((1, per_in), F32)
    outs = pl.pallas_call(
        finish,
        in_specs=[vmem_spec] * 3,
        out_specs=[vmem_spec] * 12,
        out_shape=[
            line, line, shape(tok_in.shape, F32), shape((1, per_tok), F32), shape(tok_out.shape, F32),
            shape((1, patches), F32), line, line, shape(ch_in.shape, F32), shape((1, per_out), F32),
            shape(ch_out.shape, F32), line,
        ],
    )(small, in_sum, out_sum.reshape(ch_out.shape))

    def by_image(array):
        return array.reshape(patches, images, width).transpose(1, 0, 2)

    flat = (0, 1, 3, 5, 6, 7, 9, 11)
    outs = [out.reshape(-1) if n in flat else out for n, out in enumerate(outs)]
    return (by_image(block_out), by_image(input_grad), *outs)


def solution(mesh):
    fused = mesh.shape["dp"] == 2 and mesh.shape["fsdp"] == 16
    return jax.shard_map(
        per_device_fused if fused else per_device,
        mesh=mesh,
        in_specs=(
            P(("dp", "fsdp"), None, None),
            P(("dp", "fsdp"), None, None),
            P(("dp", "fsdp"), None),
            P("fsdp"),
            P("fsdp"),
            P("fsdp", None),
            P("fsdp"),
            P("fsdp", None),
            P(),
            P("fsdp"),
            P("fsdp"),
            P("fsdp", None),
            P("fsdp"),
            P("fsdp", None),
            P("fsdp"),
        ),
        out_specs=(
            P(("dp", "fsdp"), None, None),
            P(("dp", "fsdp"), None, None),
            P("fsdp"),
            P("fsdp"),
            P("fsdp", None),
            P("fsdp"),
            P("fsdp", None),
            P(),
            P("fsdp"),
            P("fsdp"),
            P("fsdp", None),
            P("fsdp"),
            P("fsdp", None),
            P("fsdp"),
        ),
        check_vma=False,
    )
```

```python
import jax
import jax.numpy as jnp
from jax import lax
from jax.experimental import pallas as pl
from jax.experimental.pallas import tpu as pltpu
from jax.sharding import PartitionSpec as P

EPSILON = 1e-06


def normalize(rows_in, gain, shift):
    centre = jnp.mean(rows_in, axis=-1, keepdims=True)
    centred = rows_in - centre
    spread = jnp.mean(centred * centred, axis=-1, keepdims=True)
    return centred * lax.rsqrt(spread + EPSILON) * gain + shift


def smooth(values):
    return jax.nn.gelu(values, approximate=True)


def forward(input_block, token_full, channel_full, output_shift):
    gain_one, shift_one, mixing_input_weight, mixing_input_bias, mixing_output_weight = token_full
    gain_two, shift_two, w_up, bias_up, w_down, bias_down = channel_full
    normalized_rows = normalize(
        input_block, gain_one.astype(jnp.float32), shift_one.astype(jnp.float32)
    )
    normalized_reduced = normalized_rows.astype(jnp.bfloat16)
    preactivation = (
        jnp.einsum(
            "qx,exj->eqj",
            mixing_input_weight,
            normalized_reduced,
            preferred_element_type=jnp.float32,
        )
        + mixing_input_bias.astype(jnp.float32)[None, :, None]
    )
    activation_reduced = smooth(preactivation).astype(jnp.bfloat16)
    branch_output = jnp.einsum(
        "hp,zhi->zpi", mixing_output_weight, activation_reduced, preferred_element_type=jnp.float32
    )
    mixing_rows = input_block + branch_output + output_shift.astype(jnp.float32)[None, :, None]
    normed_two = normalize(mixing_rows, gain_two.astype(jnp.float32), shift_two.astype(jnp.float32))
    normed_two_low = normed_two.astype(jnp.bfloat16)
    pre_two = jnp.einsum(
        "bsd,df->bsf", normed_two_low, w_up, preferred_element_type=jnp.float32
    ) + bias_up.astype(jnp.float32)
    act_two_low = smooth(pre_two).astype(jnp.bfloat16)
    result = (
        mixing_rows
        + jnp.einsum("bsf,fd->bsd", act_two_low, w_down, preferred_element_type=jnp.float32)
        + bias_down.astype(jnp.float32)
    )
    kept = (
        normalized_reduced,
        preactivation,
        activation_reduced,
        mixing_rows,
        normed_two_low,
        pre_two,
        act_two_low,
    )
    return (result, kept)


def backward(grad_out, input_block, kept, token_full, channel_full):
    (
        normalized_reduced,
        preactivation,
        activation_reduced,
        mixing_rows,
        normed_two_low,
        pre_two,
        act_two_low,
    ) = kept
    gain_one, shift_one, mixing_input_weight, mixing_input_bias, mixing_output_weight = token_full
    gain_two, shift_two, w_up, bias_up, w_down, bias_down = channel_full
    grad_out_low = grad_out.astype(jnp.bfloat16)
    grad_act_two = jnp.einsum(
        "bsd,fd->bsf", grad_out_low, w_down, preferred_element_type=jnp.float32
    )
    grad_w_down = jnp.einsum(
        "bsf,bsd->fd", act_two_low, grad_out_low, preferred_element_type=jnp.float32
    )
    grad_bias_down = jnp.sum(grad_out, axis=(0, 1))
    grad_pre_two = jax.vjp(smooth, pre_two)[1](grad_act_two)[0]
    grad_bias_up = jnp.sum(grad_pre_two, axis=(0, 1))
    grad_pre_two_low = grad_pre_two.astype(jnp.bfloat16)
    grad_normed_two = jnp.einsum(
        "bsf,df->bsd", grad_pre_two_low, w_up, preferred_element_type=jnp.float32
    )
    grad_w_up = jnp.einsum(
        "bsd,bsf->df", normed_two_low, grad_pre_two_low, preferred_element_type=jnp.float32
    )
    norm_two_back = jax.vjp(
        normalize, mixing_rows, gain_two.astype(jnp.float32), shift_two.astype(jnp.float32)
    )[1]
    grad_through, grad_gain_two, grad_shift_two = norm_two_back(grad_normed_two)
    grad_mixed = grad_out + grad_through
    grad_out_shift = jnp.sum(grad_mixed, axis=(0, 2))
    mixing_gradient_reduced = grad_mixed.astype(jnp.bfloat16)
    grad_act = jnp.einsum(
        "qx,exj->eqj",
        mixing_output_weight,
        mixing_gradient_reduced,
        preferred_element_type=jnp.float32,
    )
    grad_w_mix_out = jnp.einsum(
        "oaq,oeq->ae",
        activation_reduced,
        mixing_gradient_reduced,
        preferred_element_type=jnp.float32,
    )
    grad_pre = jax.vjp(smooth, preactivation)[1](grad_act)[0]
    grad_bias_mix_in = jnp.sum(grad_pre, axis=(0, 2))
    preactivation_gradient_reduced = grad_pre.astype(jnp.bfloat16)
    grad_normed = jnp.einsum(
        "hp,zhi->zpi",
        mixing_input_weight,
        preactivation_gradient_reduced,
        preferred_element_type=jnp.float32,
    )
    grad_w_mix_in = jnp.einsum(
        "oaq,oeq->ae",
        preactivation_gradient_reduced,
        normalized_reduced,
        preferred_element_type=jnp.float32,
    )
    norm_one_back = jax.vjp(
        normalize, input_block, gain_one.astype(jnp.float32), shift_one.astype(jnp.float32)
    )[1]
    grad_inner, grad_gain_one, grad_shift_one = norm_one_back(grad_normed)
    grad_x = grad_mixed + grad_inner
    grad_list = (
        grad_gain_one,
        grad_shift_one,
        grad_w_mix_in,
        grad_bias_mix_in,
        grad_w_mix_out,
        grad_gain_two,
        grad_shift_two,
        grad_w_up,
        grad_bias_up,
        grad_w_down,
        grad_bias_down,
    )
    return (grad_x, grad_list, grad_out_shift)


def per_device(
    tokens,
    cotangent,
    counts,
    ln1_gain,
    ln1_bias,
    tok_in,
    tok_in_bias,
    tok_out,
    tok_out_bias,
    ln2_gain,
    ln2_bias,
    ch_in,
    ch_in_bias,
    ch_out,
    ch_out_bias,
):
    micro_total = counts.shape[1]
    per_micro = tokens.shape[0] // micro_total
    outputs = []
    input_grads = []
    grad_sums = None
    shift_sum = jnp.zeros((tok_out_bias.shape[0],), jnp.float32)
    for micro in range(micro_total):
        lower = micro * per_micro
        input_block = tokens[lower : lower + per_micro].astype(jnp.float32)
        live_rows = (jnp.arange(per_micro) < counts[0, micro]).astype(jnp.float32)[:, None, None]
        grad_out = cotangent[lower : lower + per_micro].astype(jnp.float32) * live_rows
        token_full = (
            lax.all_gather(ln1_gain, "fsdp", axis=0, tiled=True),
            lax.all_gather(ln1_bias, "fsdp", axis=0, tiled=True),
            lax.all_gather(tok_in, "fsdp", axis=0, tiled=True),
            lax.all_gather(tok_in_bias, "fsdp", axis=0, tiled=True),
            lax.all_gather(tok_out, "fsdp", axis=0, tiled=True),
        )
        channel_full = (
            lax.all_gather(ln2_gain, "fsdp", axis=0, tiled=True),
            lax.all_gather(ln2_bias, "fsdp", axis=0, tiled=True),
            lax.all_gather(ch_in, "fsdp", axis=0, tiled=True),
            lax.all_gather(ch_in_bias, "fsdp", axis=0, tiled=True),
            lax.all_gather(ch_out, "fsdp", axis=0, tiled=True),
            lax.all_gather(ch_out_bias, "fsdp", axis=0, tiled=True),
        )
        result, kept = forward(input_block, token_full, channel_full, tok_out_bias)
        outputs.append((result * live_rows).astype(jnp.bfloat16))
        token_back = (
            lax.all_gather(ln1_gain, "fsdp", axis=0, tiled=True),
            lax.all_gather(ln1_bias, "fsdp", axis=0, tiled=True),
            lax.all_gather(tok_in, "fsdp", axis=0, tiled=True),
            lax.all_gather(tok_in_bias, "fsdp", axis=0, tiled=True),
            lax.all_gather(tok_out, "fsdp", axis=0, tiled=True),
        )
        channel_back = (
            lax.all_gather(ln2_gain, "fsdp", axis=0, tiled=True),
            lax.all_gather(ln2_bias, "fsdp", axis=0, tiled=True),
            lax.all_gather(ch_in, "fsdp", axis=0, tiled=True),
            lax.all_gather(ch_in_bias, "fsdp", axis=0, tiled=True),
            lax.all_gather(ch_out, "fsdp", axis=0, tiled=True),
            lax.all_gather(ch_out_bias, "fsdp", axis=0, tiled=True),
        )
        grad_x, grad_list, grad_out_shift = backward(
            grad_out, input_block, kept, token_back, channel_back
        )
        input_grads.append(grad_x.astype(jnp.bfloat16))
        shift_sum = shift_sum + grad_out_shift
        grad_sums = (
            grad_list
            if grad_sums is None
            else tuple(jax.tree.map(jnp.add, tuple(grad_sums), tuple(grad_list)))
        )
    grad_sums = (
        lax.psum_scatter(grad_sums[0], "fsdp", scatter_dimension=0, tiled=True),
        lax.psum_scatter(grad_sums[1], "fsdp", scatter_dimension=0, tiled=True),
        lax.psum_scatter(grad_sums[2], "fsdp", scatter_dimension=0, tiled=True),
        lax.psum_scatter(grad_sums[3], "fsdp", scatter_dimension=0, tiled=True),
        lax.psum_scatter(grad_sums[4], "fsdp", scatter_dimension=0, tiled=True),
        lax.psum_scatter(grad_sums[5], "fsdp", scatter_dimension=0, tiled=True),
        lax.psum_scatter(grad_sums[6], "fsdp", scatter_dimension=0, tiled=True),
        lax.psum_scatter(grad_sums[7], "fsdp", scatter_dimension=0, tiled=True),
        lax.psum_scatter(grad_sums[8], "fsdp", scatter_dimension=0, tiled=True),
        lax.psum_scatter(grad_sums[9], "fsdp", scatter_dimension=0, tiled=True),
        lax.psum_scatter(grad_sums[10], "fsdp", scatter_dimension=0, tiled=True),
    )
    shards = lax.psum(
        (
            grad_sums[0],
            grad_sums[1],
            grad_sums[2],
            grad_sums[3],
            grad_sums[4],
            grad_sums[5],
            grad_sums[6],
            grad_sums[7],
            grad_sums[8],
            grad_sums[9],
            grad_sums[10],
        ),
        "dp",
    )
    shift_total = lax.psum(shift_sum, ("dp", "fsdp"))
    block_out = jnp.concatenate(outputs, axis=0)
    input_grad = jnp.concatenate(input_grads, axis=0)
    return (
        block_out,
        input_grad,
        shards[0],
        shards[1],
        shards[2],
        shards[3],
        shards[4],
        shift_total,
        shards[5],
        shards[6],
        shards[7],
        shards[8],
        shards[9],
        shards[10],
    )


MESH = pl.DeviceIdType.MESH
NN = (((1,), (0,)), ((), ()))
NT = (((1,), (1,)), ((), ()))
TN = (((0,), (0,)), ((), ()))
F32 = jnp.float32
BF16 = jnp.bfloat16
CHUNKS = 6
BLOCK = 784
SPAN = 224
LANES = 128
ROOM = 200
C_A = 0.7978845608
C_B = 0.7978845608 * 0.044715


def dot(left, right, dims=NN):
    return lax.dot_general(left, right, dims, preferred_element_type=F32)


def gelu_and_slope(v):
    ratio = C_B * (v * v) + C_A
    t = jnp.tanh(v * ratio)
    h = 0.5 * t + 0.5
    act = v * h
    slope = h + act * (1.0 - t) * (3.0 * ratio - 2.0 * C_A)
    return act, slope


def row_stats(v):
    mean = jnp.mean(v, axis=-1, keepdims=True)
    centred = v - mean
    spread = jnp.mean(centred * centred, axis=-1, keepdims=True)
    root = lax.rsqrt(spread + EPSILON)
    return centred * root, root, mean


def take(buf, rows, count=6):
    return jnp.concatenate([buf.at[t][rows, :] for t in range(count)], axis=1)


def put(buf, rows, value):
    for t in range(value.shape[1] // LANES):
        buf.at[t][rows, :] = value[:, LANES * t : LANES * (t + 1)]


def mega(
    counts, tokens, cotangent, vector_row, tok_in_own, tok_out_own, ch_in_own, ch_out_own,
    block_out, input_grad, ch_in_grad, ch_out_grad, small_out, gathered, act_hbm, slope_hbm, unit_two_hbm,
    normed_two, grad_rows, result_acc, grad_two_acc, stats, w_in, w_out,
    grads, core_in, cross_out, cross_keep, cross_in, line_out, line_keep, line_in, shards, stage_in,
    small_sum, own_weights, small, tok_in, tok_in_t, tok_out, tok_out_t, vectors, hidden_bias,
    vector_sums, hidden_sums, tok_in_sum, tok_out_sum,
    small_sems, z_sems, z_local, x_sems, swap_sems, core_sems, cross_sems, line_sems, end_sems, load_sems, weight_sems,
):
    total_rows, width = tokens.shape
    images, hidden = act_hbm.shape[0], act_hbm.shape[1]
    patches = total_rows // images
    per_micro = images // counts.shape[1]
    owners = 16
    tiles = width // LANES
    c = lax.axis_index("dp")
    f = lax.axis_index("fsdp")
    zi, qi = f // 4, f % 4
    partner = (1 - c, f)

    def cross(k):
        return (c, zi * 4 + (qi ^ k))

    def line(k):
        return (c, (zi ^ k) * 4 + qi)

    def remote(src, dst, sems, index, device):
        return pltpu.make_async_remote_copy(
            src_ref=src, dst_ref=dst, send_sem=sems.at[(0,) + index], recv_sem=sems.at[(1,) + index],
            device_id=device, device_id_type=MESH,
        )

    def span_rows(b):
        return pl.ds(pl.multiple_of(b * SPAN, 16), SPAN)

    spans = total_rows // SPAN

    parts = total_rows // (16 * images)
    rest = total_rows - parts * 16 * images

    def part_rows(b):
        return pl.ds(pl.multiple_of(b * 16 * images, 16), 16 * images)

    last_part = pl.ds(parts * 16 * images, rest)

    def row_loads(b, rows):
        return (
            pltpu.make_async_copy(tokens.at[rows], normed_two.at[rows], load_sems.at[0, b]),
            pltpu.make_async_copy(cotangent.at[rows], grad_rows.at[rows], load_sems.at[1, b]),
        )

    for b in range(parts):
        for copy in row_loads(b, part_rows(b)):
            copy.start()
    for copy in row_loads(parts, last_part):
        copy.start()
    barrier = pltpu.get_barrier_semaphore()
    for device in [partner] + [cross(k) for k in (1, 2, 3)] + [line(k) for k in (1, 2, 3)]:
        pl.semaphore_signal(barrier, inc=1, device_id=device, device_id_type=MESH)

    row = vector_row[...].astype(F32)

    def vector_at(offset, length, lanes=256):
        moved = row if offset == 0 else pltpu.roll(row, width - offset, 1)
        lane = lax.broadcasted_iota(jnp.int32, (1, lanes), 1)
        return jnp.where(lane < length, moved[:, 0:lanes], 0.0)

    lane = lax.broadcasted_iota(jnp.int32, (24, 256), 1)
    bias_column = jnp.transpose(jnp.broadcast_to(vector_at(240, 24, LANES), (LANES, LANES)))[0:24, 0:1]
    pad = jnp.zeros((24, 256 - patches), F32)
    padded = jnp.concatenate([tok_in_own[...].astype(F32), pad], axis=1)
    padded = jnp.where(lane == 200, jnp.broadcast_to(bias_column, (24, 256)), padded)
    rows_a = [vector_at(48 * r, 48) for r in range(5)] + [vector_at(264, 192), jnp.zeros((2, 256), F32)]
    packed_a = jnp.concatenate([padded] + rows_a, axis=0)
    padded = jnp.concatenate([tok_out_own[...].astype(F32), pad], axis=1)
    bias_rows = jnp.concatenate([vector_at(456, patches), jnp.zeros((7, 256), F32)], axis=0)
    packed_b = jnp.concatenate([padded, bias_rows], axis=0)
    small[c, zi, qi] = jnp.where(c == 0, packed_a, packed_b).astype(BF16)

    def small_line(k):
        return remote(small.at[c, zi, qi], small.at[c, zi, qi], small_sems, (k - 1,), line(k))

    def small_cross(k):
        return remote(small.at[c, :, qi], small.at[c, :, qi], small_sems, (k + 2,), cross(k))

    def small_swap():
        return remote(small.at[c], small.at[c], small_sems, (6,), partner)

    def z_copy(j, k):
        return remote(own_weights.at[j], gathered.at[c, j, zi, qi], z_sems, (j, k - 1), line(k))

    def z_own(j):
        return pltpu.make_async_copy(own_weights.at[j], gathered.at[c, j, zi, qi], z_local.at[j])

    def x_copy(j, k):
        return remote(gathered.at[c, j, :, qi], gathered.at[c, j, :, qi], x_sems, (j, k - 1), cross(k))

    def swap_copy(j):
        return remote(gathered.at[c, j], gathered.at[c, j], swap_sems, (j,), partner)

    def z_start(j):
        z_own(j).start()
        for k in (1, 2, 3):
            z_copy(j, k).start()

    def x_start(j):
        for k in (1, 2, 3):
            z_copy(j, k).wait()
        z_own(j).wait()
        for k in (1, 2, 3):
            x_copy(j, k).start()

    def swap_start(j):
        for k in (1, 2, 3):
            x_copy(j, k).wait()
        swap_copy(j).start()

    def core_copy(p, rows):
        return remote(
            grads.at[1 - c, :, :, pl.ds(0, rows)], core_in.at[p, :, :, pl.ds(0, rows)], core_sems, (p,), partner
        )

    def cross_copy(p, rows, k):
        return remote(
            cross_out.at[k - 1, :, pl.ds(0, rows)], cross_in.at[p, k - 1, :, pl.ds(0, rows)],
            cross_sems, (p, k - 1), cross(k),
        )

    def line_copy(p, rows, k):
        return remote(
            line_out.at[k - 1, pl.ds(0, rows)], line_in.at[p, k - 1, pl.ds(0, rows)], line_sems, (p, k - 1), line(k)
        )

    def cross_start(p, rows):
        core_copy(p, rows).wait()

        def per_line(z, carry):
            for k in range(4):
                q = qi ^ k
                total = grads[c, z, q, 0:rows] + core_in[p, z, q, 0:rows]
                if k == 0:
                    cross_keep[z, 0:rows] = total
                else:
                    cross_out[k - 1, z, 0:rows] = total.astype(BF16)
            return carry

        lax.fori_loop(0, 4, per_line, 0)
        for k in (1, 2, 3):
            cross_copy(p, rows, k).start()

    def line_start(p, rows):
        for k in (1, 2, 3):
            cross_copy(p, rows, k).wait()
        for k in range(4):
            z = zi ^ k
            total = cross_keep[z, 0:rows]
            for m in range(3):
                total = total + cross_in[p, m, z, 0:rows].astype(F32)
            if k == 0:
                line_keep[0:rows] = total
            else:
                line_out[k - 1, 0:rows] = total.astype(BF16)
        for k in (1, 2, 3):
            line_copy(p, rows, k).start()

    def line_finish(p, rows):
        for k in (1, 2, 3):
            line_copy(p, rows, k).wait()
        total = line_keep[0:rows]
        for m in range(3):
            total = total + line_in[p, m, 0:rows].astype(F32)
        return total

    piece = grads.shape[3]

    def live_rows():
        image = lax.broadcasted_iota(jnp.int32, (images, 1), 0)
        live = jnp.zeros((images, 1), F32)
        for micro in range(counts.shape[1]):
            inside = (image >= micro * per_micro) & (image < micro * per_micro + counts[0, micro])
            live = jnp.where(inside, 1.0, live)
        return jnp.broadcast_to(live, (images, width))

    def masked(value, live):
        return (value.reshape(-1, images, width) * live[None]).reshape(value.shape)

    def row_sum(value):
        return jnp.sum(value.reshape(4, value.shape[0] // 32, 8, width).sum(1), axis=0)

    stat_lane = lax.broadcasted_iota(jnp.int32, (SPAN, LANES), 1)

    def image_rows(i):
        return pl.ds(i, patches, stride=images)

    def own_rows():
        @pl.when(c == 0)
        def _():
            group = lax.broadcasted_iota(jnp.int32, (48, LANES), 1) >> 5
            for j in range(CHUNKS):
                for b in range(2):
                    for t in range(2):
                        tile = None
                        for g in range(4):
                            source = 192 * (8 * b + 4 * t + g) + 32 * j
                            part = ch_in_own[:, source // LANES * LANES : (source // LANES + 1) * LANES].astype(F32)
                            shift = (32 * g - source) % LANES
                            part = part if shift == 0 else pltpu.roll(part, shift, 1)
                            tile = part if tile is None else jnp.where(group == g, part, tile)
                        own_weights[j, 48 * b : 48 * b + 48, LANES * t : LANES * (t + 1)] = tile.astype(BF16)

        @pl.when(c == 1)
        def _():
            for j in range(CHUNKS):
                for b in range(3):
                    own_weights[j, 32 * b : 32 * b + 32] = ch_out_own[32 * j : 32 * j + 32, 256 * b : 256 * b + 256]

    def norm_one():
        pl.semaphore_wait(barrier, 7)
        for k in (1, 2, 3):
            small_line(k).start()
        own_rows()
        z_start(0)
        live = live_rows()

        def part(b, rows):
            count = rows.size
            each = count // images
            for copy in row_loads(b, rows):
                copy.wait()
            unit, root, mean = row_stats(normed_two[rows].astype(F32))
            for t in range(tiles):
                by_image = jnp.swapaxes(unit[:, LANES * t : LANES * (t + 1)].reshape(each, images, LANES), 0, 1)
                for i in range(images):
                    grad_two_acc[t, pl.ds(pl.multiple_of(ROOM * i + 16 * b, 8), each)] = by_image[i]
            stat = lax.broadcasted_iota(jnp.int32, (count, LANES), 1)
            stats[rows] = jnp.where(stat < 32, root, mean)
            grad = masked(grad_rows[rows].astype(F32), live)
            grad_rows[rows] = grad.astype(BF16)
            return row_sum(grad)

        def step(b, carry):
            carry = carry + part(b, part_rows(b))

            @pl.when(b == 3)
            def _():
                for k in (1, 2, 3):
                    small_line(k).wait()
                for k in (1, 2, 3):
                    small_cross(k).start()
                z_start(1)

            @pl.when(b == 9)
            def _():
                for k in (1, 2, 3):
                    small_cross(k).wait()
                small_swap().start()

            return carry

        sums = lax.fori_loop(0, parts, step, jnp.zeros((8, width), F32))
        sums = sums + part(parts, last_part)
        vector_sums[...] = jnp.zeros(vector_sums.shape, F32)
        vector_sums[4:5] = jnp.sum(sums, axis=0, keepdims=True)
    norm_one()
    hidden_sums[...] = jnp.zeros(hidden_sums.shape, F32)
    tok_in_sum[...] = jnp.zeros(tok_in_sum.shape, F32)
    tok_out_sum[...] = jnp.zeros(tok_out_sum.shape, F32)
    small_swap().wait()

    part_a = small[0].astype(F32).reshape(owners, 32, 256)
    part_b = small[1].astype(F32).reshape(owners, 32, 256)
    full_in = part_a[:, 0:24].reshape(hidden, 256)
    full_out = part_b[:, 0:24].reshape(hidden, 256)
    tok_in[...] = full_in.astype(BF16)
    tok_in_t[...] = jnp.transpose(full_in).astype(BF16)
    tok_out[...] = full_out.astype(BF16)
    out_rows = jnp.concatenate([full_out, bias_rows, jnp.zeros((120, 256), F32)], axis=0)
    tok_out_t[...] = jnp.transpose(out_rows).astype(BF16)

    flat_a = part_a.reshape(owners * 32, 256).astype(BF16)
    pick_r = lax.broadcasted_iota(jnp.int32, (8, owners * 32), 0)
    pick_p = lax.broadcasted_iota(jnp.int32, (8, owners * 32), 1)
    pick = jnp.where((pick_p & 31) == 24 + pick_r, 1.0, 0.0).astype(BF16)
    col = lax.broadcasted_iota(jnp.int32, (256, width), 1)
    lane = lax.broadcasted_iota(jnp.int32, (256, width), 0)
    spread = jnp.where(lane == col - 48 * ((col * 43691) >> 21), 1.0, 0.0).astype(BF16)
    own_n = (lax.broadcasted_iota(jnp.int32, (owners * 32, width), 1) * 43691) >> 21
    own_p = lax.broadcasted_iota(jnp.int32, (owners * 32, width), 0) >> 5
    vectors[...] = dot(pick, jnp.where(own_n == own_p, dot(flat_a, spread), 0.0).astype(BF16))
    span_n = owners * 32
    own_n = lax.broadcasted_iota(jnp.int32, (span_n, span_n), 1) >> 5
    own_p = lax.broadcasted_iota(jnp.int32, (span_n, span_n), 0) >> 5
    col = lax.broadcasted_iota(jnp.int32, (256, span_n), 1)
    lane = lax.broadcasted_iota(jnp.int32, (256, span_n), 0)
    for j in range(CHUNKS):
        spread = jnp.where(lane == 32 * j + (col & 31), 1.0, 0.0).astype(BF16)
        rows = dot(pick, jnp.where(own_n == own_p, dot(flat_a, spread), 0.0).astype(BF16))
        hidden_bias[j] = rows[5:6]

    def weight_loads(j, p):
        return [
            pltpu.make_async_copy(
                gathered.at[0, j, :, :, pl.ds(48 * b, 48)], w_in.at[p, :, :, :, pl.ds(256 * b, 256)], weight_sems.at[b]
            )
            for b in range(2)
        ] + [
            pltpu.make_async_copy(
                gathered.at[1, j, :, :, pl.ds(32 * b, 32)], w_out.at[p, :, :, :, pl.ds(256 * b, 256)],
                weight_sems.at[2 + b],
            )
            for b in range(3)
        ]

    ones_low = jnp.where(lax.broadcasted_iota(jnp.int32, (64, width), 0) == 8, 1.0, 0.0).astype(BF16)
    ones_act = jnp.where(lax.broadcasted_iota(jnp.int32, (128, width), 0) == 0, 1.0, 0.0).astype(BF16)

    def token_forward(act_buf, slope_buf, normed, unit_buf, out_sems, unit_sems):
        def stores(i, slot):
            return (
                pltpu.make_async_copy(act_buf.at[slot, pl.ds(0, hidden)], act_hbm.at[i], out_sems.at[slot, 0]),
                pltpu.make_async_copy(slope_buf.at[slot], slope_hbm.at[i], out_sems.at[slot, 1]),
            )

        for slot in range(4):
            act_buf[slot, hidden : hidden + 128] = ones_act
        for n in range(2):
            normed[n, 192:256] = ones_low

        def pair(g, base):
            @pl.when(g >= 2)
            def _():
                for n in range(2):
                    for copy in stores(2 * g - 4 + n, base + n):
                        copy.wait()

            @pl.when(g == 0)
            def _():
                x_start(0)
                z_start(2)

            @pl.when(g == 4)
            def _():
                x_start(1)
                z_start(3)

            for n in range(2):
                unit = take(grad_two_acc, pl.ds(pl.multiple_of(ROOM * (2 * g + n), 8), patches))
                normed[n, 0:patches] = (unit * vectors[0:1] + vectors[1:2]).astype(BF16)
            pre = [dot(tok_in[...], normed[n]) for n in range(2)]
            for n in range(2):
                act, slope = gelu_and_slope(pre[n])
                act_buf[base + n, 0:hidden] = act.astype(BF16)
                slope_buf[base + n] = slope.astype(BF16)
            mixed = [dot(tok_out_t[...], act_buf[base + n]) for n in range(2)]
            for n in range(2):
                put(result_acc, image_rows(2 * g + n), mixed[n][0:patches])
                for copy in stores(2 * g + n, base + n):
                    copy.start()

        def pairs(h, carry):
            for half in range(2):
                pair(2 * h + half, 2 * half)
            return carry

        lax.fori_loop(0, images // 4, pairs, 0)
        for i in range(images - 4, images):
            for copy in stores(i, i % 4):
                copy.wait()
        swap_start(0)
        x_start(2)
        z_start(4)

        def unit_two_store(b):
            return pltpu.make_async_copy(unit_buf.at[b % 4], unit_two_hbm.at[span_rows(b)], unit_sems.at[b % 4])

        def span(b, carry):
            rows = span_rows(b)

            @pl.when(b >= 4)
            def _():
                unit_two_store(b - 4).wait()

            mixed = normed_two[rows].astype(F32) + take(result_acc, rows)
            put(result_acc, rows, mixed)
            unit, root, _ = row_stats(mixed)
            stats[rows] = jnp.where(stat_lane < 64, stats[rows], root)
            unit_buf[b % 4] = unit.astype(BF16)
            unit_two_store(b).start()
            normed_two[rows] = (unit * vectors[2:3] + vectors[3:4]).astype(BF16)
            put(grad_two_acc, rows, jnp.zeros((SPAN, width), F32))

            @pl.when(b == 10)
            def _():
                swap_copy(0).wait()
                for copy in weight_loads(0, 0):
                    copy.start()
                swap_start(1)
                x_start(3)
                z_start(5)

            return carry

        lax.fori_loop(0, spans, span, 0)
        for b in range(spans - 4, spans):
            unit_two_store(b).wait()

    pl.run_scoped(
        token_forward,
        pltpu.VMEM((4, hidden + 128, width), BF16),
        pltpu.VMEM((4, hidden, width), BF16),
        pltpu.VMEM((2, 256, width), BF16),
        pltpu.VMEM((4, SPAN, width), BF16),
        pltpu.SemaphoreType.DMA((4, 2)),
        pltpu.SemaphoreType.DMA((4,)),
    )

    def channel(act_all, slope_all):
        chunk = w_in.shape[-1]

        for copy in weight_loads(0, 0):
            copy.wait()

        def tick(j, carry):
            p = j % 2

            @pl.when(j >= 1)
            def _():
                core_copy(1 - p, piece).start()

            def block(b, inner):
                rows = pl.ds(pl.multiple_of(b * BLOCK, 16), BLOCK)
                up = w_in[p].reshape(width, chunk)
                down = w_out[p].reshape(chunk, width)
                pre = dot(normed_two[rows], up) + hidden_bias[j]
                grad_act = dot(grad_rows[rows], down, NT)
                act, slope = gelu_and_slope(pre)
                grad_pre = grad_act * slope
                hidden_sums[j] += jnp.sum(grad_pre.reshape(BLOCK // 112, 14, 8, chunk).sum(1), axis=0)
                act_all[rows] = act.astype(BF16)
                slope_all[rows] = grad_pre.astype(BF16)
                forward_part = dot(act_all[rows], down)
                for t in range(tiles):
                    result_acc[t, rows] += forward_part[:, LANES * t : LANES * (t + 1)]
                backward_part = dot(slope_all[rows], up, NT)
                for t in range(tiles):
                    grad_two_acc[t, rows] += backward_part[:, LANES * t : LANES * (t + 1)]

                @pl.when((b == 0) & (j >= 2))
                def _():
                    line_start(p, piece)

                @pl.when((b == 1) & (j >= 1))
                def _():
                    cross_start(1 - p, piece)

                @pl.when((b == 0) & (j == 0))
                def _():
                    x_start(4)
                    swap_start(2)

                @pl.when((b == 2) & (j == 0))
                def _():
                    x_start(5)

                @pl.when((b == 2) & (j >= 2))
                def _():
                    shards[j - 2] = line_finish(p, piece)

                @pl.when((b == 2) & (j + 1 < CHUNKS))
                def _():
                    swap_copy(j + 1).wait()
                    for copy in weight_loads(j + 1, 1 - p):
                        copy.start()

                @pl.when((b == 3) & (j + 3 < CHUNKS))
                def _():
                    swap_start(j + 3)

                return inner

            lax.fori_loop(0, total_rows // BLOCK, block, 0)
            up_grad = dot(normed_two[...], slope_all[...], TN)
            for b in range(2):
                grads[0, :, :, 48 * b : 48 * b + 48] = up_grad[:, 256 * b : 256 * b + 256].reshape(4, 4, 48, 256)
            down_grad = dot(act_all[...], grad_rows[...], TN)
            for b in range(3):
                grads[1, :, :, 32 * b : 32 * b + 32] = down_grad[:, 256 * b : 256 * b + 256].reshape(4, 4, 32, 256)

            @pl.when(j + 1 < CHUNKS)
            def _():
                for copy in weight_loads(j + 1, 1 - p):
                    copy.wait()

            return carry

        lax.fori_loop(0, CHUNKS, tick, 0)

    pl.run_scoped(
        channel,
        pltpu.VMEM((total_rows, 512), BF16),
        pltpu.VMEM((total_rows, 512), BF16),
    )

    def stage_out_copy(b):
        return remote(
            shards.at[:, pl.ds(32 * b, 32)], ch_out_grad.at[:, :, pl.ds(256 * b, 256)], end_sems, (b,), partner
        )

    def stage_out_own(b):
        return pltpu.make_async_copy(
            shards.at[:, pl.ds(32 * b, 32)], ch_out_grad.at[:, :, pl.ds(256 * b, 256)], end_sems.at[0, 4 + b]
        )

    def send_stages():
        @pl.when(c == 0)
        def _():
            remote(stage_in, ch_in_grad, end_sems, (0,), partner).start()
            pltpu.make_async_copy(stage_in, ch_in_grad, end_sems.at[0, 4]).start()

        @pl.when(c == 1)
        def _():
            for b in range(3):
                stage_out_copy(b).start()
                stage_out_own(b).start()

    def fill_stages():
        @pl.when(c == 0)
        def _():
            group = lax.broadcasted_iota(jnp.int32, (48, LANES), 1) >> 5
            for t in range(24):
                tile = None
                for g in range(4):
                    unit = LANES * t + 32 * g
                    o, j = unit // 192, unit % 192 // 32
                    b, source = o // 8, 32 * (o % 8)
                    part = shards[j, 48 * b : 48 * b + 48, source // LANES * LANES : (source // LANES + 1) * LANES]
                    shift = (32 * g - source) % LANES
                    part = part if shift == 0 else pltpu.roll(part, shift, 1)
                    tile = part if tile is None else jnp.where(group == g, part, tile)
                stage_in[:, LANES * t : LANES * (t + 1)] = tile

    def token_backward(units, unit_buf, out_buf, x_load_sems, in_sems, unit_sems, out_sems):
        def act_at(slot, count):
            return normed_two.at[pl.ds(512 * slot, count)]

        def slope_at(slot):
            return grad_rows.at[pl.ds(384 * slot, hidden)]

        def loads(i, slot):
            return (
                pltpu.make_async_copy(act_hbm.at[i], act_at(slot, hidden), in_sems.at[slot, 0]),
                pltpu.make_async_copy(slope_hbm.at[i], slope_at(slot), in_sems.at[slot, 1]),
            )

        def unit_two_load(b):
            return pltpu.make_async_copy(unit_two_hbm.at[span_rows(b)], unit_buf.at[b % 4], unit_sems.at[b % 4])

        def x_load(b):
            return pltpu.make_async_copy(tokens.at[span_rows(b)], normed_two.at[span_rows(b)], x_load_sems.at[b])

        core_copy(1, piece).start()
        for b in range(spans):
            x_load(b).start()
            if b < 3:
                unit_two_load(b).start()
        live = live_rows()

        def out_store(b, slot):
            return pltpu.make_async_copy(out_buf.at[slot], block_out.at[span_rows(b)], out_sems.at[slot])

        def span(b, sums):
            slot = b % 2

            @pl.when(b + 3 < spans)
            def _():
                unit_two_load(b + 3).start()

            @pl.when(b >= 2)
            def _():
                out_store(b - 2, slot).wait()

            x_load(b).wait()
            unit_two_load(b).wait()
            rows = span_rows(b)
            put(units, rows, (normed_two[rows].astype(F32) - stats[rows, 32:33]) * stats[rows, 0:1])
            unit = unit_buf[b % 4].astype(F32)
            root = stats[rows, 64:65]
            grad = take(grad_two_acc, rows)
            weighted = grad * unit
            scaled = grad * vectors[2:3]
            inner = jnp.mean(weighted * vectors[2:3], axis=-1, keepdims=True)
            mixed = grad_rows[rows].astype(F32) + root * (
                scaled - jnp.mean(scaled, axis=-1, keepdims=True) - unit * inner
            )
            put(grad_two_acc, rows, mixed)
            out_buf[slot] = masked(take(result_acc, rows) + vectors[4:5], live).astype(BF16)
            out_store(b, slot).start()

            @pl.when(b == 2)
            def _():
                line_start(0, piece)

            @pl.when(b == 7)
            def _():
                cross_start(1, piece)

            return sums[0] + row_sum(weighted), sums[1] + row_sum(grad)

        zero = jnp.zeros((8, width), F32)
        sums = lax.fori_loop(0, spans, span, (zero, zero))
        for b in (spans - 2, spans - 1):
            out_store(b, b % 2).wait()
        for n in range(2):
            for copy in loads(n, n):
                copy.start()
        for slot in range(4):
            normed_two[512 * slot + hidden : 512 * slot + 512] = ones_act
        for n in range(2):
            normed_two[2048 + 256 * n + 192 : 2048 + 256 * n + 256] = ones_low
            normed_two[2560 + 256 * n + 192 : 2560 + 256 * n + 256] = jnp.zeros((64, width), BF16)
        vector_sums[2:3] = jnp.sum(sums[0], axis=0, keepdims=True)
        vector_sums[3:4] = jnp.sum(sums[1], axis=0, keepdims=True)
        shards[CHUNKS - 2] = line_finish(0, piece)

        def pair(g, base):
            @pl.when(g + 1 < images // 2)
            def _():
                for n in range(2):
                    for copy in loads(2 * g + 2 + n, 2 - base + n):
                        copy.start()

            for n in range(2):
                for copy in loads(2 * g + n, base + n):
                    copy.wait()

            @pl.when(g == 3)
            def _():
                line_start(1, piece)

            @pl.when(g == 6)
            def _():
                shards[CHUNKS - 1] = line_finish(1, piece)
                fill_stages()
                send_stages()

            for n in range(2):
                low = take(grad_two_acc, image_rows(2 * g + n))
                normed_two[2560 + 256 * n : 2560 + 256 * n + patches] = low.astype(BF16)
            unit = [take(units, image_rows(2 * g + n)) for n in range(2)]
            for n in range(2):
                normed_two[2048 + 256 * n : 2048 + 256 * n + patches] = (
                    unit[n] * vectors[0:1] + vectors[1:2]
                ).astype(BF16)
            lows = [normed_two[2560 + 256 * n : 2816 + 256 * n] for n in range(2)]
            grad_act = [dot(tok_out[...], lows[n]) for n in range(2)]
            for n in range(2):
                grad_rows[1536 + 384 * n : 1920 + 384 * n] = (
                    grad_act[n] * slope_at(base + n)[...].astype(F32)
                ).astype(BF16)
            tok_out_sum[...] += dot(act_at(base, 512)[...], lows[0], NT) + dot(act_at(base + 1, 512)[...], lows[1], NT)
            pres = [grad_rows[1536 + 384 * n : 1920 + 384 * n] for n in range(2)]
            grad = [dot(tok_in_t[...], pres[n])[0:patches] for n in range(2)]
            tok_in_sum[...] += dot(pres[0], normed_two[2048:2304], NT) + dot(pres[1], normed_two[2304:2560], NT)
            for n in range(2):
                put(result_acc, image_rows(2 * g + n), grad[n])
            gain = grad[0] * unit[0] + grad[1] * unit[1]
            vector_sums[0:1] += jnp.sum(gain, axis=0, keepdims=True)
            vector_sums[1:2] += jnp.sum(grad[0] + grad[1], axis=0, keepdims=True)

        def pairs(h, carry):
            for half in range(2):
                pair(2 * h + half, 2 * half)
            return carry

        lax.fori_loop(0, images // 4, pairs, 0)

        grads[0, :, :, 0:24] = tok_in_sum[...].reshape(4, 4, 24, 256)
        grads[1, :, :, 0:24] = tok_out_sum[0:hidden].reshape(4, 4, 24, 256)
        sums = vector_sums[...]
        hidden_rows = jnp.concatenate(
            [jnp.sum(hidden_sums[j], axis=0, keepdims=True) for j in range(CHUNKS)] + [jnp.zeros((2, 512), F32)], axis=0
        )
        for o in range(owners):
            moved = sums if o == 0 else pltpu.roll(sums, width - 48 * o, 1)
            grads[0, o // 4, o % 4, 24:32, 0:128] = moved[:, 0:128]
            grads[0, o // 4, o % 4, 24:32, 128:256] = jnp.zeros((8, 128), F32)
            grads[0, o // 4, o % 4, 31:32] = tok_out_sum[hidden : hidden + 1]
            moved = hidden_rows if o == 0 else pltpu.roll(hidden_rows, 512 - 32 * o, 1)
            grads[1, o // 4, o % 4, 24:32, 0:128] = moved[:, 0:128]
            grads[1, o // 4, o % 4, 24:32, 128:256] = jnp.zeros((8, 128), F32)
        core_copy(0, 32).start()

        def grad_store(b, slot):
            return pltpu.make_async_copy(out_buf.at[slot], input_grad.at[span_rows(b)], out_sems.at[slot])

        def last(b, carry):
            slot = b % 2

            @pl.when(b >= 2)
            def _():
                grad_store(b - 2, slot).wait()

            rows = span_rows(b)
            unit = take(units, rows)
            root = stats[rows, 0:1]
            scaled = take(result_acc, rows) * vectors[0:1]
            inner = jnp.mean(scaled * unit, axis=-1, keepdims=True)
            out_buf[slot] = (
                take(grad_two_acc, rows)
                + root * (scaled - jnp.mean(scaled, axis=-1, keepdims=True) - unit * inner)
            ).astype(BF16)
            grad_store(b, slot).start()

            @pl.when(b == 3)
            def _():
                cross_start(0, 32)

            @pl.when(b == spans - 3)
            def _():
                line_start(0, 32)

            return carry

        lax.fori_loop(0, spans, last, 0)
        for b in (spans - 2, spans - 1):
            grad_store(b, b % 2).wait()

    pl.run_scoped(
        token_backward,
        pltpu.VMEM((tiles, total_rows, LANES), F32),
        pltpu.VMEM((4, SPAN, width), BF16),
        pltpu.VMEM((2, SPAN, width), BF16),
        pltpu.SemaphoreType.DMA((spans,)),
        pltpu.SemaphoreType.DMA((4, 2)),
        pltpu.SemaphoreType.DMA((4,)),
        pltpu.SemaphoreType.DMA((2,)),
    )

    small_sum[...] = line_finish(0, 32)
    small_end = remote(small_sum, small_out.at[c], end_sems, (3,), partner)
    small_own = pltpu.make_async_copy(small_sum, small_out.at[c], end_sems.at[1, 4])
    small_end.start()
    small_own.start()
    small_end.wait()
    small_own.wait()

    @pl.when(c == 0)
    def _():
        remote(stage_in, ch_in_grad, end_sems, (0,), partner).wait_send()
        pltpu.make_async_copy(stage_in, ch_in_grad, end_sems.at[0, 4]).wait()
        for b in range(3):
            stage_out_copy(b).wait_recv()

    @pl.when(c == 1)
    def _():
        for b in range(3):
            stage_out_copy(b).wait_send()
            stage_out_own(b).wait()
        remote(stage_in, ch_in_grad, end_sems, (0,), partner).wait_recv()


def finish(small, ch_in_sum, ch_out_sum, *outs):
    gain_one, bias_one, tok_in, tok_in_bias, tok_out, tok_out_bias, gain_two, bias_two, ch_in, ch_in_bias, ch_out, ch_out_bias = outs
    per_tok, patches = tok_in.shape
    ch_in[...] = ch_in_sum[...]
    ch_out[...] = ch_out_sum[...]
    tok_in[...] = small[0, 0:per_tok, 0:patches]
    tok_out[...] = small[1, 0:per_tok, 0:patches]
    column = jnp.broadcast_to(small[0, 0:32, 200:201], (32, LANES))
    flipped = jnp.transpose(jnp.concatenate([column, jnp.zeros((LANES - 32, LANES), F32)], axis=0))
    tok_in_bias[...] = flipped[0:1, 0:per_tok]
    tok_out_bias[...] = small[0, 31:32, 0:patches]
    for r, out in enumerate((gain_one, bias_one, gain_two, bias_two, ch_out_bias)):
        out[...] = small[0, 24 + r : 25 + r, 0 : out.shape[1]]
    each = ch_in_bias.shape[1] // CHUNKS
    lane = lax.broadcasted_iota(jnp.int32, (1, 256), 1)
    total = jnp.zeros((1, 256), F32)
    for j in range(CHUNKS):
        part = small[1, 24 + j : 25 + j]
        part = part if j == 0 else pltpu.roll(part, each * j, 1)
        total = jnp.where((lane >= each * j) & (lane < each * (j + 1)), part, total)
    ch_in_bias[...] = total[:, 0 : ch_in_bias.shape[1]]


def per_device_fused(
    tokens, cotangent, counts, ln1_gain, ln1_bias, tok_in, tok_in_bias, tok_out, tok_out_bias,
    ln2_gain, ln2_bias, ch_in, ch_in_bias, ch_out, ch_out_bias,
):
    images, patches, width = tokens.shape
    per_in, inner = ch_in.shape
    per_out = ch_out.shape[0]
    per_tok = tok_in.shape[0]
    owners = width // per_in
    hidden = per_tok * owners
    each = per_out // CHUNKS
    chunk = each * owners
    rows = images * patches

    def by_patch(array):
        return array.transpose(1, 0, 2).reshape(rows, width)

    vector_row = jnp.zeros((width,), F32)
    offset = 0
    for vector in (ln1_gain, ln1_bias, ln2_gain, ln2_bias, ch_out_bias, tok_in_bias, ch_in_bias, tok_out_bias):
        length = vector.shape[0]
        vector_row = vector_row + jnp.pad(vector, (offset, width - offset - length)).astype(F32)
        offset += length
    vector_row = vector_row[None]
    any_spec = pl.BlockSpec(memory_space=pl.ANY)
    vmem_spec = pl.BlockSpec(memory_space=pltpu.VMEM)
    vmem = pltpu.VMEM
    dma = pltpu.SemaphoreType.DMA
    shape = jax.ShapeDtypeStruct
    tiled = (width // LANES, rows, LANES)
    results = pl.pallas_call(
        mega,
        in_specs=[pl.BlockSpec(memory_space=pltpu.SMEM), any_spec, any_spec] + [vmem_spec] * 5,
        out_specs=[any_spec] * 9,
        out_shape=[
            shape((rows, width), BF16),
            shape((rows, width), BF16),
            shape(ch_in.shape, F32),
            shape((CHUNKS, each, width), F32),
            shape((2, 32, 256), F32),
            shape((2, CHUNKS, 4, 4, 96, 256), BF16),
            shape((images, hidden, width), BF16),
            shape((images, hidden, width), BF16),
            shape((rows, width), BF16),
        ],
        scratch_shapes=[
            vmem((rows, width), BF16),
            vmem((rows, width), BF16),
            vmem(tiled, F32),
            vmem((width // LANES, images * ROOM, LANES), F32),
            vmem((rows, LANES), F32),
            vmem((2, 4, 4, per_in, chunk), BF16),
            vmem((2, 4, 4, each, width), BF16),
            vmem((2, 4, 4, 96, 256), F32),
            vmem((2, 4, 4, 96, 256), F32),
            vmem((3, 4, 96, 256), BF16),
            vmem((4, 96, 256), F32),
            vmem((2, 3, 4, 96, 256), BF16),
            vmem((3, 96, 256), BF16),
            vmem((96, 256), F32),
            vmem((2, 3, 96, 256), BF16),
            vmem((CHUNKS, 96, 256), F32),
            vmem(ch_in.shape, F32),
            vmem((32, 256), F32),
            vmem((CHUNKS, 96, 256), BF16),
            vmem((2, 4, 4, 32, 256), BF16),
            vmem((hidden, 256), BF16),
            vmem((256, hidden), BF16),
            vmem((hidden, 256), BF16),
            vmem((256, hidden + 128), BF16),
            vmem((8, width), F32),
            vmem((CHUNKS, 1, chunk), F32),
            vmem((8, width), F32),
            vmem((CHUNKS, 8, chunk), F32),
            vmem((hidden, 256), F32),
            vmem((hidden + 128, 256), F32),
            dma((2, 7)),
            dma((2, CHUNKS, 3)),
            dma((CHUNKS,)),
            dma((2, CHUNKS, 3)),
            dma((2, CHUNKS)),
            dma((2, 2)),
            dma((2, 2, 3)),
            dma((2, 2, 3)),
            dma((2, 7)),
            dma((2, 14)),
            dma((5,)),
        ],
        compiler_params=pltpu.CompilerParams(
            collective_id=0, has_side_effects=True, vmem_limit_bytes=61 * 1024 * 1024
        ),
        cost_estimate=pl.CostEstimate(
            flops=12 * rows * width * inner, bytes_accessed=100_000_000, transcendentals=rows * inner
        ),
    )(counts, by_patch(tokens), by_patch(cotangent), vector_row, tok_in, tok_out, ch_in, ch_out)
    block_out, input_grad, in_sum, out_sum, small = results[:5]
    line = shape((1, per_in), F32)
    outs = pl.pallas_call(
        finish,
        in_specs=[vmem_spec] * 3,
        out_specs=[vmem_spec] * 12,
        out_shape=[
            line, line, shape(tok_in.shape, F32), shape((1, per_tok), F32), shape(tok_out.shape, F32),
            shape((1, patches), F32), line, line, shape(ch_in.shape, F32), shape((1, per_out), F32),
            shape(ch_out.shape, F32), line,
        ],
    )(small, in_sum, out_sum.reshape(ch_out.shape))

    def by_image(array):
        return array.reshape(patches, images, width).transpose(1, 0, 2)

    flat = (0, 1, 3, 5, 6, 7, 9, 11)
    outs = [out.reshape(-1) if n in flat else out for n, out in enumerate(outs)]
    return (by_image(block_out), by_image(input_grad), *outs)


def solution(mesh):
    fused = mesh.shape["dp"] == 2 and mesh.shape["fsdp"] == 16
    return jax.shard_map(
        per_device_fused if fused else per_device,
        mesh=mesh,
        in_specs=(
            P(("dp", "fsdp"), None, None),
            P(("dp", "fsdp"), None, None),
            P(("dp", "fsdp"), None),
            P("fsdp"),
            P("fsdp"),
            P("fsdp", None),
            P("fsdp"),
            P("fsdp", None),
            P(),
            P("fsdp"),
            P("fsdp"),
            P("fsdp", None),
            P("fsdp"),
            P("fsdp", None),
            P("fsdp"),
        ),
        out_specs=(
            P(("dp", "fsdp"), None, None),
            P(("dp", "fsdp"), None, None),
            P("fsdp"),
            P("fsdp"),
            P("fsdp", None),
            P("fsdp"),
            P("fsdp", None),
            P(),
            P("fsdp"),
            P("fsdp"),
            P("fsdp", None),
            P("fsdp"),
            P("fsdp", None),
            P("fsdp"),
        ),
        check_vma=False,
    )
```
